512 devices in a mesh: row: 16 (over z_hi, x, core), col: 32 (over y, z_lo).
Axes of the slice: x: 4, y: 8, z: 8 (z_hi: 2, z_lo: 4; z = z_hi * 4 + z_lo), core: 2. Of those that a mesh axis runs over, the one named last changes fastest.
Arguments:
- vectors: bfloat16 [16, 32, 4096], P(None, 'row', 'col')
- tile_values: bfloat16 [16, 2048, 64, 128], P('row', 'col'), may hold values from -0.09375 to 0.09375
- tile_coords: int32 [2, 16, 4096], P(None, 'row', 'col'), may hold values from 0 to 2047, as said below
- tile_counts: int32 [16, 32], P('row', 'col'), may hold values from 32 to 128, as said below
- energies: float32 [32, 4096], P('row', 'col'), may hold values from 0.3 to 3
Outputs:
- residual: bfloat16 [16, 32, 4096], P(None, 'row', 'col')
- image: float32 [16, 32, 4096], P(None, 'row', 'col')
The draws below stay inside these ranges and needn't reach their ends.
Inputs may be any that keep to these rules, and one draw needn't show every extreme that they name: `tile_coords`: every slot of device (r, c) holds a tile row i with ((i // 2) % 32) // 2 == r and a tile column j with (j // 2) % 32 == c. The slots below the device's count hold distinct tiles with i <= j; later slots hold tiles of the same device's region and are not part of the Hamiltonian. `tile_counts`: devices (r, c) with c // 2 == r hold exactly 128 live slots; one other device holds exactly 32.
All inputs are finite; a program needn't handle non-finite values.
Results may differ from the reference program's by a relative error of at most 0.0075.
Values may be sent and summed in bfloat16 or wider, within the bound.
No kernel may reach another device: no remote copies, remote signals or barrier semaphores. Data moves between devices by JAX's collectives and lax.ppermute only.
A program may use at most 64 MiB of HBM per device.

```python
import math
import jax
import jax.numpy as jnp
from jax import lax

COLS = 16
TILE = 64
PAIR = 128
PPB = 32
TB = 128
ROW_GROUPS = 16
BLOCKS = 32
SPAN = 2
NT = 2048


def tile_layout(key):
    device_total = ROW_GROUPS * BLOCKS
    region = 4 * SPAN * PPB * PPB
    device_ids = jnp.arange(device_total, dtype=jnp.int32)
    grid_row = device_ids // BLOCKS
    grid_col = device_ids % BLOCKS
    position = jnp.arange(region, dtype=jnp.int32)
    local_row = position // (2 * PPB)
    local_col = position % (2 * PPB)
    row_block = grid_row[:, None] * SPAN + local_row[None, :] // (2 * PPB)
    tile_row = 2 * (local_row[None, :] // 2 % PPB * BLOCKS + row_block) + local_row[None, :] % 2
    tile_col = 2 * (local_col[None, :] // 2 * BLOCKS + grid_col[:, None]) + local_col[None, :] % 2
    upper = tile_row <= tile_col
    device_keys = jax.random.split(jax.random.fold_in(key, 11), device_total)
    shuffled = jax.vmap(lambda device_key: jax.random.permutation(device_key, region))(device_keys)
    ranking = jnp.where(upper, 0, region) + shuffled.astype(jnp.int32)
    chosen = jnp.argsort(ranking, axis=1)[:, :TB]
    rows_pick = jnp.take_along_axis(tile_row, chosen, axis=1)
    cols_pick = jnp.take_along_axis(tile_col, chosen, axis=1)
    coords = jnp.stack([rows_pick, cols_pick]).reshape(2, ROW_GROUPS, BLOCKS * TB).astype(jnp.int32)
    diagonal = grid_col // SPAN == grid_row
    reduction = jax.random.randint(jax.random.fold_in(key, 13), (device_total,), 0, TB - TB // 4 + 1, dtype=jnp.int32)
    light_row = jax.random.randint(jax.random.fold_in(key, 17), (), 0, ROW_GROUPS, dtype=jnp.int32)
    light_shift = jax.random.randint(jax.random.fold_in(key, 19), (), 0, BLOCKS - SPAN, dtype=jnp.int32)
    light_col = (light_row * SPAN + SPAN + light_shift) % BLOCKS
    counts = jnp.where(diagonal, TB, TB - reduction)
    counts = jnp.where((grid_row == light_row) & (grid_col == light_col), TB // 4, counts)
    return (coords, counts.reshape(ROW_GROUPS, BLOCKS).astype(jnp.int32))


def draw_tile_coords(key, part):
    return tile_layout(key)[0]


def draw_tile_counts(key, part):
    return tile_layout(key)[1]


def draw_vectors(key, part):
    key = jax.random.fold_in(key, 3)
    key_values = jax.random.fold_in(key, 1)
    key_rows = jax.random.fold_in(key, 2)
    key_columns = jax.random.fold_in(key, 5)
    shape = (COLS, PPB, BLOCKS * PAIR)
    row_scale = jnp.exp(jax.random.uniform(key_rows, (1, PPB, BLOCKS * PAIR), jnp.float32, -1.15, 1.15))
    column_scale = jnp.exp(jax.random.uniform(key_columns, (COLS, 1, 1), jnp.float32, -0.55, 0.55))
    values = jax.random.normal(key_values, shape, jnp.float32) * column_scale * row_scale
    return values.astype(jnp.bfloat16)


def shard_levels(own_key, dims, cuts, smallest, largest):
    def one(dim, shards_of):
        steps = jax.random.uniform(jax.random.fold_in(jax.random.fold_in(own_key, 6), dim), (shards_of,), jnp.float32, smallest / len(cuts), largest / len(cuts))
        return jnp.repeat(jnp.exp(steps), dims[dim] // shards_of).reshape((-1,) + (1,) * (len(dims) - dim - 1))

    level = one(*cuts[0])
    for cut in cuts[1:]:
        level = level * one(*cut)
    return level


def scatter_about(stream_key, extent, scale, most, shards=(), kind=jnp.bfloat16):
    values = jax.random.normal(stream_key, extent, jnp.float32) * scale
    if len(shards) > 0:
        values = shard_levels(stream_key, extent, shards, -0.22, 0.18) * values
    return jnp.clip(values, min=-most, max=most).astype(kind)


def setup_inputs(seed: int = 0) -> dict:
    arg_keys = jax.random.split(jax.random.key(seed), 6)
    vectors = draw_vectors(jax.random.fold_in(arg_keys[5], 71), 0)
    tile_values = scatter_about(arg_keys[1], (ROW_GROUPS, BLOCKS * TB // 2, TILE, PAIR), (TB * ROW_GROUPS * TILE // PPB) ** -0.5, 0.09375, ((0, 16), (1, 32)))
    tile_coords = draw_tile_coords(jax.random.fold_in(arg_keys[5], 71), 0)
    tile_counts = draw_tile_counts(jax.random.fold_in(arg_keys[5], 71), 0)
    energies = jnp.clip(jnp.exp(math.log(3.0) - 2.3025851 * jax.random.uniform(arg_keys[4], (PPB, BLOCKS * PAIR), jnp.float32) ** shard_levels(arg_keys[4], (PPB, BLOCKS * PAIR), ((0, 16), (1, 32)), -0.2, 0.2)), 0.3, 3.0)
    return {"vectors": vectors, "tile_values": tile_values, "tile_coords": tile_coords, "tile_counts": tile_counts, "energies": energies}


def rayleigh_solve(gram_vectors, gram_product):
    factor = jnp.linalg.cholesky(gram_vectors)
    halfway = lax.linalg.triangular_solve(factor, gram_product, left_side=True, lower=True)
    return lax.linalg.triangular_solve(factor, halfway, left_side=True, lower=True, transpose_a=True)

def apply_hamiltonian(vector_block, tile_values, tile_coords, tile_counts, energies):
    device_total = ROW_GROUPS * BLOCKS
    tile_view = vector_block.reshape(COLS, NT, TILE).astype(jnp.float32)
    packs = tile_values.reshape(device_total, TB // 2, TILE, 2, TILE)
    rows_all = tile_coords[0].reshape(device_total, TB)
    cols_all = tile_coords[1].reshape(device_total, TB)
    counts_all = tile_counts.reshape(device_total)

    def device_step(running, slot_data):
        pack, rows_dev, cols_dev, count_dev = slot_data
        live_mask = (jnp.arange(TB, dtype=jnp.int32) < count_dev).astype(jnp.float32)
        matrix_f = pack.astype(jnp.float32)
        x_column = tile_view[:, cols_dev, :].reshape(COLS, TB // 2, 2, TILE)
        x_row = tile_view[:, rows_dev, :].reshape(COLS, TB // 2, 2, TILE)
        forward = jnp.einsum('hatb,khtb->khta', matrix_f, x_column, precision=lax.Precision.HIGHEST)
        backward = jnp.einsum('hatb,khta->khtb', matrix_f, x_row, precision=lax.Precision.HIGHEST)
        forward = forward.reshape(COLS, TB, TILE) * live_mask[None, :, None]
        backward = backward.reshape(COLS, TB, TILE) * live_mask[None, :, None]
        running = running.at[:, rows_dev, :].add(forward)
        running = running.at[:, cols_dev, :].add(backward)
        return (running, None)
    running = jnp.zeros((COLS, NT, TILE), jnp.float32)
    running, _ = lax.scan(device_step, running, (packs, rows_all, cols_all, counts_all))
    result = running.reshape(COLS, PPB, BLOCKS * PAIR)
    return result + energies[None] * vector_block.astype(jnp.float32)

def reference(vectors, tile_values, tile_coords, tile_counts, energies):
    product = apply_hamiltonian(vectors, tile_values, tile_coords, tile_counts, energies)
    flat_vectors = vectors.reshape(COLS, -1)
    flat_product = product.reshape(COLS, -1)
    gram_vectors = jnp.dot(flat_vectors.astype(jnp.float32), flat_vectors.T.astype(jnp.float32), preferred_element_type=jnp.float32)
    gram_product = jnp.dot(flat_vectors.astype(jnp.float32), flat_product.T, precision=lax.Precision.HIGHEST)
    rayleigh = rayleigh_solve(gram_vectors, gram_product)
    shifted = jnp.dot(rayleigh.T, flat_vectors.astype(jnp.float32), precision=lax.Precision.HIGHEST)
    residual = (flat_product - shifted).astype(jnp.bfloat16).reshape(vectors.shape)
    image = apply_hamiltonian(residual, tile_values, tile_coords, tile_counts, energies)
    return (residual, image)
```

```python
import functools

import jax
import jax.numpy as jnp
from jax import lax
from jax.experimental import pallas as pl
from jax.experimental.pallas import tpu as pltpu
from jax.sharding import PartitionSpec as P

F32 = jnp.float32
BF16 = jnp.bfloat16
VECS = 16
LANES = 128
HALF = 64
NR = 16
NC = 32
GROUP = 6
PAIRS = NR * GROUP
SLOTS = 128
DEAD = 2 * PAIRS
VMEM = pl.BlockSpec(memory_space=pltpu.VMEM)
SMEM = pl.BlockSpec(memory_space=pltpu.SMEM)
NT_DIMS = (((1,), (1,)), ((), ()))


def shape(*dims, dtype=BF16):
    return jax.ShapeDtypeStruct(dims, dtype)


def call(kernel, outs, n_in, scratch=(), smem_first=False, limit=None):
    specs = [VMEM] * n_in
    if smem_first:
        specs[0] = SMEM
    return pl.pallas_call(
        kernel,
        out_shape=outs,
        in_specs=specs,
        out_specs=jax.tree.map(lambda _: VMEM, outs),
        scratch_shapes=list(scratch),
        compiler_params=pltpu.CompilerParams(vmem_limit_bytes=limit or 32 * 1024 * 1024),
    )


def lane_index():
    return lax.broadcasted_iota(jnp.int32, (VECS, LANES), 1)


def split3(value):
    high = value.astype(BF16)
    rest = value - high.astype(F32)
    middle = rest.astype(BF16)
    low = (rest - middle.astype(F32)).astype(BF16)
    return high, middle, low


def spread_kernel(x_ref, out_ref):
    for k in range(NC):
        out_ref[k] = x_ref[...]


def regroup_kernel(own_ref, in_ref, out_ref):
    for r in range(NR):
        for s in range(2):
            for j in range(2):
                out_ref[r, 2 * s + j] = in_ref[2 * r + s, j]
        for j in range(2):
            out_ref[r, 4 + j] = own_ref[j]


def tiles_kernel(with_gram, *refs):
    if with_gram:
        idx_ref, x_ref, w_ref, own_ref, e_ref, out_ref, field, acc_row, acc_col = refs
    else:
        idx_ref, x_ref, w_ref, out_ref, field, acc_row, acc_col = refs
    lane = lane_index()
    low_half = lane < HALF
    zero = jnp.zeros((VECS, LANES), F32)
    half_mask = [low_half, jnp.logical_not(low_half)]
    half_one = [jnp.where(m, 1.0, 0.0).astype(BF16) for m in half_mask]

    def duplicate(r, carry):
        for g in range(GROUP):
            value = x_ref[r, g].astype(F32)
            turned = pltpu.roll(value, HALF, 1)
            field[(r * GROUP + g) * 2] = jnp.where(low_half, value, turned).astype(BF16)
            field[(r * GROUP + g) * 2 + 1] = jnp.where(low_half, turned, value).astype(BF16)
            for h in range(2):
                acc_row[(r * GROUP + g) * 2 + h] = zero
                acc_col[(r * GROUP + g) * 2 + h] = zero
        return carry

    lax.fori_loop(0, NR, duplicate, 0)
    field[DEAD] = zero.astype(BF16)
    acc_row[DEAD] = zero
    acc_col[DEAD] = zero

    def group(q, carry):
        rows, cols = [], []
        for k in range(4):
            rows.append(idx_ref[0, q * 4 + k])
            cols.append(idx_ref[1, q * 4 + k])
        w = w_ref[pl.ds(2 * q, 2)].reshape(2 * HALF, LANES)
        left_f = jnp.concatenate([field[cols[k]] * half_one[k % 2] for k in range(4)], axis=0)
        left_b = jnp.concatenate([field[rows[k]] * half_one[k // 2] for k in range(4)], axis=0)
        forward = lax.dot_general(left_f, w, NT_DIMS, preferred_element_type=F32)
        backward = jnp.dot(left_b, w, preferred_element_type=F32)
        for k in range(4):
            piece = slice(k * VECS, (k + 1) * VECS)
            acc_row[rows[k]] += jnp.where(half_mask[k // 2], forward[piece], 0.0)
            acc_col[cols[k]] += jnp.where(half_mask[k % 2], backward[piece], 0.0)
        return carry

    lax.fori_loop(0, SLOTS // 4, group, 0)

    def fold(acc, p):
        first, second = acc[2 * p], acc[2 * p + 1]
        return jnp.where(low_half, first, second) + pltpu.roll(
            jnp.where(low_half, second, first), HALF, 1
        )

    def pack(r, carry):
        for g in range(4):
            out_ref[r, g] = fold(acc_row, r * GROUP + g).astype(BF16)
        for g in range(4, GROUP):
            total = fold(acc_col, r * GROUP + g)
            out_ref[r, g] = total.astype(BF16)
            if with_gram:
                x = x_ref[r, g]
                for part in split3(total):
                    carry = carry + lax.dot_general(x, part, NT_DIMS, preferred_element_type=F32)
        return carry

    if not with_gram:
        lax.fori_loop(0, NR, pack, 0)
        return
    cross = lax.fori_loop(0, NR, pack, jnp.zeros((VECS, VECS), F32))
    gram = jnp.zeros((VECS, VECS), F32)
    for j in range(2):
        own = own_ref[j]
        gram = gram + lax.dot_general(own, own, NT_DIMS, preferred_element_type=F32)
        weighted = own.astype(F32) * (0.5 * e_ref[j : j + 1, :])
        for part in split3(weighted):
            cross = cross + lax.dot_general(own, part, NT_DIMS, preferred_element_type=F32)
    message = gram_message(gram, cross)
    for r in range(NR):
        out_ref[r, GROUP] = message


def widen(value):
    return jnp.concatenate([value, jnp.zeros((VECS, LANES - VECS), F32)], axis=1)


def message_of(gram, cross):
    total = jnp.zeros((VECS, LANES), F32)
    for base, value in ((0, gram), (HALF, cross)):
        for n, part in enumerate(split3(value)):
            part = part.astype(F32)
            total = total + (pltpu.roll(part, base + n * VECS, 1) if base + n else part)
    return total.astype(BF16)


def gram_message(gram, cross):
    return message_of(widen(gram), widen(cross))


def read_message(total):
    keep = lane_index() < VECS
    found = []
    for base in (0, HALF):
        value = jnp.zeros((VECS, LANES), F32)
        for n in (2, 1, 0):
            shift = base + n * VECS
            value = value + (pltpu.roll(total, LANES - shift, 1) if shift else total)
        found.append(jnp.where(keep, value, 0.0))
    return found


def collect_kernel(with_gram, in_ref, out_ref, back_ref):
    for r in range(NR):
        for s in range(2):
            for j in range(2):
                out_ref[2 * r + s, j] = in_ref[r, 2 * s + j]
    for j in range(2):
        total = in_ref[0, 4 + j].astype(F32)
        for r in range(1, NR):
            total = total + in_ref[r, 4 + j].astype(F32)
        back_ref[j] = total
    if with_gram:
        total = in_ref[0, GROUP].astype(F32)
        for r in range(1, NR):
            total = total + in_ref[r, GROUP].astype(F32)
        message = message_of(*read_message(total))
        for c in range(NC):
            out_ref[c, 2] = message


def solve_kernel(in_ref, back_ref, own_ref, e_ref, out_ref, residual_ref):
    def total_of(g):
        total = in_ref[0, g].astype(F32)
        for c in range(1, NC):
            total = total + in_ref[c, g].astype(F32)
        return total

    gram, cross = read_message(total_of(2))
    wide = jnp.concatenate([cross, jnp.zeros((LANES - VECS, LANES), F32)], axis=0)
    cross = cross + jnp.transpose(wide)[:VECS]
    state = jnp.concatenate([gram, cross], axis=0)
    lane = lax.broadcasted_iota(jnp.int32, (2 * VECS, LANES), 1)
    for p in range(VECS):
        column = state[:, p : p + 1]
        pivot = state[p : p + 1, :]
        scaled = pivot / state[p : p + 1, p : p + 1]
        scaled = jnp.where(lane[:1] == p, 0.0, scaled)
        own_column = column / state[p : p + 1, p : p + 1]
        state = jnp.where(lane == p, own_column, state - column * scaled)
    mix = state[VECS:]
    for j in range(2):
        v = own_ref[j].astype(F32)
        product = total_of(j) + back_ref[j] + e_ref[j : j + 1, :] * v
        shifted = jnp.zeros((VECS, LANES), F32)
        for k in range(VECS):
            shifted = shifted + mix[:, k : k + 1] * v[k : k + 1, :]
        value = (product - shifted).astype(BF16)
        residual_ref[j] = value
        for c in range(NC):
            out_ref[c, j] = value


def finish_kernel(in_ref, back_ref, own_ref, e_ref, out_ref):
    for j in range(2):
        total = in_ref[0, j].astype(F32)
        for c in range(1, NC):
            total = total + in_ref[c, j].astype(F32)
        out_ref[j] = total + back_ref[j] + e_ref[j : j + 1, :] * own_ref[j].astype(F32)


def exchange(value, axis):
    return lax.all_to_all(value, axis, split_axis=0, concat_axis=0, tiled=True)


def apply_tiles(own, spread, index, tiles, energies, with_gram):
    by_block = exchange(spread, "col")
    grouped = call(regroup_kernel, shape(NR, GROUP, VECS, LANES), 2)(own, by_block)
    fields = exchange(grouped, "row")
    scratch = [
        pltpu.VMEM((DEAD + 1, VECS, LANES), BF16),
        pltpu.VMEM((DEAD + 1, VECS, LANES), F32),
        pltpu.VMEM((DEAD + 1, VECS, LANES), F32),
    ]
    extra = 1 if with_gram else 0
    args = (index, fields, tiles) + ((own, energies) if with_gram else ())
    partial = call(
        functools.partial(tiles_kernel, with_gram),
        shape(NR, GROUP + extra, VECS, LANES),
        len(args),
        scratch,
        smem_first=True,
    )(*args)
    moved = exchange(partial, "row")
    by_block, back = call(
        functools.partial(collect_kernel, with_gram),
        (shape(NC, 2 + extra, VECS, LANES), shape(2, VECS, LANES, dtype=F32)),
        1,
    )(moved)
    return exchange(by_block, "col"), back


def shards(vectors, tile_values, tile_coords, tile_counts, energies):
    tiles = tile_values[0]
    coords = tile_coords[:, 0]
    pair = coords // 2
    major = pair // NC
    within = jnp.stack([(pair[0] % 2) * 2 + major[0] % 2, 4 + major[1] % 2])
    index = ((major // 2) * GROUP + within) * 2 + coords % 2
    live = jnp.arange(SLOTS, dtype=jnp.int32) < tile_counts[0, 0]
    index = jnp.where(live[None], index, DEAD)

    own = jnp.transpose(vectors, (1, 0, 2))
    spread = call(spread_kernel, shape(NC, 2, VECS, LANES), 1)(own)
    forward, back = apply_tiles(own, spread, index, tiles, energies, True)
    spread, residual = call(
        solve_kernel, (shape(NC, 2, VECS, LANES), shape(2, VECS, LANES)), 4
    )(forward, back, own, energies)
    forward, back = apply_tiles(residual, spread, index, tiles, energies, False)
    image = call(finish_kernel, shape(2, VECS, LANES, dtype=F32), 4)(
        forward, back, residual, energies
    )
    return jnp.transpose(residual, (1, 0, 2)), jnp.transpose(image, (1, 0, 2))


def solution(mesh):
    in_specs = (
        P(None, "row", "col"),
        P("row", "col", None, None),
        P(None, "row", "col"),
        P("row", "col"),
        P("row", "col"),
    )
    out_specs = (P(None, "row", "col"), P(None, "row", "col"))
    return jax.shard_map(shards, mesh=mesh, in_specs=in_specs, out_specs=out_specs, check_vma=False)
```

```python
import functools

import jax
import jax.numpy as jnp
from jax import lax
from jax.experimental import pallas as pl
from jax.experimental.pallas import tpu as pltpu
from jax.sharding import PartitionSpec as P

F32 = jnp.float32
BF16 = jnp.bfloat16
VECS = 16
LANES = 128
HALF = 64
NR = 16
NC = 32
GROUP = 6
SLOTS = 128
UNROLL = 8
ROW_DEAD = NR * 8
COL_DEAD = NR * 4
VMEM = pl.BlockSpec(memory_space=pltpu.VMEM)
SMEM = pl.BlockSpec(memory_space=pltpu.SMEM)
NT_DIMS = (((1,), (1,)), ((), ()))


def shape(*dims, dtype=BF16):
    return jax.ShapeDtypeStruct(dims, dtype)


def call(kernel, outs, n_in, scratch=(), smem_first=False, limit=None):
    specs = [VMEM] * n_in
    if smem_first:
        specs[0] = SMEM
    return pl.pallas_call(
        kernel,
        out_shape=outs,
        in_specs=specs,
        out_specs=jax.tree.map(lambda _: VMEM, outs),
        scratch_shapes=list(scratch),
        compiler_params=pltpu.CompilerParams(vmem_limit_bytes=limit or 32 * 1024 * 1024),
    )


def lane_index():
    return lax.broadcasted_iota(jnp.int32, (VECS, LANES), 1)


def split3(value):
    high = value.astype(BF16)
    rest = value - high.astype(F32)
    middle = rest.astype(BF16)
    low = (rest - middle.astype(F32)).astype(BF16)
    return high, middle, low


def spread_kernel(x_ref, out_ref, own_ref):
    for j in range(2):
        value = x_ref[:, j, :]
        own_ref[j] = value
        for c in range(NC):
            out_ref[c, j * VECS : (j + 1) * VECS] = value


def regroup_kernel(own_ref, in_ref, out_ref):
    wide = 2 * VECS
    for r in range(NR):
        for s in range(2):
            out_ref[r, s * wide : (s + 1) * wide] = in_ref[2 * r + s, :wide]
        for j in range(2):
            out_ref[r, 2 * wide + j * VECS : 2 * wide + (j + 1) * VECS] = own_ref[j]


def tiles_kernel(with_gram, *refs):
    if with_gram:
        idx_ref, x_ref, w_ref, own_ref, e_ref, out_ref, *scratch = refs
    else:
        idx_ref, x_ref, w_ref, out_ref, *scratch = refs
    field_row, field_col, acc_row, acc_col = scratch[:4]
    low_half = lane_index() < HALF
    zero = jnp.zeros((VECS, LANES), F32)
    half_mask = [low_half, jnp.logical_not(low_half)]
    half_one = [jnp.where(m, 1.0, 0.0).astype(BF16) for m in half_mask]

    def part(g):
        return slice(g * VECS, (g + 1) * VECS)

    def place(r, g):
        if g < 4:
            return field_row, acc_row, r * 8 + g * 2
        return field_col, acc_col, r * 4 + (g - 4) * 2

    def duplicate(r, carry):
        for g in range(GROUP):
            value = x_ref[r, part(g)].astype(F32)
            turned = pltpu.roll(value, HALF, 1)
            field, acc, at = place(r, g)
            field[at] = jnp.where(low_half, value, turned).astype(BF16)
            field[at + 1] = jnp.where(low_half, turned, value).astype(BF16)
            acc[at] = zero
            acc[at + 1] = zero
        return carry

    lax.fori_loop(0, NR, duplicate, 0, unroll=4)
    for field, acc, dead in ((field_row, acc_row, ROW_DEAD), (field_col, acc_col, COL_DEAD)):
        field[dead] = zero.astype(BF16)
        acc[dead] = zero

    def block(b, carry):
        work = []
        for u in range(UNROLL):
            q = b * UNROLL + u
            rows = [idx_ref[0, q * 4 + k] for k in range(4)]
            cols = [idx_ref[1, q * 4 + k] for k in range(4)]
            w = w_ref[pl.ds(2 * q, 2)].reshape(2 * HALF, LANES)
            left_f = jnp.concatenate([field_col[cols[k]] * half_one[k % 2] for k in range(4)], axis=0)
            left_b = jnp.concatenate([field_row[rows[k]] * half_one[k // 2] for k in range(4)], axis=0)
            forward = lax.dot_general(left_f, w, NT_DIMS, preferred_element_type=F32)
            backward = jnp.dot(left_b, w, preferred_element_type=F32)
            work.append((rows, cols, forward, backward))
        for rows, cols, forward, backward in work:
            for k in range(4):
                acc_row[rows[k]] += jnp.where(half_mask[k // 2], forward[part(k)], 0.0)
                acc_col[cols[k]] += jnp.where(half_mask[k % 2], backward[part(k)], 0.0)
        return carry

    lax.fori_loop(0, SLOTS // 4 // UNROLL, block, 0)

    def pack(r, carry):
        for g in range(GROUP):
            _, acc, at = place(r, g)
            first, second = acc[at], acc[at + 1]
            total = jnp.where(low_half, first, second) + pltpu.roll(
                jnp.where(low_half, second, first), HALF, 1
            )
            out_ref[r, part(g)] = total.astype(BF16)
            if with_gram and g >= 4:
                for n, term in enumerate(split3(total)):
                    scratch[4][n, r * 2 + g - 4] = term
        return carry

    lax.fori_loop(0, NR, pack, 0, unroll=4)
    if not with_gram:
        return
    terms = scratch[4]
    left = jnp.concatenate(
        [jnp.concatenate([terms[n, p] for p in range(2 * NR)], axis=1) for n in range(3)], axis=0
    )
    right = jnp.concatenate([x_ref[r, part(g)] for r in range(NR) for g in (4, 5)], axis=1)
    crosses = lax.dot_general(left, right, NT_DIMS, preferred_element_type=F32)
    cross = crosses[:VECS] + crosses[VECS : 2 * VECS] + crosses[2 * VECS :]
    gram = jnp.zeros((VECS, VECS), F32)
    for j in range(2):
        own = own_ref[j]
        gram = gram + lax.dot_general(own, own, NT_DIMS, preferred_element_type=F32)
        weighted = own.astype(F32) * (0.5 * e_ref[j : j + 1, :])
        for term in split3(weighted):
            cross = cross + lax.dot_general(term, own, NT_DIMS, preferred_element_type=F32)
    message = message_of(widen(gram), widen(cross))
    for r in range(NR):
        out_ref[r, part(GROUP)] = message


def widen(value):
    return jnp.concatenate([value, jnp.zeros((VECS, LANES - VECS), F32)], axis=1)


def message_of(gram, cross):
    total = jnp.zeros((VECS, LANES), F32)
    for base, value in ((0, gram), (HALF, cross)):
        for n, part in enumerate(split3(value)):
            part = part.astype(F32)
            total = total + (pltpu.roll(part, base + n * VECS, 1) if base + n else part)
    return total.astype(BF16)


def read_message(total):
    keep = lane_index() < VECS
    found = []
    for base in (0, HALF):
        value = jnp.zeros((VECS, LANES), F32)
        for n in (2, 1, 0):
            shift = base + n * VECS
            value = value + (pltpu.roll(total, LANES - shift, 1) if shift else total)
        found.append(jnp.where(keep, value, 0.0))
    return found


def collect_kernel(with_gram, in_ref, out_ref, back_ref):
    wide = 2 * VECS
    for r in range(NR):
        for s in range(2):
            out_ref[2 * r + s, :wide] = in_ref[r, s * wide : (s + 1) * wide]

    def total_of(g):
        part = slice(g * VECS, (g + 1) * VECS)
        total = in_ref[0, part].astype(F32)
        for r in range(1, NR):
            total = total + in_ref[r, part].astype(F32)
        return total

    for j in range(2):
        back_ref[j] = total_of(4 + j)
    if with_gram:
        message = message_of(*read_message(total_of(GROUP)))
        for c in range(NC):
            out_ref[c, wide:] = message


def sum_over(in_ref, g):
    part = slice(g * VECS, (g + 1) * VECS)
    total = in_ref[0, part].astype(F32)
    for c in range(1, NC):
        total = total + in_ref[c, part].astype(F32)
    return total


def solve_kernel(in_ref, back_ref, own_ref, e_ref, out_ref, residual_ref, result_ref):
    gram, cross = read_message(sum_over(in_ref, 2))
    wide = jnp.concatenate([cross, jnp.zeros((LANES - VECS, LANES), F32)], axis=0)
    cross = cross + jnp.transpose(wide)[:VECS]
    state = jnp.concatenate([gram, cross], axis=0)
    lane = lax.broadcasted_iota(jnp.int32, (2 * VECS, LANES), 1)
    for p in range(VECS):
        column = state[:, p : p + 1]
        pivot = state[p : p + 1, :]
        scaled = pivot / state[p : p + 1, p : p + 1]
        scaled = jnp.where(lane[:1] == p, 0.0, scaled)
        own_column = column / state[p : p + 1, p : p + 1]
        state = jnp.where(lane == p, own_column, state - column * scaled)
    mix = state[VECS:]
    for j in range(2):
        v = own_ref[j].astype(F32)
        product = sum_over(in_ref, j) + back_ref[j] + e_ref[j : j + 1, :] * v
        shifted = jnp.zeros((VECS, LANES), F32)
        for k in range(VECS):
            shifted = shifted + mix[:, k : k + 1] * v[k : k + 1, :]
        value = (product - shifted).astype(BF16)
        residual_ref[j] = value
        result_ref[:, j, :] = value
        for c in range(NC):
            out_ref[c, j * VECS : (j + 1) * VECS] = value


def finish_kernel(in_ref, back_ref, own_ref, e_ref, out_ref):
    for j in range(2):
        total = sum_over(in_ref, j) + back_ref[j]
        out_ref[:, j, :] = total + e_ref[j : j + 1, :] * own_ref[j].astype(F32)


def exchange(value, axis):
    return lax.all_to_all(value, axis, split_axis=0, concat_axis=0, tiled=True)


def apply_tiles(own, spread, index, tiles, energies, with_gram):
    by_block = exchange(spread, "col")
    grouped = call(regroup_kernel, shape(NR, GROUP * VECS, LANES), 2)(own, by_block)
    fields = exchange(grouped, "row")
    scratch = [
        pltpu.VMEM((ROW_DEAD + 1, VECS, LANES), BF16),
        pltpu.VMEM((COL_DEAD + 1, VECS, LANES), BF16),
        pltpu.VMEM((ROW_DEAD + 1, VECS, LANES), F32),
        pltpu.VMEM((COL_DEAD + 1, VECS, LANES), F32),
    ]
    extra = 0
    args = (index, fields, tiles)
    if with_gram:
        extra = 1
        args = args + (own, energies)
        scratch.append(pltpu.VMEM((3, 2 * NR, VECS, LANES), BF16))
    partial = call(
        functools.partial(tiles_kernel, with_gram),
        shape(NR, (GROUP + extra) * VECS, LANES),
        len(args),
        scratch,
        smem_first=True,
    )(*args)
    moved = exchange(partial, "row")
    by_block, back = call(
        functools.partial(collect_kernel, with_gram),
        (shape(NC, (2 + extra) * VECS, LANES), shape(2, VECS, LANES, dtype=F32)),
        1,
    )(moved)
    return exchange(by_block, "col"), back


def shards(vectors, tile_values, tile_coords, tile_counts, energies):
    tiles = tile_values[0]
    coords = tile_coords[:, 0]
    pair = coords // 2
    major = pair // NC
    rows = (major[0] // 2 * 4 + pair[0] % 2 * 2 + major[0] % 2) * 2 + coords[0] % 2
    cols = major[1] * 2 + coords[1] % 2
    live = jnp.arange(SLOTS, dtype=jnp.int32) < tile_counts[0, 0]
    index = jnp.stack([jnp.where(live, rows, ROW_DEAD), jnp.where(live, cols, COL_DEAD)])
    vectors, index = lax.optimization_barrier((vectors, index))

    spread, own = call(
        spread_kernel, (shape(NC, 2 * VECS, LANES), shape(2, VECS, LANES)), 1
    )(vectors)
    forward, back = apply_tiles(own, spread, index, tiles, energies, True)
    spread, residual, result = call(
        solve_kernel,
        (shape(NC, 2 * VECS, LANES), shape(2, VECS, LANES), shape(VECS, 2, LANES)),
        4,
    )(forward, back, own, energies)
    forward, back = apply_tiles(residual, spread, index, tiles, energies, False)
    image = call(finish_kernel, shape(VECS, 2, LANES, dtype=F32), 4)(
        forward, back, residual, energies
    )
    return result, image


def solution(mesh):
    in_specs = (
        P(None, "row", "col"),
        P("row", "col", None, None),
        P(None, "row", "col"),
        P("row", "col"),
        P("row", "col"),
    )
    out_specs = (P(None, "row", "col"), P(None, "row", "col"))
    return jax.shard_map(shards, mesh=mesh, in_specs=in_specs, out_specs=out_specs, check_vma=False)
```

```python
import functools

import jax
import jax.numpy as jnp
import numpy as np
from jax import lax
from jax.experimental import pallas as pl
from jax.experimental.pallas import tpu as pltpu
from jax.sharding import PartitionSpec as P

F32 = jnp.float32
BF16 = jnp.bfloat16
VECS = 16
LANES = 128
HALF = 64
NR = 16
NC = 32
GROUP = 6
SLOTS = 128
UNROLL = 16
ROW_DEAD = NR * 8
COL_DEAD = NR * 4
ROW = ("x", "core", "zh")
COL = ("zl", "y")
VMEM = pl.BlockSpec(memory_space=pltpu.VMEM)
SMEM = pl.BlockSpec(memory_space=pltpu.SMEM)
NT_DIMS = (((1,), (1,)), ((), ()))


def row_at(r):
    return (r % 8) * 2 + r // 8


def col_at(c):
    return (c % 4) * 8 + c // 4


def shape(*dims, dtype=BF16):
    return jax.ShapeDtypeStruct(dims, dtype)


def call(kernel, outs, n_in, scratch=(), scalars=(), first=VMEM, limit=32):
    specs = [SMEM if n in scalars else first for n in range(n_in)]
    return pl.pallas_call(
        kernel,
        out_shape=outs,
        in_specs=specs,
        out_specs=jax.tree.map(lambda _: VMEM, outs),
        scratch_shapes=list(scratch),
        compiler_params=pltpu.CompilerParams(vmem_limit_bytes=limit * 1024 * 1024),
    )


def lane_index():
    return lax.broadcasted_iota(jnp.int32, (VECS, LANES), 1)


def split3(value):
    high = value.astype(BF16)
    rest = value - high.astype(F32)
    middle = rest.astype(BF16)
    low = (rest - middle.astype(F32)).astype(BF16)
    return high, middle, low


def spread_kernel(
    x_hbm, coords_hbm, counts_hbm, e_hbm, out_ref, own_ref, index_ref, energy_ref, x_ref, coords_ref, counts_ref, sems
):
    pairs = ((x_hbm, x_ref), (coords_hbm, coords_ref), (counts_hbm, counts_ref), (e_hbm, energy_ref))
    copies = [pltpu.make_async_copy(a, b, sems.at[n]) for n, (a, b) in enumerate(pairs)]
    for copy in copies:
        copy.start()
    for copy in copies:
        copy.wait()
    for j in range(2):
        value = x_ref[:, j, :]
        own_ref[j] = value
        for c in range(NC):
            out_ref[c, j * VECS : (j + 1) * VECS] = value
    live = lax.broadcasted_iota(jnp.int32, (1, SLOTS), 1) < counts_ref[0, 0]
    for n, dead in ((0, ROW_DEAD), (1, COL_DEAD)):
        coords = coords_ref[n]
        major = coords >> 6
        source = major >> 1
        group = ((source & 7) << 1) + (source >> 3)
        if n == 0:
            group = group * 2 + ((coords >> 1) & 1)
        tile = (group * 2 + (major & 1)) * 2 + (coords & 1)
        index_ref[n : n + 1] = jnp.where(live, tile, dead)


def regroup_kernel(own_ref, in_ref, out_ref):
    wide = 2 * VECS
    for r in range(NR):
        at = row_at(r)
        for s in range(2):
            out_ref[at, s * wide : (s + 1) * wide] = in_ref[col_at(2 * r + s), :wide]
        for j in range(2):
            out_ref[at, 2 * wide + j * VECS : 2 * wide + (j + 1) * VECS] = own_ref[j]


def tiles_kernel(with_gram, *refs):
    if with_gram:
        idx_ref, x_ref, w_ref, own_ref, e_ref, out_ref, *scratch = refs
    else:
        idx_ref, x_ref, w_ref, out_ref, *scratch = refs
    field_row, field_col, acc_row, acc_col = scratch[:4]
    low_half = lane_index() < HALF
    zero = jnp.zeros((VECS, LANES), F32)
    half_mask = [low_half, jnp.logical_not(low_half)]
    half_one = [jnp.where(m, 1.0, 0.0).astype(BF16) for m in half_mask]

    def part(g):
        return slice(g * VECS, (g + 1) * VECS)

    def place(r, g):
        if g < 4:
            return field_row, acc_row, r * 8 + g * 2
        return field_col, acc_col, r * 4 + (g - 4) * 2

    def duplicate(r, carry):
        for g in range(GROUP):
            value = x_ref[r, part(g)].astype(F32)
            turned = pltpu.roll(value, HALF, 1)
            field, acc, at = place(r, g)
            field[at] = jnp.where(low_half, value, turned).astype(BF16)
            field[at + 1] = jnp.where(low_half, turned, value).astype(BF16)
            acc[at] = zero
            acc[at + 1] = zero
        return carry

    lax.fori_loop(0, NR, duplicate, 0, unroll=4)
    for field, acc, dead in ((field_row, acc_row, ROW_DEAD), (field_col, acc_col, COL_DEAD)):
        field[dead] = zero.astype(BF16)
        acc[dead] = zero

    def block(b, carry):
        work = []
        for u in range(UNROLL):
            q = b * UNROLL + u
            rows = [idx_ref[0, q * 4 + k] for k in range(4)]
            cols = [idx_ref[1, q * 4 + k] for k in range(4)]
            w = w_ref[pl.ds(2 * q, 2)].reshape(2 * HALF, LANES)
            left_f = jnp.concatenate([field_col[cols[k]] * half_one[k % 2] for k in range(4)], axis=0)
            left_b = jnp.concatenate([field_row[rows[k]] * half_one[k // 2] for k in range(4)], axis=0)
            forward = lax.dot_general(left_f, w, NT_DIMS, preferred_element_type=F32)
            backward = jnp.dot(left_b, w, preferred_element_type=F32)
            work.append((rows, cols, forward, backward))
        for rows, cols, forward, backward in work:
            for k in range(4):
                acc_row[rows[k]] += jnp.where(half_mask[k // 2], forward[part(k)], 0.0)
                acc_col[cols[k]] += jnp.where(half_mask[k % 2], backward[part(k)], 0.0)
        return carry

    lax.fori_loop(0, SLOTS // 4 // UNROLL, block, 0)

    def pack(r, carry):
        for g in range(GROUP):
            _, acc, at = place(r, g)
            first, second = acc[at], acc[at + 1]
            total = jnp.where(low_half, first, second) + pltpu.roll(
                jnp.where(low_half, second, first), HALF, 1
            )
            out_ref[r, part(g)] = total.astype(BF16)
            if with_gram and g >= 4:
                for n, term in enumerate(split3(total)):
                    scratch[4][n, r * 2 + g - 4] = term
        return carry

    lax.fori_loop(0, NR, pack, 0, unroll=4)
    if not with_gram:
        return
    terms = scratch[4]
    left = jnp.concatenate(
        [jnp.concatenate([terms[n, p] for p in range(2 * NR)], axis=1) for n in range(3)], axis=0
    )
    right = jnp.concatenate([x_ref[r, part(g)] for r in range(NR) for g in (4, 5)], axis=1)
    crosses = lax.dot_general(left, right, NT_DIMS, preferred_element_type=F32)
    cross = crosses[:VECS] + crosses[VECS : 2 * VECS] + crosses[2 * VECS :]
    gram = jnp.zeros((VECS, VECS), F32)
    for j in range(2):
        own = own_ref[j]
        gram = gram + lax.dot_general(own, own, NT_DIMS, preferred_element_type=F32)
        weighted = own.astype(F32) * (0.5 * e_ref[j : j + 1, :])
        for term in split3(weighted):
            cross = cross + lax.dot_general(term, own, NT_DIMS, preferred_element_type=F32)
    message = message_of(widen(gram), widen(cross))
    for r in range(NR):
        out_ref[r, part(GROUP)] = message


def widen(value):
    return jnp.concatenate([value, jnp.zeros((VECS, LANES - VECS), F32)], axis=1)


def message_of(gram, cross):
    total = jnp.zeros((VECS, LANES), F32)
    for base, value in ((0, gram), (HALF, cross)):
        for n, part in enumerate(split3(value)):
            part = part.astype(F32)
            total = total + (pltpu.roll(part, base + n * VECS, 1) if base + n else part)
    return total.astype(BF16)


def read_message(total):
    keep = lane_index() < VECS
    found = []
    for base in (0, HALF):
        value = jnp.zeros((VECS, LANES), F32)
        for n in (2, 1, 0):
            shift = base + n * VECS
            value = value + (pltpu.roll(total, LANES - shift, 1) if shift else total)
        found.append(jnp.where(keep, value, 0.0))
    return found


def collect_kernel(with_gram, in_ref, out_ref, back_ref):
    wide = 2 * VECS
    for r in range(NR):
        for s in range(2):
            out_ref[col_at(2 * r + s), :wide] = in_ref[row_at(r), s * wide : (s + 1) * wide]

    def total_of(g):
        part = slice(g * VECS, (g + 1) * VECS)
        total = in_ref[0, part].astype(F32)
        for r in range(1, NR):
            total = total + in_ref[r, part].astype(F32)
        return total

    for j in range(2):
        back_ref[j] = total_of(4 + j)
    if with_gram:
        message = message_of(*read_message(total_of(GROUP)))
        for c in range(NC):
            out_ref[c, wide:] = message


def sum_over(in_ref, g):
    part = slice(g * VECS, (g + 1) * VECS)
    total = in_ref[0, part].astype(F32)
    for c in range(1, NC):
        total = total + in_ref[c, part].astype(F32)
    return total


def solve_kernel(in_ref, back_ref, own_ref, e_ref, out_ref, residual_ref, result_ref):
    gram, cross = read_message(sum_over(in_ref, 2))
    wide = jnp.concatenate([cross, jnp.zeros((LANES - VECS, LANES), F32)], axis=0)
    cross = cross + jnp.transpose(wide)[:VECS]
    state = jnp.concatenate([gram, cross], axis=0)
    lane = lax.broadcasted_iota(jnp.int32, (2 * VECS, LANES), 1)
    for p in range(0, VECS, 2):
        first, second = state[:, p : p + 1], state[:, p + 1 : p + 2]
        a, b = first[p : p + 1], second[p : p + 1]
        c, d = first[p + 1 : p + 2], second[p + 1 : p + 2]
        scale = 1.0 / (a * d - b * c)
        new_first = (first * d - second * c) * scale
        new_second = (second * a - first * b) * scale
        rest = state - new_first * state[p : p + 1] - new_second * state[p + 1 : p + 2]
        state = jnp.where(lane == p, new_first, jnp.where(lane == p + 1, new_second, rest))
    mix = state[VECS:]
    for j in range(2):
        v = own_ref[j].astype(F32)
        product = sum_over(in_ref, j) + back_ref[j] + e_ref[j : j + 1, :] * v
        shifted = jnp.zeros((VECS, LANES), F32)
        for k in range(VECS):
            shifted = shifted + mix[:, k : k + 1] * v[k : k + 1, :]
        value = (product - shifted).astype(BF16)
        residual_ref[j] = value
        result_ref[:, j, :] = value
        for c in range(NC):
            out_ref[c, j * VECS : (j + 1) * VECS] = value


def finish_kernel(in_ref, back_ref, own_ref, e_ref, out_ref):
    for j in range(2):
        total = sum_over(in_ref, j) + back_ref[j]
        out_ref[:, j, :] = total + e_ref[j : j + 1, :] * own_ref[j].astype(F32)


def exchange(value, axis):
    return lax.all_to_all(value, axis, split_axis=0, concat_axis=0, tiled=True)


def apply_tiles(own, spread, index, tiles, energies, with_gram):
    by_block = exchange(spread, COL)
    grouped = call(regroup_kernel, shape(NR, GROUP * VECS, LANES), 2)(own, by_block)
    fields = exchange(grouped, ROW)
    scratch = [
        pltpu.VMEM((ROW_DEAD + 1, VECS, LANES), BF16),
        pltpu.VMEM((COL_DEAD + 1, VECS, LANES), BF16),
        pltpu.VMEM((ROW_DEAD + 1, VECS, LANES), F32),
        pltpu.VMEM((COL_DEAD + 1, VECS, LANES), F32),
    ]
    extra = 0
    args = (index, fields, tiles)
    if with_gram:
        extra = 1
        args = args + (own, energies)
        scratch.append(pltpu.VMEM((3, 2 * NR, VECS, LANES), BF16))
    partial = call(
        functools.partial(tiles_kernel, with_gram),
        shape(NR, (GROUP + extra) * VECS, LANES),
        len(args),
        scratch,
        scalars=(0,),
    )(*args)
    moved = exchange(partial, ROW)
    by_block, back = call(
        functools.partial(collect_kernel, with_gram),
        (shape(NC, (2 + extra) * VECS, LANES), shape(2, VECS, LANES, dtype=F32)),
        1,
    )(moved)
    return exchange(by_block, COL), back


def shards(vectors, tile_values, tile_coords, tile_counts, energies):
    tiles = tile_values[0]
    spread, own, index, energies = call(
        spread_kernel,
        (
            shape(NC, 2 * VECS, LANES),
            shape(2, VECS, LANES),
            shape(2, SLOTS, dtype=jnp.int32),
            shape(2, LANES, dtype=F32),
        ),
        4,
        [
            pltpu.VMEM((VECS, 2, LANES), BF16),
            pltpu.VMEM((2, 1, SLOTS), jnp.int32),
            pltpu.SMEM((1, 1), jnp.int32),
            pltpu.SemaphoreType.DMA((4,)),
        ],
        first=pl.BlockSpec(memory_space=pl.ANY),
        limit=60,
    )(vectors, tile_coords, tile_counts, energies)
    forward, back = apply_tiles(own, spread, index, tiles, energies, True)
    spread, residual, result = call(
        solve_kernel,
        (shape(NC, 2 * VECS, LANES), shape(2, VECS, LANES), shape(VECS, 2, LANES)),
        4,
    )(forward, back, own, energies)
    forward, back = apply_tiles(residual, spread, index, tiles, energies, False)
    image = call(finish_kernel, shape(VECS, 2, LANES, dtype=F32), 4)(
        forward, back, residual, energies
    )
    return result, image


def solution(mesh):
    devices = np.asarray(mesh.devices).reshape(2, 4, 2, 8, 4)
    fine = jax.sharding.Mesh(devices, ("zh", "x", "core", "y", "zl"))
    row, col = ("zh", "x", "core"), ("y", "zl")
    in_specs = (
        P(None, row, col),
        P(row, col, None, None),
        P(None, row, col),
        P(row, col),
        P(row, col),
    )
    out_specs = (P(None, row, col), P(None, row, col))
    return jax.shard_map(shards, mesh=fine, in_specs=in_specs, out_specs=out_specs, check_vma=False)
```

```python
import functools

import jax
import jax.numpy as jnp
import numpy as np
from jax import lax
from jax.experimental import pallas as pl
from jax.experimental.pallas import tpu as pltpu
from jax.sharding import PartitionSpec as P

F32 = jnp.float32
BF16 = jnp.bfloat16
VECS = 16
LANES = 128
HALF = 64
MESSAGE = 8
NR = 16
NC = 32
GROUP = 6
SLOTS = 128
UNROLL = 16
ROW_DEAD = NR * 8
COL_DEAD = NR * 4
ROW = ("x", "core", "zh")
COL = ("zl", "y")
VMEM = pl.BlockSpec(memory_space=pltpu.VMEM)
SMEM = pl.BlockSpec(memory_space=pltpu.SMEM)
NT_DIMS = (((1,), (1,)), ((), ()))


def row_at(r):
    return (r % 8) * 2 + r // 8


def col_at(c):
    return (c % 4) * 8 + c // 4


def shape(*dims, dtype=BF16):
    return jax.ShapeDtypeStruct(dims, dtype)


def call(kernel, outs, n_in, scratch=(), scalars=(), first=VMEM, limit=32):
    specs = [SMEM if n in scalars else first for n in range(n_in)]
    return pl.pallas_call(
        kernel,
        out_shape=outs,
        in_specs=specs,
        out_specs=jax.tree.map(lambda _: VMEM, outs),
        scratch_shapes=list(scratch),
        compiler_params=pltpu.CompilerParams(vmem_limit_bytes=limit * 1024 * 1024),
    )


def lane_index():
    return lax.broadcasted_iota(jnp.int32, (VECS, LANES), 1)


def split2(value):
    high = value.astype(BF16)
    return high, (value - high.astype(F32)).astype(BF16)


def split3(value):
    high = value.astype(BF16)
    rest = value - high.astype(F32)
    middle = rest.astype(BF16)
    low = (rest - middle.astype(F32)).astype(BF16)
    return high, middle, low


def spread_kernel(
    x_hbm, coords_hbm, counts_hbm, e_hbm, out_ref, index_ref, energy_ref, x_ref, coords_ref, counts_ref, sems
):
    pairs = ((x_hbm, x_ref), (coords_hbm, coords_ref), (counts_hbm, counts_ref), (e_hbm, energy_ref))
    copies = [pltpu.make_async_copy(a, b, sems.at[n]) for n, (a, b) in enumerate(pairs)]
    for copy in copies:
        copy.start()
    for copy in copies:
        copy.wait()
    for j in range(2):
        value = x_ref[:, j, :]
        for c in range(NC):
            out_ref[c, j * VECS : (j + 1) * VECS] = value
    live = lax.broadcasted_iota(jnp.int32, (1, SLOTS), 1) < counts_ref[0, 0]
    for n, dead in ((0, ROW_DEAD), (1, COL_DEAD)):
        coords = coords_ref[n]
        major = coords >> 6
        source = major >> 1
        group = ((source & 7) << 1) + (source >> 3)
        if n == 0:
            group = group * 2 + ((coords >> 1) & 1)
        tile = (group * 2 + (major & 1)) * 2 + (coords & 1)
        index_ref[n : n + 1] = jnp.where(live, tile, dead)


def regroup_kernel(in_ref, out_ref, own_ref):
    wide = 2 * VECS
    own = in_ref[lax.axis_index("zl") * 8 + lax.axis_index("y")]
    for j in range(2):
        own_ref[j] = own[j * VECS : (j + 1) * VECS]
    for r in range(NR):
        at = row_at(r)
        for s in range(2):
            out_ref[at, s * wide : (s + 1) * wide] = in_ref[col_at(2 * r + s)]
        out_ref[at, 2 * wide :] = own


def tiles_kernel(with_gram, *refs):
    if with_gram:
        idx_ref, x_ref, w_ref, own_ref, e_ref, out_ref, *scratch = refs
    else:
        idx_ref, x_ref, w_ref, out_ref, *scratch = refs
    field_row, field_col, acc_row, acc_col = scratch[:4]
    low_half = lane_index() < HALF
    zero = jnp.zeros((VECS, LANES), F32)
    half_mask = [low_half, jnp.logical_not(low_half)]
    half_one = [jnp.where(m, 1.0, 0.0).astype(BF16) for m in half_mask]

    def part(g):
        return slice(g * VECS, (g + 1) * VECS)

    def place(r, g):
        if g < 4:
            return field_row, acc_row, r * 8 + g * 2
        return field_col, acc_col, r * 4 + (g - 4) * 2

    def duplicate(r, carry):
        for g in range(GROUP):
            value = x_ref[r, part(g)].astype(F32)
            turned = pltpu.roll(value, HALF, 1)
            field, acc, at = place(r, g)
            field[at] = jnp.where(low_half, value, turned).astype(BF16)
            field[at + 1] = jnp.where(low_half, turned, value).astype(BF16)
            acc[at] = zero
            acc[at + 1] = zero
        return carry

    lax.fori_loop(0, NR, duplicate, 0, unroll=4)
    for field, acc, dead in ((field_row, acc_row, ROW_DEAD), (field_col, acc_col, COL_DEAD)):
        field[dead] = zero.astype(BF16)
        acc[dead] = zero

    def block(b, carry):
        work = []
        for u in range(UNROLL):
            q = b * UNROLL + u
            rows = [idx_ref[0, q * 4 + k] for k in range(4)]
            cols = [idx_ref[1, q * 4 + k] for k in range(4)]
            w = w_ref[pl.ds(2 * q, 2)].reshape(2 * HALF, LANES)
            left_f = jnp.concatenate([field_col[cols[k]] * half_one[k % 2] for k in range(4)], axis=0)
            left_b = jnp.concatenate([field_row[rows[k]] * half_one[k // 2] for k in range(4)], axis=0)
            forward = lax.dot_general(left_f, w, NT_DIMS, preferred_element_type=F32)
            backward = jnp.dot(left_b, w, preferred_element_type=F32)
            work.append((rows, cols, forward, backward))
        for rows, cols, forward, backward in work:
            for k in range(4):
                acc_row[rows[k]] += jnp.where(half_mask[k // 2], forward[part(k)], 0.0)
                acc_col[cols[k]] += jnp.where(half_mask[k % 2], backward[part(k)], 0.0)
        return carry

    lax.fori_loop(0, SLOTS // 4 // UNROLL, block, 0)

    def pack(r, carry):
        for g in range(GROUP):
            _, acc, at = place(r, g)
            first, second = acc[at], acc[at + 1]
            total = jnp.where(low_half, first, second) + pltpu.roll(
                jnp.where(low_half, second, first), HALF, 1
            )
            out_ref[r, part(g)] = total.astype(BF16)
            if with_gram and g >= 4:
                for n, term in enumerate(split3(total)):
                    scratch[4][n, r * 2 + g - 4] = term
        return carry

    lax.fori_loop(0, NR, pack, 0, unroll=4)
    if not with_gram:
        return
    terms = scratch[4]
    left = jnp.concatenate(
        [jnp.concatenate([terms[n, p] for p in range(2 * NR)], axis=1) for n in range(3)], axis=0
    )
    right = jnp.concatenate([x_ref[r, part(g)] for r in range(NR) for g in (4, 5)], axis=1)
    crosses = lax.dot_general(left, right, NT_DIMS, preferred_element_type=F32)
    cross = crosses[:VECS] + crosses[VECS : 2 * VECS] + crosses[2 * VECS :]
    gram = jnp.zeros((VECS, VECS), F32)
    for j in range(2):
        own = own_ref[j]
        gram = gram + lax.dot_general(own, own, NT_DIMS, preferred_element_type=F32)
        weighted = own.astype(F32) * (0.5 * e_ref[j : j + 1, :])
        for term in split3(weighted):
            cross = cross + lax.dot_general(term, own, NT_DIMS, preferred_element_type=F32)
    message = message_of(widen(gram), widen(cross))
    for r in range(NR):
        out_ref[r, GROUP * VECS :] = message


def widen(value):
    return jnp.concatenate([value, jnp.zeros((VECS, LANES - VECS), F32)], axis=1)


def message_of(gram, cross):
    total = jnp.zeros((VECS, LANES), F32)
    for n, part in enumerate(split2(gram) + split2(cross)):
        part = part.astype(F32)
        total = total + (pltpu.roll(part, n * VECS, 1) if n else part)
    return (total[:MESSAGE] + pltpu.roll(total[MESSAGE:], HALF, 1)).astype(BF16)


def read_message(total):
    total = jnp.concatenate([total, pltpu.roll(total, HALF, 1)], axis=0)
    keep = lane_index() < VECS
    found = []
    for n in (0, 2):
        high = pltpu.roll(total, LANES - n * VECS, 1) if n else total
        low = pltpu.roll(total, LANES - (n + 1) * VECS, 1)
        found.append(jnp.where(keep, high + low, 0.0))
    return found


def sum_over(in_ref, start, rows):
    total = in_ref[0, start : start + rows].astype(F32)
    for n in range(1, in_ref.shape[0]):
        total = total + in_ref[n, start : start + rows].astype(F32)
    return total


def collect_kernel(with_gram, in_ref, out_ref, back_ref):
    wide = 2 * VECS
    for r in range(NR):
        for s in range(2):
            out_ref[col_at(2 * r + s), :wide] = in_ref[row_at(r), s * wide : (s + 1) * wide]

    for j in range(2):
        back_ref[j] = sum_over(in_ref, (4 + j) * VECS, VECS)
    if with_gram:
        message = message_of(*read_message(sum_over(in_ref, GROUP * VECS, MESSAGE)))
        for c in range(NC):
            out_ref[c, wide:] = message


def solve_kernel(in_ref, back_ref, own_ref, e_ref, out_ref, result_ref):
    gram, cross = read_message(sum_over(in_ref, 2 * VECS, MESSAGE))
    wide = jnp.concatenate([cross, jnp.zeros((LANES - VECS, LANES), F32)], axis=0)
    cross = cross + jnp.transpose(wide)[:VECS]
    state = jnp.concatenate([gram, cross], axis=0)
    lane = lax.broadcasted_iota(jnp.int32, (2 * VECS, LANES), 1)
    for p in range(VECS):
        column = state[:, p : p + 1] * (1.0 / state[p : p + 1, p : p + 1])
        state = jnp.where(lane == p, column, state - column * state[p : p + 1])
    mix = state[VECS:]
    for j in range(2):
        v = own_ref[j].astype(F32)
        product = sum_over(in_ref, j * VECS, VECS) + back_ref[j] + e_ref[j : j + 1, :] * v
        shifted = jnp.zeros((VECS, LANES), F32)
        for k in range(VECS):
            shifted = shifted + mix[:, k : k + 1] * v[k : k + 1, :]
        value = (product - shifted).astype(BF16)
        result_ref[:, j, :] = value
        for c in range(NC):
            out_ref[c, j * VECS : (j + 1) * VECS] = value


def finish_kernel(in_ref, back_ref, own_ref, e_ref, out_ref):
    for j in range(2):
        total = sum_over(in_ref, j * VECS, VECS) + back_ref[j]
        out_ref[:, j, :] = total + e_ref[j : j + 1, :] * own_ref[j].astype(F32)


def exchange(value, axis):
    return lax.all_to_all(value, axis, split_axis=0, concat_axis=0, tiled=True)


def apply_tiles(spread, index, tiles, energies, with_gram):
    by_block = exchange(spread, COL)
    grouped, own = call(
        regroup_kernel, (shape(NR, GROUP * VECS, LANES), shape(2, VECS, LANES)), 1
    )(by_block)
    fields = exchange(grouped, ROW)
    scratch = [
        pltpu.VMEM((ROW_DEAD + 1, VECS, LANES), BF16),
        pltpu.VMEM((COL_DEAD + 1, VECS, LANES), BF16),
        pltpu.VMEM((ROW_DEAD + 1, VECS, LANES), F32),
        pltpu.VMEM((COL_DEAD + 1, VECS, LANES), F32),
    ]
    message = 0
    args = (index, fields, tiles)
    if with_gram:
        message = MESSAGE
        args = args + (own, energies)
        scratch.append(pltpu.VMEM((3, 2 * NR, VECS, LANES), BF16))
    partial = call(
        functools.partial(tiles_kernel, with_gram),
        shape(NR, GROUP * VECS + message, LANES),
        len(args),
        scratch,
        scalars=(0,),
    )(*args)
    moved = exchange(partial, ROW)
    by_block, back = call(
        functools.partial(collect_kernel, with_gram),
        (shape(NC, 2 * VECS + message, LANES), shape(2, VECS, LANES, dtype=F32)),
        1,
    )(moved)
    return exchange(by_block, COL), back, own


def shards(vectors, tile_values, tile_coords, tile_counts, energies):
    tiles = tile_values[0]
    spread, index, energies = call(
        spread_kernel,
        (
            shape(NC, 2 * VECS, LANES),
            shape(2, SLOTS, dtype=jnp.int32),
            shape(2, LANES, dtype=F32),
        ),
        4,
        [
            pltpu.VMEM((VECS, 2, LANES), BF16),
            pltpu.VMEM((2, 1, SLOTS), jnp.int32),
            pltpu.SMEM((1, 1), jnp.int32),
            pltpu.SemaphoreType.DMA((4,)),
        ],
        first=pl.BlockSpec(memory_space=pl.ANY),
        limit=60,
    )(vectors, tile_coords, tile_counts, energies)
    forward, back, own = apply_tiles(spread, index, tiles, energies, True)
    spread, result = call(
        solve_kernel, (shape(NC, 2 * VECS, LANES), shape(VECS, 2, LANES)), 4
    )(forward, back, own, energies)
    forward, back, residual = apply_tiles(spread, index, tiles, energies, False)
    image = call(finish_kernel, shape(VECS, 2, LANES, dtype=F32), 4)(
        forward, back, residual, energies
    )
    return result, image


def solution(mesh):
    devices = np.asarray(mesh.devices).reshape(2, 4, 2, 8, 4)
    fine = jax.sharding.Mesh(devices, ("zh", "x", "core", "y", "zl"))
    row, col = ("zh", "x", "core"), ("y", "zl")
    in_specs = (
        P(None, row, col),
        P(row, col, None, None),
        P(None, row, col),
        P(row, col),
        P(row, col),
    )
    out_specs = (P(None, row, col), P(None, row, col))
    return jax.shard_map(shards, mesh=fine, in_specs=in_specs, out_specs=out_specs, check_vma=False)
```

```python
import functools

import jax
import jax.numpy as jnp
import numpy as np
from jax import lax
from jax.experimental import pallas as pl
from jax.experimental.pallas import tpu as pltpu
from jax.sharding import PartitionSpec as P

F32 = jnp.float32
BF16 = jnp.bfloat16
VECS = 16
LANES = 128
HALF = 64
MESSAGE = 8
NR = 16
NC = 32
GROUP = 6
PIECES = 32
SLOTS = 128
UNROLL = 16
ROW_DEAD = NR * 8
COL_DEAD = NR * 4
ROW = ("x", "core", "zh")
COL = ("zl", "y")
PIECE = ("x", "zh", "zl")
OWNER = ("y", "core")
VMEM = pl.BlockSpec(memory_space=pltpu.VMEM)
SMEM = pl.BlockSpec(memory_space=pltpu.SMEM)
NT_DIMS = (((1,), (1,)), ((), ()))


def row_at(r):
    return (r % 8) * 2 + r // 8


def col_at(c):
    return (c % 4) * 8 + c // 4


def shape(*dims, dtype=BF16):
    return jax.ShapeDtypeStruct(dims, dtype)


def call(kernel, outs, n_in, scratch=(), scalars=(), first=VMEM, limit=32):
    specs = [SMEM if n in scalars else first for n in range(n_in)]
    return pl.pallas_call(
        kernel,
        out_shape=outs,
        in_specs=specs,
        out_specs=jax.tree.map(lambda _: VMEM, outs),
        scratch_shapes=list(scratch),
        compiler_params=pltpu.CompilerParams(vmem_limit_bytes=limit * 1024 * 1024),
    )


def lane_index():
    return lax.broadcasted_iota(jnp.int32, (VECS, LANES), 1)


def split2(value):
    high = value.astype(BF16)
    return high, (value - high.astype(F32)).astype(BF16)


def split3(value):
    high = value.astype(BF16)
    rest = value - high.astype(F32)
    middle = rest.astype(BF16)
    low = (rest - middle.astype(F32)).astype(BF16)
    return high, middle, low


def piece_at(x, zh, core, j):
    return x * 8 + zh * 4 + core * 2 + j


def locate(by_row, x, zh, core, j, slot):
    if by_row:
        place = slot * 2 + j if slot < 2 else 4 + j
        return x * 4 + core * 2 + zh, slice(place * VECS, (place + 1) * VECS)
    return piece_at(x, zh, core, j), slice(slot * VECS, (slot + 1) * VECS)


INNER = [(zh, core, j) for zh in range(2) for core in range(2) for j in range(2)]


def spread_kernel(
    x_hbm, coords_hbm, counts_hbm, e_hbm, out_ref, index_ref, energy_ref, x_ref, coords_ref, counts_ref, sems
):
    pairs = ((x_hbm, x_ref), (coords_hbm, coords_ref), (counts_hbm, counts_ref), (e_hbm, energy_ref))
    copies = [pltpu.make_async_copy(a, b, sems.at[n]) for n, (a, b) in enumerate(pairs)]
    for copy in copies:
        copy.start()
    for copy in copies:
        copy.wait()
    for j in range(2):
        value = x_ref[:, j, :]
        for c in range(NC):
            out_ref[c, j * VECS : (j + 1) * VECS] = value
    live = lax.broadcasted_iota(jnp.int32, (1, SLOTS), 1) < counts_ref[0, 0]
    for n, dead in ((0, ROW_DEAD), (1, COL_DEAD)):
        coords = coords_ref[n]
        major = coords >> 6
        piece = ((major >> 2) & 3) * 8 + (major >> 4) * 4 + (major & 3)
        if n == 0:
            piece = piece * 2 + ((coords >> 1) & 1)
        index_ref[n : n + 1] = jnp.where(live, piece * 2 + (coords & 1), dead)


def regroup_kernel(in_ref, out_ref, own_ref, kept_ref, sent_ref):
    wide = 2 * VECS
    y, zl, core = lax.axis_index("y"), lax.axis_index("zl"), lax.axis_index("core")
    own = in_ref[zl * 8 + y]
    half = lax.rem(zl, 2) == 0
    for j in range(2):
        own_ref[j] = own[j * VECS : (j + 1) * VECS]
        for target, side in ((kept_ref, core), (sent_ref, 1 - core)):
            value = in_ref[(side * 2 + j) * 8 + y]
            target[j] = jnp.where(half, value[:VECS], value[VECS:])
    for r in range(NR):
        at = row_at(r)
        for s in range(2):
            out_ref[at, s * wide : (s + 1) * wide] = in_ref[col_at(2 * r + s)]
        out_ref[at, 2 * wide :] = own


def regroup_back_kernel(in_ref, out_ref):
    y, core = lax.axis_index("y"), lax.axis_index("core")
    for zl in range(4):
        column = in_ref[y * 2 + zl // 2, (zl % 2) * VECS : (zl % 2 + 1) * VECS]
        for block in range(8):
            zh, x = block // 4, block % 4
            at = (x * 2 + zh) * 4 + zl
            out_ref[at, : 2 * VECS] = in_ref[block * 2 + core]
            out_ref[at, 2 * VECS :] = column


def tiles_kernel(first, *refs):
    if first:
        idx_ref, x_ref, w_ref, own_ref, e_ref, out_ref, *scratch = refs
    else:
        idx_ref, x_ref, w_ref, out_ref, own_ref, *scratch = refs
    field_row, field_col, acc_row, acc_col = scratch[:4]
    low_half = lane_index() < HALF
    zero = jnp.zeros((VECS, LANES), F32)
    half_mask = [low_half, jnp.logical_not(low_half)]
    half_one = [jnp.where(m, 1.0, 0.0).astype(BF16) for m in half_mask]
    own_piece = piece_at(lax.axis_index("x"), lax.axis_index("zh"), lax.axis_index("core"), 0)

    def part(g):
        return slice(g * VECS, (g + 1) * VECS)

    def place(piece, slot):
        if slot < 2:
            return field_row, acc_row, (piece * 2 + slot) * 2
        return field_col, acc_col, piece * 2

    def duplicate(x, carry):
        for zh, core, j in INNER:
            for slot in range(3):
                chunk, rows = locate(first, x, zh, core, j, slot)
                value = x_ref[chunk, rows].astype(F32)
                turned = pltpu.roll(value, HALF, 1)
                field, acc, at = place(piece_at(x, zh, core, j), slot)
                field[at] = jnp.where(low_half, value, turned).astype(BF16)
                field[at + 1] = jnp.where(low_half, turned, value).astype(BF16)
                acc[at] = zero
                acc[at + 1] = zero
        return carry

    lax.fori_loop(0, 4, duplicate, 0)
    for field, acc, dead in ((field_row, acc_row, ROW_DEAD), (field_col, acc_col, COL_DEAD)):
        field[dead] = zero.astype(BF16)
        acc[dead] = zero

    def block(b, carry):
        work = []
        for u in range(UNROLL):
            q = b * UNROLL + u
            rows = [idx_ref[0, q * 4 + k] for k in range(4)]
            cols = [idx_ref[1, q * 4 + k] for k in range(4)]
            w = w_ref[pl.ds(2 * q, 2)].reshape(2 * HALF, LANES)
            left_f = jnp.concatenate([field_col[cols[k]] * half_one[k % 2] for k in range(4)], axis=0)
            left_b = jnp.concatenate([field_row[rows[k]] * half_one[k // 2] for k in range(4)], axis=0)
            forward = lax.dot_general(left_f, w, NT_DIMS, preferred_element_type=F32)
            backward = jnp.dot(left_b, w, preferred_element_type=F32)
            work.append((rows, cols, forward, backward))
        for rows, cols, forward, backward in work:
            for k in range(4):
                acc_row[rows[k]] += jnp.where(half_mask[k // 2], forward[part(k)], 0.0)
                acc_col[cols[k]] += jnp.where(half_mask[k % 2], backward[part(k)], 0.0)
        return carry

    lax.fori_loop(0, SLOTS // 4 // UNROLL, block, 0)

    def add_energies(j):
        value = own_ref[j].astype(F32) * (0.5 * e_ref[j : j + 1, :])
        at = (own_piece + j) * 2
        for h in range(2):
            acc_col[at + h] += jnp.where(half_mask[h], value, 0.0)

    def folded(piece, slot):
        _, acc, at = place(piece, slot)
        one, two = acc[at], acc[at + 1]
        return jnp.where(low_half, one, two) + pltpu.roll(jnp.where(low_half, two, one), HALF, 1)

    def pack(x, carry):
        for zh, core, j in INNER:
            piece = piece_at(x, zh, core, j)
            for slot in range(3):
                total = folded(piece, slot)
                chunk, rows = locate(not first, x, zh, core, j, slot)
                out_ref[chunk, rows] = total.astype(BF16)
                if first and slot == 2:
                    for n, term in enumerate(split3(total)):
                        scratch[4][n, piece] = term
        return carry

    if not first:
        lax.fori_loop(0, 4, pack, 0)
        for j in range(2):
            own_ref[j] = x_ref[own_piece + j, part(2)]
        return

    for j in range(2):
        add_energies(j)
    lax.fori_loop(0, 4, pack, 0)
    terms = scratch[4]
    left = jnp.concatenate(
        [jnp.concatenate([terms[n, p] for p in range(PIECES)], axis=1) for n in range(3)], axis=0
    )
    pieces = []
    for x in range(4):
        for zh, core, j in INNER:
            chunk, rows = locate(True, x, zh, core, j, 2)
            pieces.append(x_ref[chunk, rows])
    crosses = lax.dot_general(
        left, jnp.concatenate(pieces, axis=1), NT_DIMS, preferred_element_type=F32
    )
    cross = crosses[:VECS] + crosses[VECS : 2 * VECS] + crosses[2 * VECS :]
    gram = jnp.zeros((VECS, VECS), F32)
    for j in range(2):
        own = own_ref[j]
        gram = gram + lax.dot_general(own, own, NT_DIMS, preferred_element_type=F32)
        add_energies(j)
        out_ref[own_piece + j, part(2)] = folded(own_piece + j, 2).astype(BF16)
    message = message_of(widen(gram), widen(cross))
    for p in range(PIECES):
        out_ref[p, 3 * VECS :] = message


def widen(value):
    return jnp.concatenate([value, jnp.zeros((VECS, LANES - VECS), F32)], axis=1)


def message_of(gram, cross):
    total = jnp.zeros((VECS, LANES), F32)
    for n, part in enumerate(split2(gram) + split2(cross)):
        part = part.astype(F32)
        total = total + (pltpu.roll(part, n * VECS, 1) if n else part)
    return (total[:MESSAGE] + pltpu.roll(total[MESSAGE:], HALF, 1)).astype(BF16)


def read_message(total):
    total = jnp.concatenate([total, pltpu.roll(total, HALF, 1)], axis=0)
    keep = lane_index() < VECS
    found = []
    for n in (0, 2):
        high = pltpu.roll(total, LANES - n * VECS, 1) if n else total
        low = pltpu.roll(total, LANES - (n + 1) * VECS, 1)
        found.append(jnp.where(keep, high + low, 0.0))
    return found


def sum_over(in_ref, start, rows, chunks=None):
    total = None
    for n in range(in_ref.shape[0]) if chunks is None else chunks:
        value = in_ref[n, start : start + rows].astype(F32)
        total = value if total is None else total + value
    return total


def collect_owner_kernel(in_ref, out_ref, back_ref):
    wide = 2 * VECS
    y, core = lax.axis_index("y"), lax.axis_index("core")
    nothing = jnp.zeros((wide, LANES), BF16)
    for block in range(8):
        zh, x = block // 4, block % 4
        chunks = [(x * 2 + zh) * 4 + zl for zl in range(4)]
        out_ref[block * 2 + core, :wide] = sum_over(in_ref, 0, wide, chunks).astype(BF16)
        out_ref[block * 2 + 1 - core, :wide] = nothing
    sums = []
    for zl in range(4):
        sums.append(sum_over(in_ref, wide, VECS, [n * 4 + zl for n in range(8)]))
    for s in range(2):
        same = core == 0
        back_ref[s] = jnp.where(same, sums[s], sums[2 + s])
        other = jnp.where(same, sums[2 + s], sums[s])
        out_ref[y * 2 + 1 - core, s * VECS : (s + 1) * VECS] = other.astype(BF16)
    message = message_of(*read_message(sum_over(in_ref, 3 * VECS, MESSAGE)))
    for n in range(2 * 8):
        out_ref[n, wide:] = message


def solve_kernel(in_ref, back_ref, kept_ref, received_ref, out_ref):
    gram, cross = read_message(sum_over(in_ref, 2 * VECS, MESSAGE))
    wide = jnp.concatenate([cross, jnp.zeros((LANES - VECS, LANES), F32)], axis=0)
    cross = cross + jnp.transpose(wide)[:VECS]
    state = jnp.concatenate([gram, cross], axis=0)
    lane = lax.broadcasted_iota(jnp.int32, (2 * VECS, LANES), 1)
    for p in range(VECS):
        column = state[:, p : p + 1] * (1.0 / state[p : p + 1, p : p + 1])
        state = jnp.where(lane == p, column, state - column * state[p : p + 1])
    mix = state[VECS:]
    mine = lax.div(lax.axis_index("zl"), 2) == lax.axis_index("core")
    for s in range(2):
        v = jnp.where(mine, kept_ref[s].astype(F32), received_ref[s].astype(F32))
        product = sum_over(in_ref, s * VECS, VECS) + back_ref[s]
        shifted = jnp.zeros((VECS, LANES), F32)
        for k in range(VECS):
            shifted = shifted + mix[:, k : k + 1] * v[k : k + 1, :]
        value = (product - shifted).astype(BF16)
        for n in range(2 * 8):
            out_ref[n, s * VECS : (s + 1) * VECS] = value


def collect_kernel(in_ref, out_ref, back_ref):
    wide = 2 * VECS
    for r in range(NR):
        for s in range(2):
            out_ref[col_at(2 * r + s)] = in_ref[row_at(r), s * wide : (s + 1) * wide]
    for j in range(2):
        back_ref[j] = sum_over(in_ref, (4 + j) * VECS, VECS)


def finish_kernel(in_ref, back_ref, own_ref, e_ref, residual_ref, out_ref):
    for j in range(2):
        own = own_ref[j]
        total = sum_over(in_ref, j * VECS, VECS) + back_ref[j]
        residual_ref[:, j, :] = own
        out_ref[:, j, :] = total + e_ref[j : j + 1, :] * own.astype(F32)


def exchange(value, axis):
    return lax.all_to_all(value, axis, split_axis=0, concat_axis=0, tiled=True)


def shards(vectors, tile_values, tile_coords, tile_counts, energies):
    tiles = tile_values[0]
    piece = shape(2, VECS, LANES)
    scratch = [
        pltpu.VMEM((ROW_DEAD + 1, VECS, LANES), BF16),
        pltpu.VMEM((COL_DEAD + 1, VECS, LANES), BF16),
        pltpu.VMEM((ROW_DEAD + 1, VECS, LANES), F32),
        pltpu.VMEM((COL_DEAD + 1, VECS, LANES), F32),
    ]
    spread, index, energies = call(
        spread_kernel,
        (
            shape(NC, 2 * VECS, LANES),
            shape(2, SLOTS, dtype=jnp.int32),
            shape(2, LANES, dtype=F32),
        ),
        4,
        [
            pltpu.VMEM((VECS, 2, LANES), BF16),
            pltpu.VMEM((2, 1, SLOTS), jnp.int32),
            pltpu.SMEM((1, 1), jnp.int32),
            pltpu.SemaphoreType.DMA((4,)),
        ],
        first=pl.BlockSpec(memory_space=pl.ANY),
        limit=60,
    )(vectors, tile_coords, tile_counts, energies)

    slab = exchange(spread, COL)
    grouped, own, kept, sent = call(
        regroup_kernel, (shape(NR, GROUP * VECS, LANES), piece, piece, piece), 1
    )(slab)
    received = lax.ppermute(sent, "core", [(0, 1), (1, 0)])
    fields = exchange(grouped, ROW)
    partial = call(
        functools.partial(tiles_kernel, True),
        shape(PIECES, 3 * VECS + MESSAGE, LANES),
        5,
        scratch + [pltpu.VMEM((3, PIECES, VECS, LANES), BF16)],
        scalars=(0,),
    )(index, fields, tiles, own, energies)
    by_owner, back = call(
        collect_owner_kernel,
        (shape(NR, 2 * VECS + MESSAGE, LANES), shape(2, VECS, LANES, dtype=F32)),
        1,
    )(exchange(partial, PIECE))
    residual = call(solve_kernel, shape(NR, 2 * VECS, LANES), 4)(
        exchange(by_owner, OWNER), back, kept, received
    )

    grouped = call(regroup_back_kernel, shape(PIECES, 3 * VECS, LANES), 1)(exchange(residual, OWNER))
    partial, own = call(
        functools.partial(tiles_kernel, False),
        (shape(NR, GROUP * VECS, LANES), piece),
        3,
        scratch,
        scalars=(0,),
    )(index, exchange(grouped, PIECE), tiles)
    by_block, back = call(
        collect_kernel, (shape(NC, 2 * VECS, LANES), shape(2, VECS, LANES, dtype=F32)), 1
    )(exchange(partial, ROW))
    return call(
        finish_kernel, (shape(VECS, 2, LANES), shape(VECS, 2, LANES, dtype=F32)), 4
    )(exchange(by_block, COL), back, own, energies)


def solution(mesh):
    devices = np.asarray(mesh.devices).reshape(2, 4, 2, 8, 4)
    fine = jax.sharding.Mesh(devices, ("zh", "x", "core", "y", "zl"))
    row, col = ("zh", "x", "core"), ("y", "zl")
    in_specs = (
        P(None, row, col),
        P(row, col, None, None),
        P(None, row, col),
        P(row, col),
        P(row, col),
    )
    out_specs = (P(None, row, col), P(None, row, col))
    return jax.shard_map(shards, mesh=fine, in_specs=in_specs, out_specs=out_specs, check_vma=False)
```

```python
import functools

import jax
import jax.numpy as jnp
import numpy as np
from jax import lax
from jax.experimental import pallas as pl
from jax.experimental.pallas import tpu as pltpu
from jax.sharding import PartitionSpec as P

F32 = jnp.float32
BF16 = jnp.bfloat16
VECS = 16
LANES = 128
HALF = 64
MESSAGE = 8
NR = 16
NC = 32
GROUP = 6
PIECES = 32
SLOTS = 128
UNROLL = 16
ROW_DEAD = NR * 8
COL_DEAD = NR * 4
ROW = ("x", "core", "zh")
COL = ("zl", "y")
PIECE = ("x", "zh", "zl")
OWNER = ("y", "core")
VMEM = pl.BlockSpec(memory_space=pltpu.VMEM)
SMEM = pl.BlockSpec(memory_space=pltpu.SMEM)
NT_DIMS = (((1,), (1,)), ((), ()))


def row_at(r):
    return (r % 8) * 2 + r // 8


def col_at(c):
    return (c % 4) * 8 + c // 4


def shape(*dims, dtype=BF16):
    return jax.ShapeDtypeStruct(dims, dtype)


def call(kernel, outs, n_in, scratch=(), scalars=(), first=VMEM, limit=32):
    specs = [SMEM if n in scalars else first for n in range(n_in)]
    return pl.pallas_call(
        kernel,
        out_shape=outs,
        in_specs=specs,
        out_specs=jax.tree.map(lambda _: VMEM, outs),
        scratch_shapes=list(scratch),
        compiler_params=pltpu.CompilerParams(vmem_limit_bytes=limit * 1024 * 1024),
    )


def lane_index():
    return lax.broadcasted_iota(jnp.int32, (VECS, LANES), 1)


def split2(value):
    high = value.astype(BF16)
    return high, (value - high.astype(F32)).astype(BF16)


def split3(value):
    high = value.astype(BF16)
    rest = value - high.astype(F32)
    middle = rest.astype(BF16)
    low = (rest - middle.astype(F32)).astype(BF16)
    return high, middle, low


def piece_at(x, zh, core, j):
    return x * 8 + zh * 4 + core * 2 + j


def locate(by_row, x, zh, core, j, slot):
    if by_row:
        place = slot * 2 + j if slot < 2 else 4 + j
        return x * 4 + core * 2 + zh, slice(place * VECS, (place + 1) * VECS)
    return piece_at(x, zh, core, j), slice(slot * VECS, (slot + 1) * VECS)


INNER = [(zh, core, j) for zh in range(2) for core in range(2) for j in range(2)]


def spread_kernel(
    x_hbm, coords_hbm, counts_hbm, e_hbm, out_ref, index_ref, energy_ref, *refs
):
    messages, (x_ref, coords_ref, counts_ref, sems) = refs[:2], refs[2:]
    pairs = ((x_hbm, x_ref), (coords_hbm, coords_ref), (counts_hbm, counts_ref), (e_hbm, energy_ref))
    copies = [pltpu.make_async_copy(a, b, sems.at[n]) for n, (a, b) in enumerate(pairs)]
    for copy in copies:
        copy.start()
    for copy in copies:
        copy.wait()
    for j in range(2):
        value = x_ref[:, j, :]
        for c in range(NC):
            out_ref[c, j * VECS : (j + 1) * VECS] = value
    odd = lax.rem(lax.axis_index("zl"), 2)
    row = lax.broadcasted_iota(jnp.int32, (VECS, LANES), 0)
    for k, message in enumerate(messages):
        message[:VECS] = jnp.where(odd == k, x_ref[:, 0, :], x_ref[:, 1, :])
        terms = jnp.zeros((VECS, LANES), F32)
        for n, term in enumerate(split3(jnp.where(odd == k, energy_ref[0:1], energy_ref[1:2]))):
            terms = jnp.where(row == n, term.astype(F32), terms)
        message[VECS:] = terms.astype(BF16)
    live = lax.broadcasted_iota(jnp.int32, (1, SLOTS), 1) < counts_ref[0, 0]
    for n, dead in ((0, ROW_DEAD), (1, COL_DEAD)):
        coords = coords_ref[n]
        major = coords >> 6
        piece = ((major >> 2) & 3) * 8 + (major >> 4) * 4 + (major & 3)
        if n == 0:
            piece = piece * 2 + ((coords >> 1) & 1)
        index_ref[n : n + 1] = jnp.where(live, piece * 2 + (coords & 1), dead)


def regroup_kernel(in_ref, even_ref, odd_ref, out_ref, own_ref, owned_ref, energy_ref):
    wide = 2 * VECS
    y, zl = lax.axis_index("y"), lax.axis_index("zl")
    own = in_ref[zl * 8 + y]
    odd = lax.rem(zl, 2)
    for j in range(2):
        own_ref[j] = own[j * VECS : (j + 1) * VECS]
        message = jnp.where(odd == j, even_ref[...], odd_ref[...])
        owned_ref[j] = message[:VECS]
        terms = message[VECS:].astype(F32)
        energy_ref[j : j + 1] = terms[0:1] + terms[1:2] + terms[2:3]
    for r in range(NR):
        at = row_at(r)
        for s in range(2):
            out_ref[at, s * wide : (s + 1) * wide] = in_ref[col_at(2 * r + s)]
        out_ref[at, 2 * wide :] = own


def regroup_back_kernel(in_ref, out_ref):
    y, core = lax.axis_index("y"), lax.axis_index("core")
    for zl in range(4):
        column = in_ref[y * 2 + zl // 2, (zl % 2) * VECS : (zl % 2 + 1) * VECS]
        for block in range(8):
            zh, x = block // 4, block % 4
            at = (x * 2 + zh) * 4 + zl
            out_ref[at, : 2 * VECS] = in_ref[block * 2 + core]
            out_ref[at, 2 * VECS :] = column


def tiles_kernel(first, *refs):
    if first:
        idx_ref, x_ref, w_ref, own_ref, e_ref, out_ref, *scratch = refs
    else:
        idx_ref, x_ref, w_ref, out_ref, own_ref, *scratch = refs
    field_row, field_col, acc_row, acc_col = scratch[:4]
    low_half = lane_index() < HALF
    zero = jnp.zeros((VECS, LANES), F32)
    half_mask = [low_half, jnp.logical_not(low_half)]
    half_one = [jnp.where(m, 1.0, 0.0).astype(BF16) for m in half_mask]
    own_piece = piece_at(lax.axis_index("x"), lax.axis_index("zh"), lax.axis_index("core"), 0)

    def part(g):
        return slice(g * VECS, (g + 1) * VECS)

    def place(piece, slot):
        if slot < 2:
            return field_row, acc_row, (piece * 2 + slot) * 2
        return field_col, acc_col, piece * 2

    def duplicate(x, carry):
        for zh, core, j in INNER:
            for slot in range(3):
                chunk, rows = locate(first, x, zh, core, j, slot)
                value = x_ref[chunk, rows].astype(F32)
                turned = pltpu.roll(value, HALF, 1)
                field, acc, at = place(piece_at(x, zh, core, j), slot)
                field[at] = jnp.where(low_half, value, turned).astype(BF16)
                field[at + 1] = jnp.where(low_half, turned, value).astype(BF16)
                acc[at] = zero
                acc[at + 1] = zero
        return carry

    lax.fori_loop(0, 4, duplicate, 0)
    for field, acc, dead in ((field_row, acc_row, ROW_DEAD), (field_col, acc_col, COL_DEAD)):
        field[dead] = zero.astype(BF16)
        acc[dead] = zero

    def block(b, carry):
        work = []
        for u in range(UNROLL):
            q = b * UNROLL + u
            rows = [idx_ref[0, q * 4 + k] for k in range(4)]
            cols = [idx_ref[1, q * 4 + k] for k in range(4)]
            w = w_ref[pl.ds(2 * q, 2)].reshape(2 * HALF, LANES)
            left_f = jnp.concatenate([field_col[cols[k]] * half_one[k % 2] for k in range(4)], axis=0)
            left_b = jnp.concatenate([field_row[rows[k]] * half_one[k // 2] for k in range(4)], axis=0)
            forward = lax.dot_general(left_f, w, NT_DIMS, preferred_element_type=F32)
            backward = jnp.dot(left_b, w, preferred_element_type=F32)
            work.append((rows, cols, forward, backward))
        for rows, cols, forward, backward in work:
            for k in range(4):
                acc_row[rows[k]] += jnp.where(half_mask[k // 2], forward[part(k)], 0.0)
                acc_col[cols[k]] += jnp.where(half_mask[k % 2], backward[part(k)], 0.0)
        return carry

    lax.fori_loop(0, SLOTS // 4 // UNROLL, block, 0)

    def folded(piece, slot):
        _, acc, at = place(piece, slot)
        one, two = acc[at], acc[at + 1]
        return jnp.where(low_half, one, two) + pltpu.roll(jnp.where(low_half, two, one), HALF, 1)

    def pack(x, carry):
        for zh, core, j in INNER:
            piece = piece_at(x, zh, core, j)
            for slot in range(3):
                total = folded(piece, slot)
                chunk, rows = locate(not first, x, zh, core, j, slot)
                out_ref[chunk, rows] = total.astype(BF16)
                if first and slot == 2:
                    for n, term in enumerate(split3(total)):
                        scratch[4][n, piece] = term
        return carry

    if not first:
        lax.fori_loop(0, 4, pack, 0)
        for j in range(2):
            own_ref[j] = x_ref[own_piece + j, part(2)]
        return

    lax.fori_loop(0, 4, pack, 0)
    terms = scratch[4]
    left = jnp.concatenate(
        [jnp.concatenate([terms[n, p] for p in range(PIECES)], axis=1) for n in range(3)], axis=0
    )
    pieces = []
    for x in range(4):
        for zh, core, j in INNER:
            chunk, rows = locate(True, x, zh, core, j, 2)
            pieces.append(x_ref[chunk, rows])
    crosses = lax.dot_general(
        left, jnp.concatenate(pieces, axis=1), NT_DIMS, preferred_element_type=F32
    )
    cross = crosses[:VECS] + crosses[VECS : 2 * VECS] + crosses[2 * VECS :]
    gram = jnp.zeros((VECS, VECS), F32)
    for j in range(2):
        own = own_ref[j]
        gram = gram + lax.dot_general(own, own, NT_DIMS, preferred_element_type=F32)
        for term in split3(own.astype(F32) * (0.5 * e_ref[j : j + 1, :])):
            cross = cross + lax.dot_general(term, own, NT_DIMS, preferred_element_type=F32)
    message = message_of(widen(gram), widen(cross))
    for p in range(PIECES):
        out_ref[p, 3 * VECS :] = message


def widen(value):
    return jnp.concatenate([value, jnp.zeros((VECS, LANES - VECS), F32)], axis=1)


def message_of(gram, cross):
    total = jnp.zeros((VECS, LANES), F32)
    for n, part in enumerate(split2(gram) + split2(cross)):
        part = part.astype(F32)
        total = total + (pltpu.roll(part, n * VECS, 1) if n else part)
    return (total[:MESSAGE] + pltpu.roll(total[MESSAGE:], HALF, 1)).astype(BF16)


def read_message(total):
    total = jnp.concatenate([total, pltpu.roll(total, HALF, 1)], axis=0)
    keep = lane_index() < VECS
    found = []
    for n in (0, 2):
        high = pltpu.roll(total, LANES - n * VECS, 1) if n else total
        low = pltpu.roll(total, LANES - (n + 1) * VECS, 1)
        found.append(jnp.where(keep, high + low, 0.0))
    return found


def sum_over(in_ref, start, rows, chunks=None):
    total = None
    for n in range(in_ref.shape[0]) if chunks is None else chunks:
        value = in_ref[n, start : start + rows].astype(F32)
        total = value if total is None else total + value
    return total


def collect_owner_kernel(in_ref, out_ref, back_ref):
    wide = 2 * VECS
    y, core = lax.axis_index("y"), lax.axis_index("core")
    nothing = jnp.zeros((wide, LANES), BF16)
    for block in range(8):
        zh, x = block // 4, block % 4
        chunks = [(x * 2 + zh) * 4 + zl for zl in range(4)]
        out_ref[block * 2 + core, :wide] = sum_over(in_ref, 0, wide, chunks).astype(BF16)
        out_ref[block * 2 + 1 - core, :wide] = nothing
    sums = []
    for zl in range(4):
        sums.append(sum_over(in_ref, wide, VECS, [n * 4 + zl for n in range(8)]))
    for s in range(2):
        same = core == 0
        back_ref[s] = jnp.where(same, sums[s], sums[2 + s])
        other = jnp.where(same, sums[2 + s], sums[s])
        out_ref[y * 2 + 1 - core, s * VECS : (s + 1) * VECS] = other.astype(BF16)
    message = message_of(*read_message(sum_over(in_ref, 3 * VECS, MESSAGE)))
    for n in range(2 * 8):
        out_ref[n, wide:] = message


def solve_kernel(in_ref, back_ref, owned_ref, e_ref, out_ref):
    gram, cross = read_message(sum_over(in_ref, 2 * VECS, MESSAGE))
    wide = jnp.concatenate([cross, jnp.zeros((LANES - VECS, LANES), F32)], axis=0)
    cross = cross + jnp.transpose(wide)[:VECS]
    state = jnp.concatenate([gram, cross], axis=0)
    lane = lax.broadcasted_iota(jnp.int32, (2 * VECS, LANES), 1)
    for p in range(VECS):
        column = state[:, p : p + 1] * (1.0 / state[p : p + 1, p : p + 1])
        state = jnp.where(lane == p, column, state - column * state[p : p + 1])
    mix = state[VECS:]
    for s in range(2):
        v = owned_ref[s].astype(F32)
        product = sum_over(in_ref, s * VECS, VECS) + back_ref[s] + e_ref[s : s + 1, :] * v
        shifted = jnp.zeros((VECS, LANES), F32)
        for k in range(VECS):
            shifted = shifted + mix[:, k : k + 1] * v[k : k + 1, :]
        value = (product - shifted).astype(BF16)
        for n in range(2 * 8):
            out_ref[n, s * VECS : (s + 1) * VECS] = value


def collect_kernel(in_ref, out_ref, back_ref):
    wide = 2 * VECS
    for r in range(NR):
        for s in range(2):
            out_ref[col_at(2 * r + s)] = in_ref[row_at(r), s * wide : (s + 1) * wide]
    for j in range(2):
        back_ref[j] = sum_over(in_ref, (4 + j) * VECS, VECS)


def finish_kernel(in_ref, back_ref, own_ref, e_ref, residual_ref, out_ref):
    for j in range(2):
        own = own_ref[j]
        total = sum_over(in_ref, j * VECS, VECS) + back_ref[j]
        residual_ref[:, j, :] = own
        out_ref[:, j, :] = total + e_ref[j : j + 1, :] * own.astype(F32)


def owner_of(n, k):
    core, zl = n // 4, n % 4
    return n, zl // 2 * 4 + core * 2 + (zl % 2 ^ k)


def exchange(value, axis):
    return lax.all_to_all(value, axis, split_axis=0, concat_axis=0, tiled=True)


def shards(vectors, tile_values, tile_coords, tile_counts, energies):
    tiles = tile_values[0]
    piece = shape(2, VECS, LANES)
    scratch = [
        pltpu.VMEM((ROW_DEAD + 1, VECS, LANES), BF16),
        pltpu.VMEM((COL_DEAD + 1, VECS, LANES), BF16),
        pltpu.VMEM((ROW_DEAD + 1, VECS, LANES), F32),
        pltpu.VMEM((COL_DEAD + 1, VECS, LANES), F32),
    ]
    spread, index, energies, *messages = call(
        spread_kernel,
        (
            shape(NC, 2 * VECS, LANES),
            shape(2, SLOTS, dtype=jnp.int32),
            shape(2, LANES, dtype=F32),
            shape(2 * VECS, LANES),
            shape(2 * VECS, LANES),
        ),
        4,
        [
            pltpu.VMEM((VECS, 2, LANES), BF16),
            pltpu.VMEM((2, 1, SLOTS), jnp.int32),
            pltpu.SMEM((1, 1), jnp.int32),
            pltpu.SemaphoreType.DMA((4,)),
        ],
        first=pl.BlockSpec(memory_space=pl.ANY),
        limit=60,
    )(vectors, tile_coords, tile_counts, energies)

    received = [
        lax.ppermute(message, ("core", "zl"), [owner_of(n, k) for n in range(8)])
        for k, message in enumerate(messages)
    ]
    slab = exchange(spread, COL)
    grouped, own, owned, owned_energies = call(
        regroup_kernel,
        (shape(NR, GROUP * VECS, LANES), piece, piece, shape(2, LANES, dtype=F32)),
        3,
    )(slab, *received)
    fields = exchange(grouped, ROW)
    partial = call(
        functools.partial(tiles_kernel, True),
        shape(PIECES, 3 * VECS + MESSAGE, LANES),
        5,
        scratch + [pltpu.VMEM((3, PIECES, VECS, LANES), BF16)],
        scalars=(0,),
    )(index, fields, tiles, own, energies)
    by_owner, back = call(
        collect_owner_kernel,
        (shape(NR, 2 * VECS + MESSAGE, LANES), shape(2, VECS, LANES, dtype=F32)),
        1,
    )(exchange(partial, PIECE))
    residual = call(solve_kernel, shape(NR, 2 * VECS, LANES), 4)(
        exchange(by_owner, OWNER), back, owned, owned_energies
    )

    grouped = call(regroup_back_kernel, shape(PIECES, 3 * VECS, LANES), 1)(exchange(residual, OWNER))
    partial, own = call(
        functools.partial(tiles_kernel, False),
        (shape(NR, GROUP * VECS, LANES), piece),
        3,
        scratch,
        scalars=(0,),
    )(index, exchange(grouped, PIECE), tiles)
    by_block, back = call(
        collect_kernel, (shape(NC, 2 * VECS, LANES), shape(2, VECS, LANES, dtype=F32)), 1
    )(exchange(partial, ROW))
    return call(
        finish_kernel, (shape(VECS, 2, LANES), shape(VECS, 2, LANES, dtype=F32)), 4
    )(exchange(by_block, COL), back, own, energies)


def solution(mesh):
    devices = np.asarray(mesh.devices).reshape(2, 4, 2, 8, 4)
    fine = jax.sharding.Mesh(devices, ("zh", "x", "core", "y", "zl"))
    row, col = ("zh", "x", "core"), ("y", "zl")
    in_specs = (
        P(None, row, col),
        P(row, col, None, None),
        P(None, row, col),
        P(row, col),
        P(row, col),
    )
    out_specs = (P(None, row, col), P(None, row, col))
    return jax.shard_map(shards, mesh=fine, in_specs=in_specs, out_specs=out_specs, check_vma=False)
```

```python
import functools

import jax
import jax.numpy as jnp
import numpy as np
from jax import lax
from jax.experimental import pallas as pl
from jax.experimental.pallas import tpu as pltpu
from jax.sharding import PartitionSpec as P

F32 = jnp.float32
BF16 = jnp.bfloat16
VECS = 16
LANES = 128
HALF = 64
MESSAGE = 8
NR = 16
NC = 32
GROUP = 6
PIECES = 32
SLOTS = 128
UNROLL = 16
ROW_DEAD = NR * 8
COL_DEAD = NR * 4
ROW = ("x", "core", "zh")
COL = ("zl", "y")
PIECE = ("x", "zh", "zl")
OWNER = ("y", "core")
VMEM = pl.BlockSpec(memory_space=pltpu.VMEM)
SMEM = pl.BlockSpec(memory_space=pltpu.SMEM)
NT_DIMS = (((1,), (1,)), ((), ()))


def row_at(r):
    return (r % 8) * 2 + r // 8


def col_at(c):
    return (c % 4) * 8 + c // 4


def shape(*dims, dtype=BF16):
    return jax.ShapeDtypeStruct(dims, dtype)


def call(kernel, outs, n_in, scratch=(), scalars=(), first=VMEM, limit=32):
    specs = [SMEM if n in scalars else first for n in range(n_in)]
    return pl.pallas_call(
        kernel,
        out_shape=outs,
        in_specs=specs,
        out_specs=jax.tree.map(lambda _: VMEM, outs),
        scratch_shapes=list(scratch),
        compiler_params=pltpu.CompilerParams(vmem_limit_bytes=limit * 1024 * 1024),
    )


def lane_index():
    return lax.broadcasted_iota(jnp.int32, (VECS, LANES), 1)


def split2(value):
    high = value.astype(BF16)
    return high, (value - high.astype(F32)).astype(BF16)


def split3(value):
    high = value.astype(BF16)
    rest = value - high.astype(F32)
    middle = rest.astype(BF16)
    low = (rest - middle.astype(F32)).astype(BF16)
    return high, middle, low


def piece_at(x, zh, core, j):
    return x * 8 + zh * 4 + core * 2 + j


def locate(by_row, x, zh, core, j, slot):
    if by_row:
        place = slot * 2 + j if slot < 2 else 4 + j
        return x * 4 + core * 2 + zh, slice(place * VECS, (place + 1) * VECS)
    return piece_at(x, zh, core, j), slice(slot * VECS, (slot + 1) * VECS)


INNER = [(zh, core, j) for zh in range(2) for core in range(2) for j in range(2)]


def spread_kernel(x_hbm, e_hbm, out_ref, even_ref, odd_ref, x_ref, e_ref, sems):
    pairs = ((x_hbm, x_ref), (e_hbm, e_ref))
    copies = [pltpu.make_async_copy(a, b, sems.at[n]) for n, (a, b) in enumerate(pairs)]
    for copy in copies:
        copy.start()
    for copy in copies:
        copy.wait()
    for j in range(2):
        value = x_ref[:, j, :]
        for c in range(NC):
            out_ref[c, j * VECS : (j + 1) * VECS] = value
    odd = lax.rem(lax.axis_index("zl"), 2)
    row = lax.broadcasted_iota(jnp.int32, (VECS, LANES), 0)
    for k, message in enumerate((even_ref, odd_ref)):
        message[:VECS] = jnp.where(odd == k, x_ref[:, 0, :], x_ref[:, 1, :])
        terms = jnp.zeros((VECS, LANES), F32)
        for n, term in enumerate(split3(jnp.where(odd == k, e_ref[0:1], e_ref[1:2]))):
            terms = jnp.where(row == n, term.astype(F32), terms)
        message[VECS:] = terms.astype(BF16)


def index_kernel(coords_ref, counts_ref, e_ref, index_ref, energy_ref):
    live = lax.broadcasted_iota(jnp.int32, (1, SLOTS), 1) < counts_ref[0, 0]
    for n, dead in ((0, ROW_DEAD), (1, COL_DEAD)):
        coords = coords_ref[n]
        major = coords >> 6
        piece = ((major >> 2) & 3) * 8 + (major >> 4) * 4 + (major & 3)
        if n == 0:
            piece = piece * 2 + ((coords >> 1) & 1)
        index_ref[n : n + 1] = jnp.where(live, piece * 2 + (coords & 1), dead)
    energy_ref[...] = e_ref[...]


def regroup_kernel(
    in_ref, even_ref, odd_ref, index_in, e_in, out_ref, own_ref, owned_ref, energy_ref, index_out, e_out
):
    index_out[...] = index_in[...]
    e_out[...] = e_in[...]
    wide = 2 * VECS
    y, zl = lax.axis_index("y"), lax.axis_index("zl")
    own = in_ref[zl * 8 + y]
    odd = lax.rem(zl, 2)
    for j in range(2):
        own_ref[j] = own[j * VECS : (j + 1) * VECS]
        message = jnp.where(odd == j, even_ref[...], odd_ref[...])
        owned_ref[j] = message[:VECS]
        terms = message[VECS:].astype(F32)
        energy_ref[j : j + 1] = terms[0:1] + terms[1:2] + terms[2:3]
    for r in range(NR):
        at = row_at(r)
        for s in range(2):
            out_ref[at, s * wide : (s + 1) * wide] = in_ref[col_at(2 * r + s)]
        out_ref[at, 2 * wide :] = own


def regroup_back_kernel(in_ref, out_ref):
    y, core = lax.axis_index("y"), lax.axis_index("core")
    for zl in range(4):
        column = in_ref[y * 2 + zl // 2, (zl % 2) * VECS : (zl % 2 + 1) * VECS]
        for block in range(8):
            zh, x = block // 4, block % 4
            at = (x * 2 + zh) * 4 + zl
            out_ref[at, : 2 * VECS] = in_ref[block * 2 + core]
            out_ref[at, 2 * VECS :] = column


def tiles_kernel(first, *refs):
    if first:
        idx_ref, x_ref, w_ref, own_ref, e_ref, out_ref, *scratch = refs
    else:
        idx_ref, x_ref, w_ref, out_ref, own_ref, *scratch = refs
    field_row, field_col, acc_row, acc_col = scratch[:4]
    low_half = lane_index() < HALF
    zero = jnp.zeros((VECS, LANES), F32)
    half_mask = [low_half, jnp.logical_not(low_half)]
    half_one = [jnp.where(m, 1.0, 0.0).astype(BF16) for m in half_mask]
    own_piece = piece_at(lax.axis_index("x"), lax.axis_index("zh"), lax.axis_index("core"), 0)

    def part(g):
        return slice(g * VECS, (g + 1) * VECS)

    def place(piece, slot):
        if slot < 2:
            return field_row, acc_row, (piece * 2 + slot) * 2
        return field_col, acc_col, piece * 2

    def duplicate(x, carry):
        for zh, core, j in INNER:
            for slot in range(3):
                chunk, rows = locate(first, x, zh, core, j, slot)
                value = x_ref[chunk, rows].astype(F32)
                turned = pltpu.roll(value, HALF, 1)
                field, acc, at = place(piece_at(x, zh, core, j), slot)
                field[at] = jnp.where(low_half, value, turned).astype(BF16)
                field[at + 1] = jnp.where(low_half, turned, value).astype(BF16)
                acc[at] = zero
                acc[at + 1] = zero
        return carry

    lax.fori_loop(0, 4, duplicate, 0)
    for field, acc, dead in ((field_row, acc_row, ROW_DEAD), (field_col, acc_col, COL_DEAD)):
        field[dead] = zero.astype(BF16)
        acc[dead] = zero

    def block(b, carry):
        work = []
        for u in range(UNROLL):
            q = b * UNROLL + u
            rows = [idx_ref[0, q * 4 + k] for k in range(4)]
            cols = [idx_ref[1, q * 4 + k] for k in range(4)]
            w = w_ref[pl.ds(2 * q, 2)].reshape(2 * HALF, LANES)
            left_f = jnp.concatenate([field_col[cols[k]] * half_one[k % 2] for k in range(4)], axis=0)
            left_b = jnp.concatenate([field_row[rows[k]] * half_one[k // 2] for k in range(4)], axis=0)
            forward = lax.dot_general(left_f, w, NT_DIMS, preferred_element_type=F32)
            backward = jnp.dot(left_b, w, preferred_element_type=F32)
            work.append((rows, cols, forward, backward))
        for rows, cols, forward, backward in work:
            for k in range(4):
                acc_row[rows[k]] += jnp.where(half_mask[k // 2], forward[part(k)], 0.0)
                acc_col[cols[k]] += jnp.where(half_mask[k % 2], backward[part(k)], 0.0)
        return carry

    lax.fori_loop(0, SLOTS // 4 // UNROLL, block, 0)

    def folded(piece, slot):
        _, acc, at = place(piece, slot)
        one, two = acc[at], acc[at + 1]
        return jnp.where(low_half, one, two) + pltpu.roll(jnp.where(low_half, two, one), HALF, 1)

    def pack(x, carry):
        for zh, core, j in INNER:
            piece = piece_at(x, zh, core, j)
            for slot in range(3):
                total = folded(piece, slot)
                chunk, rows = locate(not first, x, zh, core, j, slot)
                out_ref[chunk, rows] = total.astype(BF16)
                if first and slot == 2:
                    for n, term in enumerate(split3(total)):
                        scratch[4][n, piece] = term
        return carry

    if not first:
        lax.fori_loop(0, 4, pack, 0)
        for j in range(2):
            own_ref[j] = x_ref[own_piece + j, part(2)]
        return

    lax.fori_loop(0, 4, pack, 0)
    terms = scratch[4]
    left = jnp.concatenate(
        [jnp.concatenate([terms[n, p] for p in range(PIECES)], axis=1) for n in range(3)], axis=0
    )
    pieces = []
    for x in range(4):
        for zh, core, j in INNER:
            chunk, rows = locate(True, x, zh, core, j, 2)
            pieces.append(x_ref[chunk, rows])
    crosses = lax.dot_general(
        left, jnp.concatenate(pieces, axis=1), NT_DIMS, preferred_element_type=F32
    )
    cross = crosses[:VECS] + crosses[VECS : 2 * VECS] + crosses[2 * VECS :]
    gram = jnp.zeros((VECS, VECS), F32)
    for j in range(2):
        own = own_ref[j]
        gram = gram + lax.dot_general(own, own, NT_DIMS, preferred_element_type=F32)
        for term in split3(own.astype(F32) * (0.5 * e_ref[j : j + 1, :])):
            cross = cross + lax.dot_general(term, own, NT_DIMS, preferred_element_type=F32)
    message = message_of(widen(gram), widen(cross))
    for p in range(PIECES):
        out_ref[p, 3 * VECS :] = message


def widen(value):
    return jnp.concatenate([value, jnp.zeros((VECS, LANES - VECS), F32)], axis=1)


def message_of(gram, cross):
    total = jnp.zeros((VECS, LANES), F32)
    for n, part in enumerate(split2(gram) + split2(cross)):
        part = part.astype(F32)
        total = total + (pltpu.roll(part, n * VECS, 1) if n else part)
    return (total[:MESSAGE] + pltpu.roll(total[MESSAGE:], HALF, 1)).astype(BF16)


def read_message(total):
    total = jnp.concatenate([total, pltpu.roll(total, HALF, 1)], axis=0)
    keep = lane_index() < VECS
    found = []
    for n in (0, 2):
        high = pltpu.roll(total, LANES - n * VECS, 1) if n else total
        low = pltpu.roll(total, LANES - (n + 1) * VECS, 1)
        found.append(jnp.where(keep, high + low, 0.0))
    return found


def sum_over(in_ref, start, rows, chunks=None):
    total = None
    for n in range(in_ref.shape[0]) if chunks is None else chunks:
        value = in_ref[n, start : start + rows].astype(F32)
        total = value if total is None else total + value
    return total


def collect_owner_kernel(in_ref, out_ref, back_ref):
    wide = 2 * VECS
    y, core = lax.axis_index("y"), lax.axis_index("core")
    nothing = jnp.zeros((wide, LANES), BF16)
    for block in range(8):
        zh, x = block // 4, block % 4
        chunks = [(x * 2 + zh) * 4 + zl for zl in range(4)]
        out_ref[block * 2 + core, :wide] = sum_over(in_ref, 0, wide, chunks).astype(BF16)
        out_ref[block * 2 + 1 - core, :wide] = nothing
    sums = []
    for zl in range(4):
        sums.append(sum_over(in_ref, wide, VECS, [n * 4 + zl for n in range(8)]))
    for s in range(2):
        same = core == 0
        back_ref[s] = jnp.where(same, sums[s], sums[2 + s])
        other = jnp.where(same, sums[2 + s], sums[s])
        out_ref[y * 2 + 1 - core, s * VECS : (s + 1) * VECS] = other.astype(BF16)
    message = message_of(*read_message(sum_over(in_ref, 3 * VECS, MESSAGE)))
    for n in range(2 * 8):
        out_ref[n, wide:] = message


def solve_kernel(in_ref, back_ref, owned_ref, e_ref, out_ref):
    gram, cross = read_message(sum_over(in_ref, 2 * VECS, MESSAGE))
    wide = jnp.concatenate([cross, jnp.zeros((LANES - VECS, LANES), F32)], axis=0)
    cross = cross + jnp.transpose(wide)[:VECS]
    state = jnp.concatenate([gram, cross], axis=0)
    lane = lax.broadcasted_iota(jnp.int32, (2 * VECS, LANES), 1)
    for p in range(VECS):
        column = state[:, p : p + 1] * (1.0 / state[p : p + 1, p : p + 1])
        state = jnp.where(lane == p, column, state - column * state[p : p + 1])
    mix = state[VECS:]
    for s in range(2):
        v = owned_ref[s].astype(F32)
        product = sum_over(in_ref, s * VECS, VECS) + back_ref[s] + e_ref[s : s + 1, :] * v
        shifted = jnp.zeros((VECS, LANES), F32)
        for k in range(VECS):
            shifted = shifted + mix[:, k : k + 1] * v[k : k + 1, :]
        value = (product - shifted).astype(BF16)
        for n in range(2 * 8):
            out_ref[n, s * VECS : (s + 1) * VECS] = value


def collect_kernel(in_ref, out_ref, back_ref):
    wide = 2 * VECS
    for r in range(NR):
        for s in range(2):
            out_ref[col_at(2 * r + s)] = in_ref[row_at(r), s * wide : (s + 1) * wide]
    for j in range(2):
        back_ref[j] = sum_over(in_ref, (4 + j) * VECS, VECS)


def finish_kernel(in_ref, back_ref, own_ref, e_ref, residual_ref, out_ref):
    for j in range(2):
        own = own_ref[j]
        total = sum_over(in_ref, j * VECS, VECS) + back_ref[j]
        residual_ref[:, j, :] = own
        out_ref[:, j, :] = total + e_ref[j : j + 1, :] * own.astype(F32)


def owner_of(n, k):
    core, zl = n // 4, n % 4
    return n, zl // 2 * 4 + core * 2 + (zl % 2 ^ k)


def exchange(value, axis):
    return lax.all_to_all(value, axis, split_axis=0, concat_axis=0, tiled=True)


def shards(vectors, tile_values, tile_coords, tile_counts, energies):
    tiles = tile_values[0]
    piece = shape(2, VECS, LANES)
    scratch = [
        pltpu.VMEM((ROW_DEAD + 1, VECS, LANES), BF16),
        pltpu.VMEM((COL_DEAD + 1, VECS, LANES), BF16),
        pltpu.VMEM((ROW_DEAD + 1, VECS, LANES), F32),
        pltpu.VMEM((COL_DEAD + 1, VECS, LANES), F32),
    ]
    index_shape, energy_shape = shape(2, SLOTS, dtype=jnp.int32), shape(2, LANES, dtype=F32)
    message = shape(2 * VECS, LANES)
    spread, *messages = call(
        spread_kernel,
        (shape(NC, 2 * VECS, LANES), message, message),
        2,
        [
            pltpu.VMEM((VECS, 2, LANES), BF16),
            pltpu.VMEM((2, LANES), F32),
            pltpu.SemaphoreType.DMA((2,)),
        ],
        first=pl.BlockSpec(memory_space=pl.ANY),
        limit=60,
    )(vectors, energies)
    received = [
        lax.ppermute(message, ("core", "zl"), [owner_of(n, k) for n in range(8)])
        for k, message in enumerate(messages)
    ]
    slab = exchange(spread, COL)
    index, energies = call(index_kernel, (index_shape, energy_shape), 3, scalars=(1,))(
        tile_coords, tile_counts, energies
    )
    grouped, own, owned, owned_energies, index, energies = call(
        regroup_kernel,
        (shape(NR, GROUP * VECS, LANES), piece, piece, energy_shape, index_shape, energy_shape),
        5,
    )(slab, *received, index, energies)
    fields = exchange(grouped, ROW)
    partial = call(
        functools.partial(tiles_kernel, True),
        shape(PIECES, 3 * VECS + MESSAGE, LANES),
        5,
        scratch + [pltpu.VMEM((3, PIECES, VECS, LANES), BF16)],
        scalars=(0,),
    )(index, fields, tiles, own, energies)
    by_owner, back = call(
        collect_owner_kernel,
        (shape(NR, 2 * VECS + MESSAGE, LANES), shape(2, VECS, LANES, dtype=F32)),
        1,
    )(exchange(partial, PIECE))
    residual = call(solve_kernel, shape(NR, 2 * VECS, LANES), 4)(
        exchange(by_owner, OWNER), back, owned, owned_energies
    )

    grouped = call(regroup_back_kernel, shape(PIECES, 3 * VECS, LANES), 1)(exchange(residual, OWNER))
    partial, own = call(
        functools.partial(tiles_kernel, False),
        (shape(NR, GROUP * VECS, LANES), piece),
        3,
        scratch,
        scalars=(0,),
    )(index, exchange(grouped, PIECE), tiles)
    by_block, back = call(
        collect_kernel, (shape(NC, 2 * VECS, LANES), shape(2, VECS, LANES, dtype=F32)), 1
    )(exchange(partial, ROW))
    return call(
        finish_kernel, (shape(VECS, 2, LANES), shape(VECS, 2, LANES, dtype=F32)), 4
    )(exchange(by_block, COL), back, own, energies)


def solution(mesh):
    devices = np.asarray(mesh.devices).reshape(2, 4, 2, 8, 4)
    fine = jax.sharding.Mesh(devices, ("zh", "x", "core", "y", "zl"))
    row, col = ("zh", "x", "core"), ("y", "zl")
    in_specs = (
        P(None, row, col),
        P(row, col, None, None),
        P(None, row, col),
        P(row, col),
        P(row, col),
    )
    out_specs = (P(None, row, col), P(None, row, col))
    return jax.shard_map(shards, mesh=fine, in_specs=in_specs, out_specs=out_specs, check_vma=False)
```

```python
import functools

import jax
import jax.numpy as jnp
import numpy as np
from jax import lax
from jax.experimental import pallas as pl
from jax.experimental.pallas import tpu as pltpu
from jax.sharding import PartitionSpec as P

F32 = jnp.float32
BF16 = jnp.bfloat16
VECS = 16
LANES = 128
HALF = 64
MESSAGE = 8
NR = 16
NC = 32
GROUP = 6
PIECES = 32
SLOTS = 128
UNROLL = 32
ROW_DEAD = NR * 8
COL_DEAD = NR * 4
ROW = ("core", "x", "zh")
COL = ("zl", "y")
PIECE = ("x", "zh", "zl")
OWNER = ("y", "core")
VMEM = pl.BlockSpec(memory_space=pltpu.VMEM)
SMEM = pl.BlockSpec(memory_space=pltpu.SMEM)
NT_DIMS = (((1,), (1,)), ((), ()))


def row_at(r):
    return (r % 2) * 8 + (r // 2 % 4) * 2 + r // 8


def col_at(c):
    return (c % 4) * 8 + c // 4


def shape(*dims, dtype=BF16):
    return jax.ShapeDtypeStruct(dims, dtype)


def call(kernel, outs, n_in, scratch=(), scalars=(), first=VMEM, limit=32):
    specs = [SMEM if n in scalars else first for n in range(n_in)]
    return pl.pallas_call(
        kernel,
        out_shape=outs,
        in_specs=specs,
        out_specs=jax.tree.map(lambda _: VMEM, outs),
        scratch_shapes=list(scratch),
        compiler_params=pltpu.CompilerParams(vmem_limit_bytes=limit * 1024 * 1024),
    )


def lane_index():
    return lax.broadcasted_iota(jnp.int32, (VECS, LANES), 1)


def split2(value):
    high = value.astype(BF16)
    return high, (value - high.astype(F32)).astype(BF16)


def split3(value):
    high = value.astype(BF16)
    rest = value - high.astype(F32)
    middle = rest.astype(BF16)
    low = (rest - middle.astype(F32)).astype(BF16)
    return high, middle, low


def piece_at(x, zh, core, j):
    return x * 8 + zh * 4 + core * 2 + j


def locate(by_row, x, zh, core, j, slot):
    if by_row:
        place = slot * 2 + j if slot < 2 else 4 + j
        return core * 8 + x * 2 + zh, slice(place * VECS, (place + 1) * VECS)
    return piece_at(x, zh, core, j), slice(slot * VECS, (slot + 1) * VECS)


INNER = [(zh, core, j) for zh in range(2) for core in range(2) for j in range(2)]


def spread_kernel(x_hbm, e_hbm, out_ref, even_ref, odd_ref, x_ref, e_ref, sems):
    pairs = ((x_hbm, x_ref), (e_hbm, e_ref))
    copies = [pltpu.make_async_copy(a, b, sems.at[n]) for n, (a, b) in enumerate(pairs)]
    for copy in copies:
        copy.start()
    for copy in copies:
        copy.wait()
    for j in range(2):
        value = x_ref[:, j, :]
        for c in range(NC):
            out_ref[c, j * VECS : (j + 1) * VECS] = value
    odd = lax.rem(lax.axis_index("zl"), 2)
    row = lax.broadcasted_iota(jnp.int32, (VECS, LANES), 0)
    for k, message in enumerate((even_ref, odd_ref)):
        message[:VECS] = jnp.where(odd == k, x_ref[:, 0, :], x_ref[:, 1, :])
        terms = jnp.zeros((VECS, LANES), F32)
        for n, term in enumerate(split3(jnp.where(odd == k, e_ref[0:1], e_ref[1:2]))):
            terms = jnp.where(row == n, term.astype(F32), terms)
        message[VECS:] = terms.astype(BF16)


def index_kernel(coords_ref, counts_ref, e_ref, index_ref, energy_ref):
    live = lax.broadcasted_iota(jnp.int32, (1, SLOTS), 1) < counts_ref[0, 0]
    for n, dead in ((0, ROW_DEAD), (1, COL_DEAD)):
        coords = coords_ref[n]
        major = coords >> 6
        piece = ((major >> 2) & 3) * 8 + (major >> 4) * 4 + (major & 3)
        if n == 0:
            piece = piece * 2 + ((coords >> 1) & 1)
        index_ref[n : n + 1] = jnp.where(live, piece * 2 + (coords & 1), dead)
    energy_ref[...] = e_ref[...]


def regroup_kernel(
    in_ref, even_ref, odd_ref, index_in, e_in, out_ref, own_ref, owned_ref, energy_ref, index_out, e_out
):
    index_out[...] = index_in[...]
    e_out[...] = e_in[...]
    wide = 2 * VECS
    y, zl = lax.axis_index("y"), lax.axis_index("zl")
    own = in_ref[zl * 8 + y]
    odd = lax.rem(zl, 2)
    for j in range(2):
        own_ref[j] = own[j * VECS : (j + 1) * VECS]
        message = jnp.where(odd == j, even_ref[...], odd_ref[...])
        owned_ref[j] = message[:VECS]
        terms = message[VECS:].astype(F32)
        energy_ref[j : j + 1] = terms[0:1] + terms[1:2] + terms[2:3]
    for r in range(NR):
        at = row_at(r)
        for s in range(2):
            out_ref[at, s * wide : (s + 1) * wide] = in_ref[col_at(2 * r + s)]
        out_ref[at, 2 * wide :] = own


def regroup_back_kernel(in_ref, out_ref):
    y, core = lax.axis_index("y"), lax.axis_index("core")
    for zl in range(4):
        column = in_ref[y * 2 + zl // 2, (zl % 2) * VECS : (zl % 2 + 1) * VECS]
        for block in range(8):
            zh, x = block // 4, block % 4
            at = (x * 2 + zh) * 4 + zl
            out_ref[at, : 2 * VECS] = in_ref[block * 2 + core]
            out_ref[at, 2 * VECS :] = column


def tiles_kernel(first, *refs):
    if first:
        index_ref, x_ref, w_ref, own_ref, e_ref, out_ref, *scratch = refs
    else:
        index_ref, x_ref, w_ref, out_ref, own_ref, *scratch = refs
    field_row, field_col, acc_row, acc_col, idx_ref, sem = scratch[:6]
    fetch = pltpu.make_async_copy(index_ref, idx_ref, sem)
    fetch.start()
    low_half = lane_index() < HALF
    zero = jnp.zeros((VECS, LANES), F32)
    half_mask = [low_half, jnp.logical_not(low_half)]
    half_one = [jnp.where(m, 1.0, 0.0).astype(BF16) for m in half_mask]
    own_piece = piece_at(lax.axis_index("x"), lax.axis_index("zh"), lax.axis_index("core"), 0)

    def part(g):
        return slice(g * VECS, (g + 1) * VECS)

    def place(piece, slot):
        if slot < 2:
            return field_row, acc_row, (piece * 2 + slot) * 2
        return field_col, acc_col, piece * 2

    def duplicate(x, carry):
        for zh, core, j in INNER:
            for slot in range(3):
                chunk, rows = locate(first, x, zh, core, j, slot)
                value = x_ref[chunk, rows].astype(F32)
                turned = pltpu.roll(value, HALF, 1)
                field, acc, at = place(piece_at(x, zh, core, j), slot)
                field[at] = jnp.where(low_half, value, turned).astype(BF16)
                field[at + 1] = jnp.where(low_half, turned, value).astype(BF16)
                acc[at] = zero
                acc[at + 1] = zero
        return carry

    lax.fori_loop(0, 4, duplicate, 0)
    for field, acc, dead in ((field_row, acc_row, ROW_DEAD), (field_col, acc_col, COL_DEAD)):
        field[dead] = zero.astype(BF16)
        acc[dead] = zero

    def block(b, carry):
        work = []
        for u in range(UNROLL):
            q = b * UNROLL + u
            rows = [idx_ref[0, q * 4 + k] for k in range(4)]
            cols = [idx_ref[1, q * 4 + k] for k in range(4)]
            w = w_ref[pl.ds(2 * q, 2)].reshape(2 * HALF, LANES)
            left_f = jnp.concatenate([field_col[cols[k]] * half_one[k % 2] for k in range(4)], axis=0)
            left_b = jnp.concatenate([field_row[rows[k]] * half_one[k // 2] for k in range(4)], axis=0)
            forward = lax.dot_general(left_f, w, NT_DIMS, preferred_element_type=F32)
            backward = jnp.dot(left_b, w, preferred_element_type=F32)
            work.append((rows, cols, forward, backward))
        for rows, cols, forward, backward in work:
            for k in range(4):
                acc_row[rows[k]] += jnp.where(half_mask[k // 2], forward[part(k)], 0.0)
                acc_col[cols[k]] += jnp.where(half_mask[k % 2], backward[part(k)], 0.0)
        return carry

    fetch.wait()
    lax.fori_loop(0, SLOTS // 4 // UNROLL, block, 0)

    def folded(piece, slot):
        _, acc, at = place(piece, slot)
        one, two = acc[at], acc[at + 1]
        return jnp.where(low_half, one, two) + pltpu.roll(jnp.where(low_half, two, one), HALF, 1)

    def pack(x, carry):
        for zh, core, j in INNER:
            piece = piece_at(x, zh, core, j)
            for slot in range(3):
                total = folded(piece, slot)
                chunk, rows = locate(not first, x, zh, core, j, slot)
                out_ref[chunk, rows] = total.astype(BF16)
                if first and slot == 2:
                    for n, term in enumerate(split3(total)):
                        scratch[6][n, piece] = term
        return carry

    if not first:
        lax.fori_loop(0, 4, pack, 0)
        for j in range(2):
            own_ref[j] = x_ref[own_piece + j, part(2)]
        return

    lax.fori_loop(0, 4, pack, 0)
    terms = scratch[6]
    left = jnp.concatenate(
        [jnp.concatenate([terms[n, p] for p in range(PIECES)], axis=1) for n in range(3)], axis=0
    )
    pieces = []
    for x in range(4):
        for zh, core, j in INNER:
            chunk, rows = locate(True, x, zh, core, j, 2)
            pieces.append(x_ref[chunk, rows])
    crosses = lax.dot_general(
        left, jnp.concatenate(pieces, axis=1), NT_DIMS, preferred_element_type=F32
    )
    cross = crosses[:VECS] + crosses[VECS : 2 * VECS] + crosses[2 * VECS :]
    gram = jnp.zeros((VECS, VECS), F32)
    for j in range(2):
        own = own_ref[j]
        gram = gram + lax.dot_general(own, own, NT_DIMS, preferred_element_type=F32)
        for term in split3(own.astype(F32) * (0.5 * e_ref[j : j + 1, :])):
            cross = cross + lax.dot_general(term, own, NT_DIMS, preferred_element_type=F32)
    message = message_of(widen(gram), widen(cross))
    for p in range(PIECES):
        out_ref[p, 3 * VECS :] = message


def widen(value):
    return jnp.concatenate([value, jnp.zeros((VECS, LANES - VECS), F32)], axis=1)


def message_of(gram, cross):
    total = jnp.zeros((VECS, LANES), F32)
    for n, part in enumerate(split2(gram) + split2(cross)):
        part = part.astype(F32)
        total = total + (pltpu.roll(part, n * VECS, 1) if n else part)
    return (total[:MESSAGE] + pltpu.roll(total[MESSAGE:], HALF, 1)).astype(BF16)


def read_message(total):
    total = jnp.concatenate([total, pltpu.roll(total, HALF, 1)], axis=0)
    keep = lane_index() < VECS
    found = []
    for n in (0, 2):
        high = pltpu.roll(total, LANES - n * VECS, 1) if n else total
        low = pltpu.roll(total, LANES - (n + 1) * VECS, 1)
        found.append(jnp.where(keep, high + low, 0.0))
    return found


def sum_over(in_ref, start, rows, chunks=None):
    total = None
    for n in range(in_ref.shape[0]) if chunks is None else chunks:
        value = in_ref[n, start : start + rows].astype(F32)
        total = value if total is None else total + value
    return total


def collect_owner_kernel(in_ref, out_ref, back_ref):
    wide = 2 * VECS
    y, core = lax.axis_index("y"), lax.axis_index("core")
    nothing = jnp.zeros((wide, LANES), BF16)
    for block in range(8):
        zh, x = block // 4, block % 4
        chunks = [(x * 2 + zh) * 4 + zl for zl in range(4)]
        out_ref[block * 2 + core, :wide] = sum_over(in_ref, 0, wide, chunks).astype(BF16)
        out_ref[block * 2 + 1 - core, :wide] = nothing
    sums = []
    for zl in range(4):
        sums.append(sum_over(in_ref, wide, VECS, [n * 4 + zl for n in range(8)]))
    for s in range(2):
        same = core == 0
        back_ref[s] = jnp.where(same, sums[s], sums[2 + s])
        other = jnp.where(same, sums[2 + s], sums[s])
        out_ref[y * 2 + 1 - core, s * VECS : (s + 1) * VECS] = other.astype(BF16)
    message = message_of(*read_message(sum_over(in_ref, 3 * VECS, MESSAGE)))
    for n in range(2 * 8):
        out_ref[n, wide:] = message


def solve_kernel(in_ref, back_ref, owned_ref, e_ref, out_ref):
    gram, cross = read_message(sum_over(in_ref, 2 * VECS, MESSAGE))
    wide = jnp.concatenate([cross, jnp.zeros((LANES - VECS, LANES), F32)], axis=0)
    cross = cross + jnp.transpose(wide)[:VECS]
    state = jnp.concatenate([gram, cross], axis=0)
    lane = lax.broadcasted_iota(jnp.int32, (2 * VECS, LANES), 1)
    for p in range(VECS):
        column = state[:, p : p + 1] * (1.0 / state[p : p + 1, p : p + 1])
        state = jnp.where(lane == p, column, state - column * state[p : p + 1])
    mix = state[VECS:]
    for s in range(2):
        v = owned_ref[s].astype(F32)
        product = sum_over(in_ref, s * VECS, VECS) + back_ref[s] + e_ref[s : s + 1, :] * v
        shifted = jnp.zeros((VECS, LANES), F32)
        for k in range(VECS):
            shifted = shifted + mix[:, k : k + 1] * v[k : k + 1, :]
        value = (product - shifted).astype(BF16)
        for n in range(2 * 8):
            out_ref[n, s * VECS : (s + 1) * VECS] = value


def collect_kernel(in_ref, out_ref, back_ref):
    wide = 2 * VECS
    for r in range(NR):
        for s in range(2):
            out_ref[col_at(2 * r + s)] = in_ref[row_at(r), s * wide : (s + 1) * wide]
    for j in range(2):
        back_ref[j] = sum_over(in_ref, (4 + j) * VECS, VECS)


def finish_kernel(in_ref, back_ref, own_ref, e_ref, residual_ref, out_ref):
    for j in range(2):
        own = own_ref[j]
        total = sum_over(in_ref, j * VECS, VECS) + back_ref[j]
        residual_ref[:, j, :] = own
        out_ref[:, j, :] = total + e_ref[j : j + 1, :] * own.astype(F32)


def owner_of(n, k):
    core, zl = n // 4, n % 4
    return n, zl // 2 * 4 + core * 2 + (zl % 2 ^ k)


def exchange(value, axis):
    return lax.all_to_all(value, axis, split_axis=0, concat_axis=0, tiled=True)


def shards(vectors, tile_values, tile_coords, tile_counts, energies):
    tiles = tile_values[0]
    piece = shape(2, VECS, LANES)
    scratch = [
        pltpu.VMEM((ROW_DEAD + 1, VECS, LANES), BF16),
        pltpu.VMEM((COL_DEAD + 1, VECS, LANES), BF16),
        pltpu.VMEM((ROW_DEAD + 1, VECS, LANES), F32),
        pltpu.VMEM((COL_DEAD + 1, VECS, LANES), F32),
        pltpu.SMEM((2, SLOTS), jnp.int32),
        pltpu.SemaphoreType.DMA,
    ]
    index_shape, energy_shape = shape(2, SLOTS, dtype=jnp.int32), shape(2, LANES, dtype=F32)
    message = shape(2 * VECS, LANES)
    spread, *messages = call(
        spread_kernel,
        (shape(NC, 2 * VECS, LANES), message, message),
        2,
        [
            pltpu.VMEM((VECS, 2, LANES), BF16),
            pltpu.VMEM((2, LANES), F32),
            pltpu.SemaphoreType.DMA((2,)),
        ],
        first=pl.BlockSpec(memory_space=pl.ANY),
        limit=60,
    )(vectors, energies)
    received = [
        lax.ppermute(message, ("core", "zl"), [owner_of(n, k) for n in range(8)])
        for k, message in enumerate(messages)
    ]
    slab = exchange(spread, COL)
    index, energies = call(index_kernel, (index_shape, energy_shape), 3, scalars=(1,))(
        tile_coords, tile_counts, energies
    )
    grouped, own, owned, owned_energies, index, energies = call(
        regroup_kernel,
        (shape(NR, GROUP * VECS, LANES), piece, piece, energy_shape, index_shape, energy_shape),
        5,
    )(slab, *received, index, energies)
    fields = exchange(grouped, ROW)
    partial = call(
        functools.partial(tiles_kernel, True),
        shape(PIECES, 3 * VECS + MESSAGE, LANES),
        5,
        scratch + [pltpu.VMEM((3, PIECES, VECS, LANES), BF16)],
    )(index, fields, tiles, own, energies)
    by_owner, back = call(
        collect_owner_kernel,
        (shape(NR, 2 * VECS + MESSAGE, LANES), shape(2, VECS, LANES, dtype=F32)),
        1,
    )(exchange(partial, PIECE))
    residual = call(solve_kernel, shape(NR, 2 * VECS, LANES), 4)(
        exchange(by_owner, OWNER), back, owned, owned_energies
    )

    grouped = call(regroup_back_kernel, shape(PIECES, 3 * VECS, LANES), 1)(exchange(residual, OWNER))
    partial, own = call(
        functools.partial(tiles_kernel, False),
        (shape(NR, GROUP * VECS, LANES), piece),
        3,
        scratch,
    )(index, exchange(grouped, PIECE), tiles)
    by_block, back = call(
        collect_kernel, (shape(NC, 2 * VECS, LANES), shape(2, VECS, LANES, dtype=F32)), 1
    )(exchange(partial, ROW))
    return call(
        finish_kernel, (shape(VECS, 2, LANES), shape(VECS, 2, LANES, dtype=F32)), 4
    )(exchange(by_block, COL), back, own, energies)


def solution(mesh):
    devices = np.asarray(mesh.devices).reshape(2, 4, 2, 8, 4)
    fine = jax.sharding.Mesh(devices, ("zh", "x", "core", "y", "zl"))
    row, col = ("zh", "x", "core"), ("y", "zl")
    in_specs = (
        P(None, row, col),
        P(row, col, None, None),
        P(None, row, col),
        P(row, col),
        P(row, col),
    )
    out_specs = (P(None, row, col), P(None, row, col))
    return jax.shard_map(shards, mesh=fine, in_specs=in_specs, out_specs=out_specs, check_vma=False)
```

```python
import functools

import jax
import jax.numpy as jnp
import numpy as np
from jax import lax
from jax.experimental import pallas as pl
from jax.experimental.pallas import tpu as pltpu
from jax.sharding import PartitionSpec as P

F32 = jnp.float32
BF16 = jnp.bfloat16
VECS = 16
LANES = 128
HALF = 64
MESSAGE = 8
NR = 16
NC = 32
GROUP = 6
PIECES = 32
SLOTS = 128
UNROLL = 32
ROW_DEAD = NR * 8
COL_DEAD = NR * 4
ROW = ("core", "x", "zh")
COL = ("zl", "y")
PIECE = ("x", "zh", "zl")
OWNER = ("y", "core")
VMEM = pl.BlockSpec(memory_space=pltpu.VMEM)
SMEM = pl.BlockSpec(memory_space=pltpu.SMEM)
NT_DIMS = (((1,), (1,)), ((), ()))


def row_at(r):
    return (r % 2) * 8 + (r // 2 % 4) * 2 + r // 8


def col_at(c):
    return (c % 4) * 8 + c // 4


def shape(*dims, dtype=BF16):
    return jax.ShapeDtypeStruct(dims, dtype)


def call(kernel, outs, n_in, scratch=(), scalars=(), first=VMEM, limit=32):
    specs = [SMEM if n in scalars else first for n in range(n_in)]
    return pl.pallas_call(
        kernel,
        out_shape=outs,
        in_specs=specs,
        out_specs=jax.tree.map(lambda _: VMEM, outs),
        scratch_shapes=list(scratch),
        compiler_params=pltpu.CompilerParams(vmem_limit_bytes=limit * 1024 * 1024),
    )


def lane_index():
    return lax.broadcasted_iota(jnp.int32, (VECS, LANES), 1)


def split2(value):
    high = value.astype(BF16)
    return high, (value - high.astype(F32)).astype(BF16)


def split3(value):
    high = value.astype(BF16)
    rest = value - high.astype(F32)
    middle = rest.astype(BF16)
    low = (rest - middle.astype(F32)).astype(BF16)
    return high, middle, low


def piece_at(x, zh, core, j):
    return x * 8 + zh * 4 + core * 2 + j


def locate(by_row, x, zh, core, j, slot):
    if by_row:
        place = slot * 2 + j if slot < 2 else 4 + j
        return core * 8 + x * 2 + zh, slice(place * VECS, (place + 1) * VECS)
    return piece_at(x, zh, core, j), slice(slot * VECS, (slot + 1) * VECS)


INNER = [(zh, core, j) for zh in range(2) for core in range(2) for j in range(2)]


def spread_kernel(x_hbm, e_hbm, out_ref, even_ref, odd_ref, x_ref, e_ref, sems):
    pairs = ((x_hbm, x_ref), (e_hbm, e_ref))
    copies = [pltpu.make_async_copy(a, b, sems.at[n]) for n, (a, b) in enumerate(pairs)]
    for copy in copies:
        copy.start()
    for copy in copies:
        copy.wait()
    for j in range(2):
        value = x_ref[:, j, :]
        for c in range(NC):
            out_ref[c, j * VECS : (j + 1) * VECS] = value
    odd = lax.rem(lax.axis_index("zl"), 2)
    row = lax.broadcasted_iota(jnp.int32, (VECS, LANES), 0)
    for k, message in enumerate((even_ref, odd_ref)):
        message[:VECS] = jnp.where(odd == k, x_ref[:, 0, :], x_ref[:, 1, :])
        terms = jnp.zeros((VECS, LANES), F32)
        for n, term in enumerate(split3(jnp.where(odd == k, e_ref[0:1], e_ref[1:2]))):
            terms = jnp.where(row == n, term.astype(F32), terms)
        message[VECS:] = terms.astype(BF16)


def index_kernel(coords_ref, counts_ref, e_ref, x_ref, index_ref, energy_ref, gram_ref, cross_ref):
    gram = jnp.zeros((VECS, VECS), F32)
    cross = jnp.zeros((VECS, VECS), F32)
    for j in range(2):
        own = x_ref[:, j, :]
        gram = gram + lax.dot_general(own, own, NT_DIMS, preferred_element_type=F32)
        for term in split3(own.astype(F32) * (0.5 * e_ref[j : j + 1, :])):
            cross = cross + lax.dot_general(term, own, NT_DIMS, preferred_element_type=F32)
    gram_ref[...] = widen(gram)
    cross_ref[...] = widen(cross)
    live = lax.broadcasted_iota(jnp.int32, (1, SLOTS), 1) < counts_ref[0, 0]
    for n, dead in ((0, ROW_DEAD), (1, COL_DEAD)):
        coords = coords_ref[n]
        major = coords >> 6
        piece = ((major >> 2) & 3) * 8 + (major >> 4) * 4 + (major & 3)
        if n == 0:
            piece = piece * 2 + ((coords >> 1) & 1)
        index_ref[n : n + 1] = jnp.where(live, piece * 2 + (coords & 1), dead)
    energy_ref[...] = e_ref[...]


def regroup_kernel(
    in_ref, even_ref, odd_ref, index_in, e_in, out_ref, owned_ref, energy_ref, index_out, e_out
):
    index_out[...] = index_in[...]
    e_out[...] = e_in[...]
    wide = 2 * VECS
    y, zl = lax.axis_index("y"), lax.axis_index("zl")
    own = in_ref[zl * 8 + y]
    odd = lax.rem(zl, 2)
    for j in range(2):
        message = jnp.where(odd == j, even_ref[...], odd_ref[...])
        owned_ref[j] = message[:VECS]
        terms = message[VECS:].astype(F32)
        energy_ref[j : j + 1] = terms[0:1] + terms[1:2] + terms[2:3]
    for r in range(NR):
        at = row_at(r)
        for s in range(2):
            out_ref[at, s * wide : (s + 1) * wide] = in_ref[col_at(2 * r + s)]
        out_ref[at, 2 * wide :] = own


def regroup_back_kernel(in_ref, out_ref):
    y, core = lax.axis_index("y"), lax.axis_index("core")
    for zl in range(4):
        column = in_ref[y * 2 + zl // 2, (zl % 2) * VECS : (zl % 2 + 1) * VECS]
        for block in range(8):
            zh, x = block // 4, block % 4
            at = (x * 2 + zh) * 4 + zl
            out_ref[at, : 2 * VECS] = in_ref[block * 2 + core]
            out_ref[at, 2 * VECS :] = column


def tiles_kernel(first, *refs):
    if first:
        index_ref, x_ref, w_ref, gram_ref, cross_ref, out_ref, *scratch = refs
    else:
        index_ref, x_ref, w_ref, out_ref, own_ref, *scratch = refs
    field_row, field_col, acc_row, acc_col, idx_ref, sem = scratch[:6]
    fetch = pltpu.make_async_copy(index_ref, idx_ref, sem)
    fetch.start()
    low_half = lane_index() < HALF
    zero = jnp.zeros((VECS, LANES), F32)
    half_mask = [low_half, jnp.logical_not(low_half)]
    half_one = [jnp.where(m, 1.0, 0.0).astype(BF16) for m in half_mask]
    own_piece = piece_at(lax.axis_index("x"), lax.axis_index("zh"), lax.axis_index("core"), 0)

    def part(g):
        return slice(g * VECS, (g + 1) * VECS)

    def place(piece, slot):
        if slot < 2:
            return field_row, acc_row, (piece * 2 + slot) * 2
        return field_col, acc_col, piece * 2

    def duplicate(x, carry):
        for zh, core, j in INNER:
            for slot in range(3):
                chunk, rows = locate(first, x, zh, core, j, slot)
                value = x_ref[chunk, rows].astype(F32)
                turned = pltpu.roll(value, HALF, 1)
                field, acc, at = place(piece_at(x, zh, core, j), slot)
                field[at] = jnp.where(low_half, value, turned).astype(BF16)
                field[at + 1] = jnp.where(low_half, turned, value).astype(BF16)
                acc[at] = zero
                acc[at + 1] = zero
        return carry

    lax.fori_loop(0, 4, duplicate, 0)
    for field, acc, dead in ((field_row, acc_row, ROW_DEAD), (field_col, acc_col, COL_DEAD)):
        field[dead] = zero.astype(BF16)
        acc[dead] = zero

    def block(b, carry):
        work = []
        for u in range(UNROLL):
            q = b * UNROLL + u
            rows = [idx_ref[0, q * 4 + k] for k in range(4)]
            cols = [idx_ref[1, q * 4 + k] for k in range(4)]
            w = w_ref[pl.ds(2 * q, 2)].reshape(2 * HALF, LANES)
            left_f = jnp.concatenate([field_col[cols[k]] * half_one[k % 2] for k in range(4)], axis=0)
            left_b = jnp.concatenate([field_row[rows[k]] * half_one[k // 2] for k in range(4)], axis=0)
            forward = lax.dot_general(left_f, w, NT_DIMS, preferred_element_type=F32)
            backward = jnp.dot(left_b, w, preferred_element_type=F32)
            work.append((rows, cols, forward, backward))
        for rows, cols, forward, backward in work:
            for k in range(4):
                acc_row[rows[k]] += jnp.where(half_mask[k // 2], forward[part(k)], 0.0)
                acc_col[cols[k]] += jnp.where(half_mask[k % 2], backward[part(k)], 0.0)
        return carry

    fetch.wait()
    lax.fori_loop(0, SLOTS // 4 // UNROLL, block, 0)

    def folded(piece, slot):
        _, acc, at = place(piece, slot)
        one, two = acc[at], acc[at + 1]
        return jnp.where(low_half, one, two) + pltpu.roll(jnp.where(low_half, two, one), HALF, 1)

    def pack(x, carry):
        for zh, core, j in INNER:
            piece = piece_at(x, zh, core, j)
            for slot in range(3):
                total = folded(piece, slot)
                chunk, rows = locate(not first, x, zh, core, j, slot)
                out_ref[chunk, rows] = total.astype(BF16)
                if first and slot == 2:
                    for n, term in enumerate(split3(total)):
                        scratch[6][n, piece] = term
        return carry

    if not first:
        lax.fori_loop(0, 4, pack, 0)
        for j in range(2):
            own_ref[j] = x_ref[own_piece + j, part(2)]
        return

    lax.fori_loop(0, 4, pack, 0)
    terms = scratch[6]
    left = jnp.concatenate(
        [jnp.concatenate([terms[n, p] for p in range(PIECES)], axis=1) for n in range(3)], axis=0
    )
    pieces = []
    for x in range(4):
        for zh, core, j in INNER:
            chunk, rows = locate(True, x, zh, core, j, 2)
            pieces.append(x_ref[chunk, rows])
    crosses = lax.dot_general(
        left, jnp.concatenate(pieces, axis=1), NT_DIMS, preferred_element_type=F32
    )
    cross = crosses[:VECS] + crosses[VECS : 2 * VECS] + crosses[2 * VECS :]
    message = message_of(gram_ref[...], cross_ref[...] + widen(cross))
    for p in range(PIECES):
        out_ref[p, 3 * VECS :] = message


def widen(value):
    return jnp.concatenate([value, jnp.zeros((VECS, LANES - VECS), F32)], axis=1)


def message_of(gram, cross):
    total = jnp.zeros((VECS, LANES), F32)
    for n, part in enumerate(split2(gram) + split2(cross)):
        part = part.astype(F32)
        total = total + (pltpu.roll(part, n * VECS, 1) if n else part)
    return (total[:MESSAGE] + pltpu.roll(total[MESSAGE:], HALF, 1)).astype(BF16)


def read_message(total):
    total = jnp.concatenate([total, pltpu.roll(total, HALF, 1)], axis=0)
    keep = lane_index() < VECS
    found = []
    for n in (0, 2):
        high = pltpu.roll(total, LANES - n * VECS, 1) if n else total
        low = pltpu.roll(total, LANES - (n + 1) * VECS, 1)
        found.append(jnp.where(keep, high + low, 0.0))
    return found


def sum_over(in_ref, start, rows, chunks=None):
    total = None
    for n in range(in_ref.shape[0]) if chunks is None else chunks:
        value = in_ref[n, start : start + rows].astype(F32)
        total = value if total is None else total + value
    return total


def collect_owner_kernel(in_ref, out_ref, back_ref):
    wide = 2 * VECS
    y, core = lax.axis_index("y"), lax.axis_index("core")
    nothing = jnp.zeros((wide, LANES), BF16)
    for block in range(8):
        zh, x = block // 4, block % 4
        chunks = [(x * 2 + zh) * 4 + zl for zl in range(4)]
        out_ref[block * 2 + core, :wide] = sum_over(in_ref, 0, wide, chunks).astype(BF16)
        out_ref[block * 2 + 1 - core, :wide] = nothing
    sums = []
    for zl in range(4):
        sums.append(sum_over(in_ref, wide, VECS, [n * 4 + zl for n in range(8)]))
    for s in range(2):
        same = core == 0
        back_ref[s] = jnp.where(same, sums[s], sums[2 + s])
        other = jnp.where(same, sums[2 + s], sums[s])
        out_ref[y * 2 + 1 - core, s * VECS : (s + 1) * VECS] = other.astype(BF16)
    message = message_of(*read_message(sum_over(in_ref, 3 * VECS, MESSAGE)))
    for n in range(2 * 8):
        out_ref[n, wide:] = message


def solve_kernel(in_ref, back_ref, owned_ref, e_ref, out_ref):
    gram, cross = read_message(sum_over(in_ref, 2 * VECS, MESSAGE))
    wide = jnp.concatenate([cross, jnp.zeros((LANES - VECS, LANES), F32)], axis=0)
    cross = cross + jnp.transpose(wide)[:VECS]
    state = jnp.concatenate([gram, cross], axis=0)
    columns = [jnp.broadcast_to(state[:, p : p + 1], (2 * VECS, LANES)) for p in range(VECS)]
    for p in range(VECS):
        scaled = columns[p] * (1.0 / columns[p][p : p + 1])
        columns = [
            scaled if q == p else column - scaled * column[p : p + 1]
            for q, column in enumerate(columns)
        ]
    for s in range(2):
        v = owned_ref[s].astype(F32)
        product = sum_over(in_ref, s * VECS, VECS) + back_ref[s] + e_ref[s : s + 1, :] * v
        shifted = jnp.zeros((VECS, LANES), F32)
        for k in range(VECS):
            shifted = shifted + columns[k][VECS:] * v[k : k + 1, :]
        value = (product - shifted).astype(BF16)
        for n in range(2 * 8):
            out_ref[n, s * VECS : (s + 1) * VECS] = value


def collect_kernel(in_ref, out_ref, back_ref):
    wide = 2 * VECS
    for r in range(NR):
        for s in range(2):
            out_ref[col_at(2 * r + s)] = in_ref[row_at(r), s * wide : (s + 1) * wide]
    for j in range(2):
        back_ref[j] = sum_over(in_ref, (4 + j) * VECS, VECS)


def finish_kernel(in_ref, back_ref, own_ref, e_ref, residual_ref, out_ref):
    for j in range(2):
        own = own_ref[j]
        total = sum_over(in_ref, j * VECS, VECS) + back_ref[j]
        residual_ref[:, j, :] = own
        out_ref[:, j, :] = total + e_ref[j : j + 1, :] * own.astype(F32)


def owner_of(n, k):
    core, zl = n // 4, n % 4
    return n, zl // 2 * 4 + core * 2 + (zl % 2 ^ k)


def exchange(value, axis):
    return lax.all_to_all(value, axis, split_axis=0, concat_axis=0, tiled=True)


def shards(vectors, tile_values, tile_coords, tile_counts, energies):
    tiles = tile_values[0]
    piece = shape(2, VECS, LANES)
    scratch = [
        pltpu.VMEM((ROW_DEAD + 1, VECS, LANES), BF16),
        pltpu.VMEM((COL_DEAD + 1, VECS, LANES), BF16),
        pltpu.VMEM((ROW_DEAD + 1, VECS, LANES), F32),
        pltpu.VMEM((COL_DEAD + 1, VECS, LANES), F32),
        pltpu.SMEM((2, SLOTS), jnp.int32),
        pltpu.SemaphoreType.DMA,
    ]
    index_shape, energy_shape = shape(2, SLOTS, dtype=jnp.int32), shape(2, LANES, dtype=F32)
    message = shape(2 * VECS, LANES)
    spread, *messages = call(
        spread_kernel,
        (shape(NC, 2 * VECS, LANES), message, message),
        2,
        [
            pltpu.VMEM((VECS, 2, LANES), BF16),
            pltpu.VMEM((2, LANES), F32),
            pltpu.SemaphoreType.DMA((2,)),
        ],
        first=pl.BlockSpec(memory_space=pl.ANY),
        limit=60,
    )(vectors, energies)
    received = [
        lax.ppermute(message, ("core", "zl"), [owner_of(n, k) for n in range(8)])
        for k, message in enumerate(messages)
    ]
    slab = exchange(spread, COL)
    sums = shape(VECS, LANES, dtype=F32)
    index, energies, gram, cross = call(
        index_kernel, (index_shape, energy_shape, sums, sums), 4, scalars=(1,)
    )(tile_coords, tile_counts, energies, vectors)
    grouped, owned, owned_energies, index, energies = call(
        regroup_kernel,
        (shape(NR, GROUP * VECS, LANES), piece, energy_shape, index_shape, energy_shape),
        5,
    )(slab, *received, index, energies)
    fields = exchange(grouped, ROW)
    partial = call(
        functools.partial(tiles_kernel, True),
        shape(PIECES, 3 * VECS + MESSAGE, LANES),
        5,
        scratch + [pltpu.VMEM((3, PIECES, VECS, LANES), BF16)],
    )(index, fields, tiles, gram, cross)
    by_owner, back = call(
        collect_owner_kernel,
        (shape(NR, 2 * VECS + MESSAGE, LANES), shape(2, VECS, LANES, dtype=F32)),
        1,
    )(exchange(partial, PIECE))
    residual = call(solve_kernel, shape(NR, 2 * VECS, LANES), 4)(
        exchange(by_owner, OWNER), back, owned, owned_energies
    )

    grouped = call(regroup_back_kernel, shape(PIECES, 3 * VECS, LANES), 1)(exchange(residual, OWNER))
    partial, own = call(
        functools.partial(tiles_kernel, False),
        (shape(NR, GROUP * VECS, LANES), piece),
        3,
        scratch,
    )(index, exchange(grouped, PIECE), tiles)
    by_block, back = call(
        collect_kernel, (shape(NC, 2 * VECS, LANES), shape(2, VECS, LANES, dtype=F32)), 1
    )(exchange(partial, ROW))
    return call(
        finish_kernel, (shape(VECS, 2, LANES), shape(VECS, 2, LANES, dtype=F32)), 4
    )(exchange(by_block, COL), back, own, energies)


def solution(mesh):
    devices = np.asarray(mesh.devices).reshape(2, 4, 2, 8, 4)
    fine = jax.sharding.Mesh(devices, ("zh", "x", "core", "y", "zl"))
    row, col = ("zh", "x", "core"), ("y", "zl")
    in_specs = (
        P(None, row, col),
        P(row, col, None, None),
        P(None, row, col),
        P(row, col),
        P(row, col),
    )
    out_specs = (P(None, row, col), P(None, row, col))
    return jax.shard_map(shards, mesh=fine, in_specs=in_specs, out_specs=out_specs, check_vma=False)
```

```python
import functools

import jax
import jax.numpy as jnp
import numpy as np
from jax import lax
from jax.experimental import pallas as pl
from jax.experimental.pallas import tpu as pltpu
from jax.sharding import PartitionSpec as P

F32 = jnp.float32
BF16 = jnp.bfloat16
VECS = 16
LANES = 128
HALF = 64
MESSAGE = 8
NR = 16
NC = 32
GROUP = 6
PIECES = 32
SLOTS = 128
UNROLL = 32
ROW_DEAD = NR * 8
COL_DEAD = NR * 4
ROW = ("core", "x", "zh")
COL = ("zl", "y")
PIECE = ("x", "zh", "zl")
OWNER = ("y", "core")
VMEM = pl.BlockSpec(memory_space=pltpu.VMEM)
SMEM = pl.BlockSpec(memory_space=pltpu.SMEM)
NT_DIMS = (((1,), (1,)), ((), ()))


def row_at(r):
    return (r % 2) * 8 + (r // 2 % 4) * 2 + r // 8


def col_at(c):
    return (c % 4) * 8 + c // 4


def shape(*dims, dtype=BF16):
    return jax.ShapeDtypeStruct(dims, dtype)


def call(kernel, outs, n_in, scratch=(), scalars=(), first=VMEM, limit=32):
    specs = [SMEM if n in scalars else first for n in range(n_in)]
    return pl.pallas_call(
        kernel,
        out_shape=outs,
        in_specs=specs,
        out_specs=jax.tree.map(lambda _: VMEM, outs),
        scratch_shapes=list(scratch),
        compiler_params=pltpu.CompilerParams(vmem_limit_bytes=limit * 1024 * 1024),
    )


def lane_index():
    return lax.broadcasted_iota(jnp.int32, (VECS, LANES), 1)


def split2(value):
    high = value.astype(BF16)
    return high, (value - high.astype(F32)).astype(BF16)


def split3(value):
    high = value.astype(BF16)
    rest = value - high.astype(F32)
    middle = rest.astype(BF16)
    low = (rest - middle.astype(F32)).astype(BF16)
    return high, middle, low


def piece_at(x, zh, core, j):
    return x * 8 + zh * 4 + core * 2 + j


def locate(by_row, x, zh, core, j, slot):
    if by_row:
        place = slot * 2 + j if slot < 2 else 4 + j
        return core * 8 + x * 2 + zh, slice(place * VECS, (place + 1) * VECS)
    return piece_at(x, zh, core, j), slice(slot * VECS, (slot + 1) * VECS)


INNER = [(zh, core, j) for zh in range(2) for core in range(2) for j in range(2)]


def spread_kernel(x_hbm, e_hbm, out_ref, even_ref, odd_ref, x_ref, e_ref, sems):
    pairs = ((x_hbm, x_ref), (e_hbm, e_ref))
    copies = [pltpu.make_async_copy(a, b, sems.at[n]) for n, (a, b) in enumerate(pairs)]
    for copy in copies:
        copy.start()
    for copy in copies:
        copy.wait()
    for j in range(2):
        value = x_ref[:, j, :]
        for c in range(NC):
            out_ref[c, j * VECS : (j + 1) * VECS] = value
    odd = lax.rem(lax.axis_index("zl"), 2)
    row = lax.broadcasted_iota(jnp.int32, (VECS, LANES), 0)
    for k, message in enumerate((even_ref, odd_ref)):
        message[:VECS] = jnp.where(odd == k, x_ref[:, 0, :], x_ref[:, 1, :])
        terms = jnp.zeros((VECS, LANES), F32)
        for n, term in enumerate(split3(jnp.where(odd == k, e_ref[0:1], e_ref[1:2]))):
            terms = jnp.where(row == n, term.astype(F32), terms)
        message[VECS:] = terms.astype(BF16)


def index_kernel(coords_ref, counts_ref, e_ref, x_ref, index_ref, energy_ref, gram_ref, cross_ref):
    gram = jnp.zeros((VECS, VECS), F32)
    cross = jnp.zeros((VECS, VECS), F32)
    for j in range(2):
        own = x_ref[:, j, :]
        gram = gram + lax.dot_general(own, own, NT_DIMS, preferred_element_type=F32)
        for term in split3(own.astype(F32) * (0.5 * e_ref[j : j + 1, :])):
            cross = cross + lax.dot_general(term, own, NT_DIMS, preferred_element_type=F32)
    gram_ref[...] = widen(gram)
    cross_ref[...] = widen(cross)
    live = lax.broadcasted_iota(jnp.int32, (1, SLOTS), 1) < counts_ref[0, 0]
    for n, dead in ((0, ROW_DEAD), (1, COL_DEAD)):
        coords = coords_ref[n]
        major = coords >> 6
        piece = ((major >> 2) & 3) * 8 + (major >> 4) * 4 + (major & 3)
        if n == 0:
            piece = piece * 2 + ((coords >> 1) & 1)
        index_ref[n : n + 1] = jnp.where(live, piece * 2 + (coords & 1), dead)
    energy_ref[...] = e_ref[...]


def regroup_kernel(
    in_ref, even_ref, odd_ref, index_in, e_in, out_ref, owned_ref, energy_ref, index_out, e_out
):
    index_out[...] = index_in[...]
    e_out[...] = e_in[...]
    wide = 2 * VECS
    y, zl = lax.axis_index("y"), lax.axis_index("zl")
    own = in_ref[zl * 8 + y]
    odd = lax.rem(zl, 2)
    for j in range(2):
        message = jnp.where(odd == j, even_ref[...], odd_ref[...])
        owned_ref[j] = message[:VECS]
        terms = message[VECS:].astype(F32)
        energy_ref[j : j + 1] = terms[0:1] + terms[1:2] + terms[2:3]
    for r in range(NR):
        at = row_at(r)
        for s in range(2):
            out_ref[at, s * wide : (s + 1) * wide] = in_ref[col_at(2 * r + s)]
        out_ref[at, 2 * wide :] = own


def regroup_back_kernel(in_ref, other_ref, out_ref):
    y, core = lax.axis_index("y"), lax.axis_index("core")
    for zl in range(4):
        rows = slice((zl % 2) * VECS, (zl % 2 + 1) * VECS)
        column = jnp.where(core == zl // 2, in_ref[y, rows], other_ref[rows])
        for block in range(8):
            zh, x = block // 4, block % 4
            at = (x * 2 + zh) * 4 + zl
            out_ref[at, : 2 * VECS] = in_ref[block]
            out_ref[at, 2 * VECS :] = column


def tiles_kernel(first, *refs):
    if first:
        index_ref, x_ref, w_ref, gram_ref, cross_ref, out_ref, *scratch = refs
    else:
        index_ref, x_ref, w_ref, out_ref, own_ref, *scratch = refs
    field_row, field_col, acc_row, acc_col, idx_ref, sem = scratch[:6]
    fetch = pltpu.make_async_copy(index_ref, idx_ref, sem)
    fetch.start()
    low_half = lane_index() < HALF
    zero = jnp.zeros((VECS, LANES), F32)
    half_mask = [low_half, jnp.logical_not(low_half)]
    half_one = [jnp.where(m, 1.0, 0.0).astype(BF16) for m in half_mask]
    own_piece = piece_at(lax.axis_index("x"), lax.axis_index("zh"), lax.axis_index("core"), 0)

    def part(g):
        return slice(g * VECS, (g + 1) * VECS)

    def place(piece, slot):
        if slot < 2:
            return field_row, acc_row, (piece * 2 + slot) * 2
        return field_col, acc_col, piece * 2

    def duplicate(x, carry):
        for zh, core, j in INNER:
            for slot in range(3):
                chunk, rows = locate(first, x, zh, core, j, slot)
                value = x_ref[chunk, rows].astype(F32)
                turned = pltpu.roll(value, HALF, 1)
                field, acc, at = place(piece_at(x, zh, core, j), slot)
                field[at] = jnp.where(low_half, value, turned).astype(BF16)
                field[at + 1] = jnp.where(low_half, turned, value).astype(BF16)
                acc[at] = zero
                acc[at + 1] = zero
        return carry

    lax.fori_loop(0, 4, duplicate, 0)
    for field, acc, dead in ((field_row, acc_row, ROW_DEAD), (field_col, acc_col, COL_DEAD)):
        field[dead] = zero.astype(BF16)
        acc[dead] = zero

    def block(b, carry):
        work = []
        for u in range(UNROLL):
            q = b * UNROLL + u
            rows = [idx_ref[0, q * 4 + k] for k in range(4)]
            cols = [idx_ref[1, q * 4 + k] for k in range(4)]
            w = w_ref[pl.ds(2 * q, 2)].reshape(2 * HALF, LANES)
            left_f = jnp.concatenate([field_col[cols[k]] * half_one[k % 2] for k in range(4)], axis=0)
            left_b = jnp.concatenate([field_row[rows[k]] * half_one[k // 2] for k in range(4)], axis=0)
            forward = lax.dot_general(left_f, w, NT_DIMS, preferred_element_type=F32)
            backward = jnp.dot(left_b, w, preferred_element_type=F32)
            work.append((rows, cols, forward, backward))
        for rows, cols, forward, backward in work:
            for k in range(4):
                acc_row[rows[k]] += jnp.where(half_mask[k // 2], forward[part(k)], 0.0)
                acc_col[cols[k]] += jnp.where(half_mask[k % 2], backward[part(k)], 0.0)
        return carry

    fetch.wait()
    lax.fori_loop(0, SLOTS // 4 // UNROLL, block, 0)

    def folded(piece, slot):
        _, acc, at = place(piece, slot)
        one, two = acc[at], acc[at + 1]
        return jnp.where(low_half, one, two) + pltpu.roll(jnp.where(low_half, two, one), HALF, 1)

    def pack(x, carry):
        for zh, core, j in INNER:
            piece = piece_at(x, zh, core, j)
            for slot in range(3):
                total = folded(piece, slot)
                chunk, rows = locate(not first, x, zh, core, j, slot)
                out_ref[chunk, rows] = total.astype(BF16)
                if first and slot == 2:
                    for n, term in enumerate(split3(total)):
                        scratch[6][n, piece] = term
        return carry

    if not first:
        lax.fori_loop(0, 4, pack, 0)
        for j in range(2):
            own_ref[j] = x_ref[own_piece + j, part(2)]
        return

    lax.fori_loop(0, 4, pack, 0)
    terms = scratch[6]
    left = jnp.concatenate(
        [jnp.concatenate([terms[n, p] for p in range(PIECES)], axis=1) for n in range(3)], axis=0
    )
    pieces = []
    for x in range(4):
        for zh, core, j in INNER:
            chunk, rows = locate(True, x, zh, core, j, 2)
            pieces.append(x_ref[chunk, rows])
    crosses = lax.dot_general(
        left, jnp.concatenate(pieces, axis=1), NT_DIMS, preferred_element_type=F32
    )
    cross = crosses[:VECS] + crosses[VECS : 2 * VECS] + crosses[2 * VECS :]
    message = message_of(gram_ref[...], cross_ref[...] + widen(cross))
    for p in range(PIECES):
        out_ref[p, 3 * VECS :] = message


def widen(value):
    return jnp.concatenate([value, jnp.zeros((VECS, LANES - VECS), F32)], axis=1)


def message_of(gram, cross):
    total = jnp.zeros((VECS, LANES), F32)
    for n, part in enumerate(split2(gram) + split2(cross)):
        part = part.astype(F32)
        total = total + (pltpu.roll(part, n * VECS, 1) if n else part)
    return (total[:MESSAGE] + pltpu.roll(total[MESSAGE:], HALF, 1)).astype(BF16)


def read_message(total):
    total = jnp.concatenate([total, pltpu.roll(total, HALF, 1)], axis=0)
    keep = lane_index() < VECS
    found = []
    for n in (0, 2):
        high = pltpu.roll(total, LANES - n * VECS, 1) if n else total
        low = pltpu.roll(total, LANES - (n + 1) * VECS, 1)
        found.append(jnp.where(keep, high + low, 0.0))
    return found


def sum_over(in_ref, start, rows, chunks=None):
    total = None
    for n in range(in_ref.shape[0]) if chunks is None else chunks:
        value = in_ref[n, start : start + rows].astype(F32)
        total = value if total is None else total + value
    return total


def collect_owner_kernel(in_ref, out_ref, back_ref):
    wide = 2 * VECS
    y, core = lax.axis_index("y"), lax.axis_index("core")
    nothing = jnp.zeros((wide, LANES), BF16)
    for block in range(8):
        zh, x = block // 4, block % 4
        chunks = [(x * 2 + zh) * 4 + zl for zl in range(4)]
        out_ref[block * 2 + core, :wide] = sum_over(in_ref, 0, wide, chunks).astype(BF16)
        out_ref[block * 2 + 1 - core, :wide] = nothing
    sums = []
    for zl in range(4):
        sums.append(sum_over(in_ref, wide, VECS, [n * 4 + zl for n in range(8)]))
    for s in range(2):
        same = core == 0
        back_ref[s] = jnp.where(same, sums[s], sums[2 + s])
        other = jnp.where(same, sums[2 + s], sums[s])
        out_ref[y * 2 + 1 - core, s * VECS : (s + 1) * VECS] = other.astype(BF16)
    message = message_of(*read_message(sum_over(in_ref, 3 * VECS, MESSAGE)))
    for n in range(2 * 8):
        out_ref[n, wide:] = message


def solve_kernel(in_ref, back_ref, owned_ref, e_ref, out_ref, sent_ref):
    gram, cross = read_message(sum_over(in_ref, 2 * VECS, MESSAGE))
    wide = jnp.concatenate([cross, jnp.zeros((LANES - VECS, LANES), F32)], axis=0)
    cross = cross + jnp.transpose(wide)[:VECS]
    state = jnp.concatenate([gram, cross], axis=0)
    columns = [jnp.broadcast_to(state[:, p : p + 1], (2 * VECS, LANES)) for p in range(VECS)]
    for p in range(VECS):
        scaled = columns[p] * (1.0 / columns[p][p : p + 1])
        columns = [
            scaled if q == p else column - scaled * column[p : p + 1]
            for q, column in enumerate(columns)
        ]
    for s in range(2):
        v = owned_ref[s].astype(F32)
        product = sum_over(in_ref, s * VECS, VECS) + back_ref[s] + e_ref[s : s + 1, :] * v
        shifted = jnp.zeros((VECS, LANES), F32)
        for k in range(VECS):
            shifted = shifted + columns[k][VECS:] * v[k : k + 1, :]
        value = (product - shifted).astype(BF16)
        sent_ref[s * VECS : (s + 1) * VECS] = value
        for n in range(8):
            out_ref[n, s * VECS : (s + 1) * VECS] = value


def collect_kernel(in_ref, out_ref, back_ref):
    wide = 2 * VECS
    for r in range(NR):
        for s in range(2):
            out_ref[col_at(2 * r + s)] = in_ref[row_at(r), s * wide : (s + 1) * wide]
    for j in range(2):
        back_ref[j] = sum_over(in_ref, (4 + j) * VECS, VECS)


def finish_kernel(in_ref, back_ref, own_ref, e_ref, residual_ref, out_ref):
    for j in range(2):
        own = own_ref[j]
        total = sum_over(in_ref, j * VECS, VECS) + back_ref[j]
        residual_ref[:, j, :] = own
        out_ref[:, j, :] = total + e_ref[j : j + 1, :] * own.astype(F32)


def owner_of(n, k):
    core, zl = n // 4, n % 4
    return n, zl // 2 * 4 + core * 2 + (zl % 2 ^ k)


def exchange(value, axis):
    return lax.all_to_all(value, axis, split_axis=0, concat_axis=0, tiled=True)


def shards(vectors, tile_values, tile_coords, tile_counts, energies):
    tiles = tile_values[0]
    piece = shape(2, VECS, LANES)
    scratch = [
        pltpu.VMEM((ROW_DEAD + 1, VECS, LANES), BF16),
        pltpu.VMEM((COL_DEAD + 1, VECS, LANES), BF16),
        pltpu.VMEM((ROW_DEAD + 1, VECS, LANES), F32),
        pltpu.VMEM((COL_DEAD + 1, VECS, LANES), F32),
        pltpu.SMEM((2, SLOTS), jnp.int32),
        pltpu.SemaphoreType.DMA,
    ]
    index_shape, energy_shape = shape(2, SLOTS, dtype=jnp.int32), shape(2, LANES, dtype=F32)
    message = shape(2 * VECS, LANES)
    spread, *messages = call(
        spread_kernel,
        (shape(NC, 2 * VECS, LANES), message, message),
        2,
        [
            pltpu.VMEM((VECS, 2, LANES), BF16),
            pltpu.VMEM((2, LANES), F32),
            pltpu.SemaphoreType.DMA((2,)),
        ],
        first=pl.BlockSpec(memory_space=pl.ANY),
        limit=60,
    )(vectors, energies)
    received = [
        lax.ppermute(message, ("core", "zl"), [owner_of(n, k) for n in range(8)])
        for k, message in enumerate(messages)
    ]
    slab = exchange(spread, COL)
    sums = shape(VECS, LANES, dtype=F32)
    index, energies, gram, cross = call(
        index_kernel, (index_shape, energy_shape, sums, sums), 4, scalars=(1,)
    )(tile_coords, tile_counts, energies, vectors)
    grouped, owned, owned_energies, index, energies = call(
        regroup_kernel,
        (shape(NR, GROUP * VECS, LANES), piece, energy_shape, index_shape, energy_shape),
        5,
    )(slab, *received, index, energies)
    fields = exchange(grouped, ROW)
    partial = call(
        functools.partial(tiles_kernel, True),
        shape(PIECES, 3 * VECS + MESSAGE, LANES),
        5,
        scratch + [pltpu.VMEM((3, PIECES, VECS, LANES), BF16)],
    )(index, fields, tiles, gram, cross)
    by_owner, back = call(
        collect_owner_kernel,
        (shape(NR, 2 * VECS + MESSAGE, LANES), shape(2, VECS, LANES, dtype=F32)),
        1,
    )(exchange(partial, PIECE))
    residual, sent = call(solve_kernel, (shape(8, 2 * VECS, LANES), message), 4)(
        exchange(by_owner, OWNER), back, owned, owned_energies
    )

    other = lax.ppermute(sent, "core", [(0, 1), (1, 0)])
    grouped = call(regroup_back_kernel, shape(PIECES, 3 * VECS, LANES), 2)(
        exchange(residual, "y"), other
    )
    partial, own = call(
        functools.partial(tiles_kernel, False),
        (shape(NR, GROUP * VECS, LANES), piece),
        3,
        scratch,
    )(index, exchange(grouped, PIECE), tiles)
    by_block, back = call(
        collect_kernel, (shape(NC, 2 * VECS, LANES), shape(2, VECS, LANES, dtype=F32)), 1
    )(exchange(partial, ROW))
    return call(
        finish_kernel, (shape(VECS, 2, LANES), shape(VECS, 2, LANES, dtype=F32)), 4
    )(exchange(by_block, COL), back, own, energies)


def solution(mesh):
    devices = np.asarray(mesh.devices).reshape(2, 4, 2, 8, 4)
    fine = jax.sharding.Mesh(devices, ("zh", "x", "core", "y", "zl"))
    row, col = ("zh", "x", "core"), ("y", "zl")
    in_specs = (
        P(None, row, col),
        P(row, col, None, None),
        P(None, row, col),
        P(row, col),
        P(row, col),
    )
    out_specs = (P(None, row, col), P(None, row, col))
    return jax.shard_map(shards, mesh=fine, in_specs=in_specs, out_specs=out_specs, check_vma=False)
```

```python
import functools

import jax
import jax.numpy as jnp
import numpy as np
from jax import lax
from jax.experimental import pallas as pl
from jax.experimental.pallas import tpu as pltpu
from jax.sharding import PartitionSpec as P

F32 = jnp.float32
BF16 = jnp.bfloat16
VECS = 16
LANES = 128
HALF = 64
MESSAGE = 8
NR = 16
NC = 32
GROUP = 6
PIECES = 32
SLOTS = 128
UNROLL = 32
ROW_DEAD = NR * 8
COL_DEAD = NR * 4
ROW = ("core", "x", "zh")
COL = ("zl", "y")
PIECE = ("x", "zh", "zl")
OWNER = ("y", "core")
VMEM = pl.BlockSpec(memory_space=pltpu.VMEM)
SMEM = pl.BlockSpec(memory_space=pltpu.SMEM)
NT_DIMS = (((1,), (1,)), ((), ()))


def row_at(r):
    return (r % 2) * 8 + (r // 2 % 4) * 2 + r // 8


def col_at(c):
    return (c % 4) * 8 + c // 4


def shape(*dims, dtype=BF16):
    return jax.ShapeDtypeStruct(dims, dtype)


def call(kernel, outs, n_in, scratch=(), scalars=(), first=VMEM, last=VMEM, limit=32):
    specs = [SMEM if n in scalars else first for n in range(n_in)]
    return pl.pallas_call(
        kernel,
        out_shape=outs,
        in_specs=specs,
        out_specs=jax.tree.map(lambda _: last, outs),
        scratch_shapes=list(scratch),
        compiler_params=pltpu.CompilerParams(vmem_limit_bytes=limit * 1024 * 1024),
    )


def lane_index():
    return lax.broadcasted_iota(jnp.int32, (VECS, LANES), 1)


def split2(value):
    high = value.astype(BF16)
    return high, (value - high.astype(F32)).astype(BF16)


def split3(value):
    high = value.astype(BF16)
    rest = value - high.astype(F32)
    middle = rest.astype(BF16)
    low = (rest - middle.astype(F32)).astype(BF16)
    return high, middle, low


def piece_at(x, zh, core, j):
    return x * 8 + zh * 4 + core * 2 + j


def locate(by_row, x, zh, core, j, slot):
    if by_row:
        place = slot * 2 + j if slot < 2 else 4 + j
        return core * 8 + x * 2 + zh, slice(place * VECS, (place + 1) * VECS)
    return piece_at(x, zh, core, j), slice(slot * VECS, (slot + 1) * VECS)


INNER = [(zh, core, j) for zh in range(2) for core in range(2) for j in range(2)]


def spread_kernel(x_hbm, e_hbm, out_hbm, even_hbm, odd_hbm, x_ref, e_ref, block_ref, even_ref, odd_ref, sems):
    fetches = [
        pltpu.make_async_copy(x_hbm, x_ref, sems.at[NC + 2]),
        pltpu.make_async_copy(e_hbm, e_ref, sems.at[NC + 3]),
    ]
    for fetch in fetches:
        fetch.start()
    fetches[0].wait()
    for j in range(2):
        block_ref[j * VECS : (j + 1) * VECS] = x_ref[:, j, :]
    copies = [pltpu.make_async_copy(block_ref, out_hbm.at[c], sems.at[c]) for c in range(NC)]
    for copy in copies:
        copy.start()
    fetches[1].wait()
    odd = lax.rem(lax.axis_index("zl"), 2)
    row = lax.broadcasted_iota(jnp.int32, (VECS, LANES), 0)
    for k, (message, target) in enumerate(((even_ref, even_hbm), (odd_ref, odd_hbm))):
        message[:VECS] = jnp.where(odd == k, x_ref[:, 0, :], x_ref[:, 1, :])
        terms = jnp.zeros((VECS, LANES), F32)
        for n, term in enumerate(split3(jnp.where(odd == k, e_ref[0:1], e_ref[1:2]))):
            terms = jnp.where(row == n, term.astype(F32), terms)
        message[VECS:] = terms.astype(BF16)
        copies.append(pltpu.make_async_copy(message, target, sems.at[NC + k]))
        copies[-1].start()
    for copy in copies:
        copy.wait()


def index_kernel(coords_ref, counts_ref, e_ref, x_ref, index_ref, energy_ref, gram_ref, cross_ref):
    gram = jnp.zeros((VECS, VECS), F32)
    cross = jnp.zeros((VECS, VECS), F32)
    for j in range(2):
        own = x_ref[:, j, :]
        gram = gram + lax.dot_general(own, own, NT_DIMS, preferred_element_type=F32)
        for term in split3(own.astype(F32) * (0.5 * e_ref[j : j + 1, :])):
            cross = cross + lax.dot_general(term, own, NT_DIMS, preferred_element_type=F32)
    gram_ref[...] = widen(gram)
    cross_ref[...] = widen(cross)
    live = lax.broadcasted_iota(jnp.int32, (1, SLOTS), 1) < counts_ref[0, 0]
    for n, dead in ((0, ROW_DEAD), (1, COL_DEAD)):
        coords = coords_ref[n]
        major = coords >> 6
        piece = ((major >> 2) & 3) * 8 + (major >> 4) * 4 + (major & 3)
        if n == 0:
            piece = piece * 2 + ((coords >> 1) & 1)
        index_ref[n : n + 1] = jnp.where(live, piece * 2 + (coords & 1), dead)
    energy_ref[...] = e_ref[...]


def regroup_kernel(
    in_ref, even_ref, odd_ref, index_in, e_in, out_ref, owned_ref, energy_ref, index_out, e_out
):
    index_out[...] = index_in[...]
    e_out[...] = e_in[...]
    wide = 2 * VECS
    y, zl = lax.axis_index("y"), lax.axis_index("zl")
    own = in_ref[zl * 8 + y]
    odd = lax.rem(zl, 2)
    for j in range(2):
        message = jnp.where(odd == j, even_ref[...], odd_ref[...])
        owned_ref[j] = message[:VECS]
        terms = message[VECS:].astype(F32)
        energy_ref[j : j + 1] = terms[0:1] + terms[1:2] + terms[2:3]
    for r in range(NR):
        at = row_at(r)
        for s in range(2):
            out_ref[at, s * wide : (s + 1) * wide] = in_ref[col_at(2 * r + s)]
        out_ref[at, 2 * wide :] = own


def regroup_back_kernel(in_ref, out_ref):
    y, core = lax.axis_index("y"), lax.axis_index("core")
    for zl in range(4):
        column = in_ref[y * 2 + zl // 2, (zl % 2) * VECS : (zl % 2 + 1) * VECS]
        for block in range(8):
            zh, x = block // 4, block % 4
            at = (x * 2 + zh) * 4 + zl
            out_ref[at, : 2 * VECS] = in_ref[block * 2 + core]
            out_ref[at, 2 * VECS :] = column


def tiles_kernel(first, *refs):
    if first:
        index_ref, x_ref, w_ref, gram_ref, cross_ref, out_ref, *scratch = refs
    else:
        index_ref, x_ref, w_ref, out_ref, own_ref, *scratch = refs
    field_row, field_col, acc_row, acc_col, idx_ref, sem = scratch[:6]
    fetch = pltpu.make_async_copy(index_ref, idx_ref, sem)
    fetch.start()
    low_half = lane_index() < HALF
    zero = jnp.zeros((VECS, LANES), F32)
    half_mask = [low_half, jnp.logical_not(low_half)]
    half_one = [jnp.where(m, 1.0, 0.0).astype(BF16) for m in half_mask]
    own_piece = piece_at(lax.axis_index("x"), lax.axis_index("zh"), lax.axis_index("core"), 0)

    def part(g):
        return slice(g * VECS, (g + 1) * VECS)

    def place(piece, slot):
        if slot < 2:
            return field_row, acc_row, (piece * 2 + slot) * 2
        return field_col, acc_col, piece * 2

    def duplicate(x, carry):
        for zh, core, j in INNER:
            for slot in range(3):
                chunk, rows = locate(first, x, zh, core, j, slot)
                value = x_ref[chunk, rows].astype(F32)
                turned = pltpu.roll(value, HALF, 1)
                field, acc, at = place(piece_at(x, zh, core, j), slot)
                field[at] = jnp.where(low_half, value, turned).astype(BF16)
                field[at + 1] = jnp.where(low_half, turned, value).astype(BF16)
                acc[at] = zero
                acc[at + 1] = zero
        return carry

    lax.fori_loop(0, 4, duplicate, 0, unroll=2)
    for field, acc, dead in ((field_row, acc_row, ROW_DEAD), (field_col, acc_col, COL_DEAD)):
        field[dead] = zero.astype(BF16)
        acc[dead] = zero

    def block(b, carry):
        work = []
        for u in range(UNROLL):
            q = b * UNROLL + u
            rows = [idx_ref[0, q * 4 + k] for k in range(4)]
            cols = [idx_ref[1, q * 4 + k] for k in range(4)]
            w = w_ref[pl.ds(2 * q, 2)].reshape(2 * HALF, LANES)
            left_f = jnp.concatenate([field_col[cols[k]] * half_one[k % 2] for k in range(4)], axis=0)
            left_b = jnp.concatenate([field_row[rows[k]] * half_one[k // 2] for k in range(4)], axis=0)
            forward = lax.dot_general(left_f, w, NT_DIMS, preferred_element_type=F32)
            backward = jnp.dot(left_b, w, preferred_element_type=F32)
            work.append((rows, cols, forward, backward))
        for rows, cols, forward, backward in work:
            for k in range(4):
                acc_row[rows[k]] += jnp.where(half_mask[k // 2], forward[part(k)], 0.0)
                acc_col[cols[k]] += jnp.where(half_mask[k % 2], backward[part(k)], 0.0)
        return carry

    fetch.wait()
    lax.fori_loop(0, SLOTS // 4 // UNROLL, block, 0)

    def folded(piece, slot):
        _, acc, at = place(piece, slot)
        one, two = acc[at], acc[at + 1]
        return jnp.where(low_half, one, two) + pltpu.roll(jnp.where(low_half, two, one), HALF, 1)

    def pack(x, carry):
        for zh, core, j in INNER:
            piece = piece_at(x, zh, core, j)
            for slot in range(3):
                total = folded(piece, slot)
                chunk, rows = locate(not first, x, zh, core, j, slot)
                out_ref[chunk, rows] = total.astype(BF16)
                if first and slot == 2:
                    for n, term in enumerate(split2(total)):
                        scratch[6][n, piece] = term
        return carry

    if not first:
        lax.fori_loop(0, 4, pack, 0, unroll=2)
        for j in range(2):
            own_ref[j] = x_ref[own_piece + j, part(2)]
        return

    lax.fori_loop(0, 4, pack, 0, unroll=2)
    terms = scratch[6]
    left = jnp.concatenate(
        [jnp.concatenate([terms[n, p] for p in range(PIECES)], axis=1) for n in range(2)], axis=0
    )
    pieces = []
    for x in range(4):
        for zh, core, j in INNER:
            chunk, rows = locate(True, x, zh, core, j, 2)
            pieces.append(x_ref[chunk, rows])
    crosses = lax.dot_general(
        left, jnp.concatenate(pieces, axis=1), NT_DIMS, preferred_element_type=F32
    )
    cross = crosses[:VECS] + crosses[VECS:]
    message = message_of(gram_ref[...], cross_ref[...] + widen(cross))
    for p in range(PIECES):
        out_ref[p, 3 * VECS :] = message


def widen(value):
    return jnp.concatenate([value, jnp.zeros((VECS, LANES - VECS), F32)], axis=1)


def message_of(gram, cross):
    total = jnp.zeros((VECS, LANES), F32)
    for n, part in enumerate(split2(gram) + split2(cross)):
        part = part.astype(F32)
        total = total + (pltpu.roll(part, n * VECS, 1) if n else part)
    return (total[:MESSAGE] + pltpu.roll(total[MESSAGE:], HALF, 1)).astype(BF16)


def read_message(total):
    total = jnp.concatenate([total, pltpu.roll(total, HALF, 1)], axis=0)
    keep = lane_index() < VECS
    found = []
    for n in (0, 2):
        high = pltpu.roll(total, LANES - n * VECS, 1) if n else total
        low = pltpu.roll(total, LANES - (n + 1) * VECS, 1)
        found.append(jnp.where(keep, high + low, 0.0))
    return found


def sum_over(in_ref, start, rows, chunks=None):
    total = None
    for n in range(in_ref.shape[0]) if chunks is None else chunks:
        value = in_ref[n, start : start + rows].astype(F32)
        total = value if total is None else total + value
    return total


def collect_owner_kernel(in_ref, out_ref, back_ref):
    wide = 2 * VECS
    y, core = lax.axis_index("y"), lax.axis_index("core")
    nothing = jnp.zeros((wide, LANES), BF16)
    for block in range(8):
        zh, x = block // 4, block % 4
        chunks = [(x * 2 + zh) * 4 + zl for zl in range(4)]
        out_ref[block * 2 + core, :wide] = sum_over(in_ref, 0, wide, chunks).astype(BF16)
        out_ref[block * 2 + 1 - core, :wide] = nothing
    sums = []
    for zl in range(4):
        sums.append(sum_over(in_ref, wide, VECS, [n * 4 + zl for n in range(8)]))
    for s in range(2):
        same = core == 0
        back_ref[s] = jnp.where(same, sums[s], sums[2 + s])
        other = jnp.where(same, sums[2 + s], sums[s])
        out_ref[y * 2 + 1 - core, s * VECS : (s + 1) * VECS] = other.astype(BF16)
    message = message_of(*read_message(sum_over(in_ref, 3 * VECS, MESSAGE)))
    for n in range(2 * 8):
        out_ref[n, wide:] = message


def solve_kernel(in_ref, back_ref, owned_ref, e_ref, out_ref):
    gram, cross = read_message(sum_over(in_ref, 2 * VECS, MESSAGE))
    wide = jnp.concatenate([cross, jnp.zeros((LANES - VECS, LANES), F32)], axis=0)
    cross = cross + jnp.transpose(wide)[:VECS]
    state = jnp.concatenate([gram, cross], axis=0)
    columns = [jnp.broadcast_to(state[:, p : p + 1], (2 * VECS, LANES)) for p in range(VECS)]
    for p in range(VECS):
        scaled = columns[p] * (1.0 / columns[p][p : p + 1])
        columns = [
            scaled if q == p else column - scaled * column[p : p + 1]
            for q, column in enumerate(columns)
        ]
    for s in range(2):
        v = owned_ref[s].astype(F32)
        product = sum_over(in_ref, s * VECS, VECS) + back_ref[s] + e_ref[s : s + 1, :] * v
        shifted = jnp.zeros((VECS, LANES), F32)
        for k in range(VECS):
            shifted = shifted + columns[k][VECS:] * v[k : k + 1, :]
        value = (product - shifted).astype(BF16)
        for n in range(2 * 8):
            out_ref[n, s * VECS : (s + 1) * VECS] = value


def collect_kernel(in_ref, out_ref, back_ref):
    wide = 2 * VECS
    for r in range(NR):
        for s in range(2):
            out_ref[col_at(2 * r + s)] = in_ref[row_at(r), s * wide : (s + 1) * wide]
    for j in range(2):
        back_ref[j] = sum_over(in_ref, (4 + j) * VECS, VECS)


def finish_kernel(in_ref, back_ref, own_ref, e_ref, residual_ref, out_ref):
    for j in range(2):
        own = own_ref[j]
        total = sum_over(in_ref, j * VECS, VECS) + back_ref[j]
        residual_ref[:, j, :] = own
        out_ref[:, j, :] = total + e_ref[j : j + 1, :] * own.astype(F32)


def owner_of(n, k):
    core, zl = n // 4, n % 4
    return n, zl // 2 * 4 + core * 2 + (zl % 2 ^ k)


def exchange(value, axis):
    return lax.all_to_all(value, axis, split_axis=0, concat_axis=0, tiled=True)


def shards(vectors, tile_values, tile_coords, tile_counts, energies):
    tiles = tile_values[0]
    piece = shape(2, VECS, LANES)
    scratch = [
        pltpu.VMEM((ROW_DEAD + 1, VECS, LANES), BF16),
        pltpu.VMEM((COL_DEAD + 1, VECS, LANES), BF16),
        pltpu.VMEM((ROW_DEAD + 1, VECS, LANES), F32),
        pltpu.VMEM((COL_DEAD + 1, VECS, LANES), F32),
        pltpu.SMEM((2, SLOTS), jnp.int32),
        pltpu.SemaphoreType.DMA,
    ]
    index_shape, energy_shape = shape(2, SLOTS, dtype=jnp.int32), shape(2, LANES, dtype=F32)
    message = shape(2 * VECS, LANES)
    spread, *messages = call(
        spread_kernel,
        (shape(NC, 2 * VECS, LANES), message, message),
        2,
        [
            pltpu.VMEM((VECS, 2, LANES), BF16),
            pltpu.VMEM((2, LANES), F32),
            pltpu.VMEM((2 * VECS, LANES), BF16),
            pltpu.VMEM((2 * VECS, LANES), BF16),
            pltpu.VMEM((2 * VECS, LANES), BF16),
            pltpu.SemaphoreType.DMA((NC + 4,)),
        ],
        first=pl.BlockSpec(memory_space=pl.ANY),
        last=pl.BlockSpec(memory_space=pl.ANY),
        limit=60,
    )(vectors, energies)
    received = [
        lax.ppermute(message, ("core", "zl"), [owner_of(n, k) for n in range(8)])
        for k, message in enumerate(messages)
    ]
    slab = exchange(spread, COL)
    sums = shape(VECS, LANES, dtype=F32)
    index, energies, gram, cross = call(
        index_kernel, (index_shape, energy_shape, sums, sums), 4, scalars=(1,)
    )(tile_coords, tile_counts, energies, vectors)
    grouped, owned, owned_energies, index, energies = call(
        regroup_kernel,
        (shape(NR, GROUP * VECS, LANES), piece, energy_shape, index_shape, energy_shape),
        5,
    )(slab, *received, index, energies)
    fields = exchange(grouped, ROW)
    partial = call(
        functools.partial(tiles_kernel, True),
        shape(PIECES, 3 * VECS + MESSAGE, LANES),
        5,
        scratch + [pltpu.VMEM((2, PIECES, VECS, LANES), BF16)],
    )(index, fields, tiles, gram, cross)
    by_owner, back = call(
        collect_owner_kernel,
        (shape(NR, 2 * VECS + MESSAGE, LANES), shape(2, VECS, LANES, dtype=F32)),
        1,
    )(exchange(partial, PIECE))
    residual = call(solve_kernel, shape(NR, 2 * VECS, LANES), 4)(
        exchange(by_owner, OWNER), back, owned, owned_energies
    )

    grouped = call(regroup_back_kernel, shape(PIECES, 3 * VECS, LANES), 1)(exchange(residual, OWNER))
    partial, own = call(
        functools.partial(tiles_kernel, False),
        (shape(NR, GROUP * VECS, LANES), piece),
        3,
        scratch,
    )(index, exchange(grouped, PIECE), tiles)
    by_block, back = call(
        collect_kernel, (shape(NC, 2 * VECS, LANES), shape(2, VECS, LANES, dtype=F32)), 1
    )(exchange(partial, ROW))
    return call(
        finish_kernel, (shape(VECS, 2, LANES), shape(VECS, 2, LANES, dtype=F32)), 4
    )(exchange(by_block, COL), back, own, energies)


def solution(mesh):
    devices = np.asarray(mesh.devices).reshape(2, 4, 2, 8, 4)
    fine = jax.sharding.Mesh(devices, ("zh", "x", "core", "y", "zl"))
    row, col = ("zh", "x", "core"), ("y", "zl")
    in_specs = (
        P(None, row, col),
        P(row, col, None, None),
        P(None, row, col),
        P(row, col),
        P(row, col),
    )
    out_specs = (P(None, row, col), P(None, row, col))
    return jax.shard_map(shards, mesh=fine, in_specs=in_specs, out_specs=out_specs, check_vma=False)
```

```python
import functools

import jax
import jax.numpy as jnp
import numpy as np
from jax import lax
from jax.experimental import pallas as pl
from jax.experimental.pallas import tpu as pltpu
from jax.sharding import PartitionSpec as P

F32 = jnp.float32
BF16 = jnp.bfloat16
VECS = 16
LANES = 128
HALF = 64
MESSAGE = 8
NR = 16
NC = 32
GROUP = 6
PIECES = 32
SLOTS = 128
UNROLL = 32
ROW_DEAD = NR * 8
COL_DEAD = NR * 4
ROW = ("core", "x", "zh")
COL = ("zl", "y")
PIECE = ("x", "zh", "zl")
OWNER = ("y", "core")
VMEM = pl.BlockSpec(memory_space=pltpu.VMEM)
SMEM = pl.BlockSpec(memory_space=pltpu.SMEM)
NT_DIMS = (((1,), (1,)), ((), ()))


def row_at(r):
    return (r % 2) * 8 + (r // 2 % 4) * 2 + r // 8


def col_at(c):
    return (c % 4) * 8 + c // 4


def shape(*dims, dtype=BF16):
    return jax.ShapeDtypeStruct(dims, dtype)


def call(kernel, outs, n_in, scratch=(), scalars=(), first=VMEM, limit=32):
    specs = [SMEM if n in scalars else first for n in range(n_in)]
    return pl.pallas_call(
        kernel,
        out_shape=outs,
        in_specs=specs,
        out_specs=jax.tree.map(lambda _: VMEM, outs),
        scratch_shapes=list(scratch),
        compiler_params=pltpu.CompilerParams(vmem_limit_bytes=limit * 1024 * 1024),
    )


def lane_index():
    return lax.broadcasted_iota(jnp.int32, (VECS, LANES), 1)


def split2(value):
    high = value.astype(BF16)
    return high, (value - high.astype(F32)).astype(BF16)


def split3(value):
    high = value.astype(BF16)
    rest = value - high.astype(F32)
    middle = rest.astype(BF16)
    low = (rest - middle.astype(F32)).astype(BF16)
    return high, middle, low


def piece_at(x, zh, core, j):
    return x * 8 + zh * 4 + core * 2 + j


def locate(by_row, x, zh, core, j, slot):
    if by_row:
        place = slot * 2 + j if slot < 2 else 4 + j
        return core * 8 + x * 2 + zh, slice(place * VECS, (place + 1) * VECS)
    return piece_at(x, zh, core, j), slice(slot * VECS, (slot + 1) * VECS)


INNER = [(zh, core, j) for zh in range(2) for core in range(2) for j in range(2)]


def spread_kernel(x_hbm, e_hbm, out_ref, even_ref, odd_ref, x_ref, e_ref, sems):
    pairs = ((x_hbm, x_ref), (e_hbm, e_ref))
    copies = [pltpu.make_async_copy(a, b, sems.at[n]) for n, (a, b) in enumerate(pairs)]
    for copy in copies:
        copy.start()
    for copy in copies:
        copy.wait()
    for j in range(2):
        value = x_ref[:, j, :]
        for c in range(NC):
            out_ref[c, j * VECS : (j + 1) * VECS] = value
    odd = lax.rem(lax.axis_index("zl"), 2)
    row = lax.broadcasted_iota(jnp.int32, (VECS, LANES), 0)
    for k, message in enumerate((even_ref, odd_ref)):
        message[:VECS] = jnp.where(odd == k, x_ref[:, 0, :], x_ref[:, 1, :])
        terms = jnp.zeros((VECS, LANES), F32)
        for n, term in enumerate(split3(jnp.where(odd == k, e_ref[0:1], e_ref[1:2]))):
            terms = jnp.where(row == n, term.astype(F32), terms)
        message[VECS:] = terms.astype(BF16)


def index_kernel(coords_ref, counts_ref, e_ref, x_ref, index_ref, energy_ref, gram_ref, cross_ref):
    gram = jnp.zeros((VECS, VECS), F32)
    cross = jnp.zeros((VECS, VECS), F32)
    for j in range(2):
        own = x_ref[:, j, :]
        gram = gram + lax.dot_general(own, own, NT_DIMS, preferred_element_type=F32)
        for term in split3(own.astype(F32) * (0.5 * e_ref[j : j + 1, :])):
            cross = cross + lax.dot_general(term, own, NT_DIMS, preferred_element_type=F32)
    gram_ref[...] = widen(gram)
    cross_ref[...] = widen(cross)
    live = lax.broadcasted_iota(jnp.int32, (1, SLOTS), 1) < counts_ref[0, 0]
    for n, dead in ((0, ROW_DEAD), (1, COL_DEAD)):
        coords = coords_ref[n]
        major = coords >> 6
        piece = ((major >> 2) & 3) * 8 + (major >> 4) * 4 + (major & 3)
        if n == 0:
            piece = piece * 2 + ((coords >> 1) & 1)
        index_ref[n : n + 1] = jnp.where(live, piece * 2 + (coords & 1), dead)
    energy_ref[...] = e_ref[...]


def regroup_kernel(
    in_ref, even_ref, odd_ref, index_in, e_in, out_ref, owned_ref, energy_ref, index_out, e_out
):
    index_out[...] = index_in[...]
    e_out[...] = e_in[...]
    wide = 2 * VECS
    y, zl = lax.axis_index("y"), lax.axis_index("zl")
    own = in_ref[zl * 8 + y]
    odd = lax.rem(zl, 2)
    for j in range(2):
        message = jnp.where(odd == j, even_ref[...], odd_ref[...])
        owned_ref[j] = message[:VECS]
        terms = message[VECS:].astype(F32)
        energy_ref[j : j + 1] = terms[0:1] + terms[1:2] + terms[2:3]
    for r in range(NR):
        at = row_at(r)
        for s in range(2):
            out_ref[at, s * wide : (s + 1) * wide] = in_ref[col_at(2 * r + s)]
        out_ref[at, 2 * wide :] = own


def regroup_back_kernel(in_ref, out_ref):
    y, core = lax.axis_index("y"), lax.axis_index("core")
    for zl in range(4):
        column = in_ref[y * 2 + zl // 2, (zl % 2) * VECS : (zl % 2 + 1) * VECS]
        for block in range(8):
            zh, x = block // 4, block % 4
            at = (x * 2 + zh) * 4 + zl
            out_ref[at, : 2 * VECS] = in_ref[block * 2 + core]
            out_ref[at, 2 * VECS :] = column


def tiles_kernel(first, *refs):
    if first:
        index_ref, x_ref, w_ref, gram_ref, cross_ref, out_ref, *scratch = refs
    else:
        index_ref, x_ref, w_ref, out_ref, own_ref, *scratch = refs
    field_row, field_col, acc_row, acc_col, idx_ref, sem = scratch[:6]
    fetch = pltpu.make_async_copy(index_ref, idx_ref, sem)
    fetch.start()
    low_half = lane_index() < HALF
    zero = jnp.zeros((VECS, LANES), F32)
    half_mask = [low_half, jnp.logical_not(low_half)]
    half_one = [jnp.where(m, 1.0, 0.0).astype(BF16) for m in half_mask]
    own_piece = piece_at(lax.axis_index("x"), lax.axis_index("zh"), lax.axis_index("core"), 0)

    def part(g):
        return slice(g * VECS, (g + 1) * VECS)

    def place(piece, slot):
        if slot < 2:
            return field_row, acc_row, (piece * 2 + slot) * 2
        return field_col, acc_col, piece * 2

    def duplicate(x, carry):
        for zh, core, j in INNER:
            for slot in range(3):
                chunk, rows = locate(first, x, zh, core, j, slot)
                value = x_ref[chunk, rows].astype(F32)
                turned = pltpu.roll(value, HALF, 1)
                field, acc, at = place(piece_at(x, zh, core, j), slot)
                field[at] = jnp.where(low_half, value, turned).astype(BF16)
                field[at + 1] = jnp.where(low_half, turned, value).astype(BF16)
                acc[at] = zero
                acc[at + 1] = zero
        return carry

    lax.fori_loop(0, 4, duplicate, 0, unroll=2)
    for field, acc, dead in ((field_row, acc_row, ROW_DEAD), (field_col, acc_col, COL_DEAD)):
        field[dead] = zero.astype(BF16)
        acc[dead] = zero

    def block(b, carry):
        work = []
        for u in range(UNROLL):
            q = b * UNROLL + u
            rows = [idx_ref[0, q * 4 + k] for k in range(4)]
            cols = [idx_ref[1, q * 4 + k] for k in range(4)]
            w = w_ref[pl.ds(2 * q, 2)].reshape(2 * HALF, LANES)
            left_f = jnp.concatenate([field_col[cols[k]] * half_one[k % 2] for k in range(4)], axis=0)
            left_b = jnp.concatenate([field_row[rows[k]] * half_one[k // 2] for k in range(4)], axis=0)
            forward = lax.dot_general(left_f, w, NT_DIMS, preferred_element_type=F32)
            backward = jnp.dot(left_b, w, preferred_element_type=F32)
            work.append((rows, cols, forward, backward))
        for rows, cols, forward, backward in work:
            for k in range(4):
                acc_row[rows[k]] += jnp.where(half_mask[k // 2], forward[part(k)], 0.0)
                acc_col[cols[k]] += jnp.where(half_mask[k % 2], backward[part(k)], 0.0)
        return carry

    fetch.wait()
    lax.fori_loop(0, SLOTS // 4 // UNROLL, block, 0)

    def folded(piece, slot):
        _, acc, at = place(piece, slot)
        one, two = acc[at], acc[at + 1]
        return jnp.where(low_half, one, two) + pltpu.roll(jnp.where(low_half, two, one), HALF, 1)

    def pack(x, carry):
        for zh, core, j in INNER:
            piece = piece_at(x, zh, core, j)
            for slot in range(3):
                total = folded(piece, slot)
                chunk, rows = locate(not first, x, zh, core, j, slot)
                out_ref[chunk, rows] = total.astype(BF16)
                if first and slot == 2:
                    for n, term in enumerate(split2(total)):
                        scratch[6][n, piece] = term
        return carry

    if not first:
        lax.fori_loop(0, 4, pack, 0, unroll=2)
        for j in range(2):
            own_ref[j] = x_ref[own_piece + j, part(2)]
        return

    lax.fori_loop(0, 4, pack, 0, unroll=2)
    terms = scratch[6]
    left = jnp.concatenate(
        [jnp.concatenate([terms[n, p] for p in range(PIECES)], axis=1) for n in range(2)], axis=0
    )
    pieces = []
    for x in range(4):
        for zh, core, j in INNER:
            chunk, rows = locate(True, x, zh, core, j, 2)
            pieces.append(x_ref[chunk, rows])
    crosses = lax.dot_general(
        left, jnp.concatenate(pieces, axis=1), NT_DIMS, preferred_element_type=F32
    )
    cross = crosses[:VECS] + crosses[VECS:]
    message = message_of(gram_ref[...], cross_ref[...] + widen(cross))
    for p in range(PIECES):
        out_ref[p, 3 * VECS :] = message


def widen(value):
    return jnp.concatenate([value, jnp.zeros((VECS, LANES - VECS), F32)], axis=1)


def message_of(gram, cross):
    total = jnp.zeros((VECS, LANES), F32)
    for n, part in enumerate(split2(gram) + split2(cross)):
        part = part.astype(F32)
        total = total + (pltpu.roll(part, n * VECS, 1) if n else part)
    return (total[:MESSAGE] + pltpu.roll(total[MESSAGE:], HALF, 1)).astype(BF16)


def read_message(total):
    total = jnp.concatenate([total, pltpu.roll(total, HALF, 1)], axis=0)
    keep = lane_index() < VECS
    found = []
    for n in (0, 2):
        high = pltpu.roll(total, LANES - n * VECS, 1) if n else total
        low = pltpu.roll(total, LANES - (n + 1) * VECS, 1)
        found.append(jnp.where(keep, high + low, 0.0))
    return found


def sum_over(in_ref, start, rows, chunks=None):
    total = None
    for n in range(in_ref.shape[0]) if chunks is None else chunks:
        value = in_ref[n, start : start + rows].astype(F32)
        total = value if total is None else total + value
    return total


def collect_owner_kernel(in_ref, out_ref, back_ref):
    wide = 2 * VECS
    y, core = lax.axis_index("y"), lax.axis_index("core")
    nothing = jnp.zeros((wide, LANES), BF16)
    for block in range(8):
        zh, x = block // 4, block % 4
        chunks = [(x * 2 + zh) * 4 + zl for zl in range(4)]
        out_ref[block * 2 + core, :wide] = sum_over(in_ref, 0, wide, chunks).astype(BF16)
        out_ref[block * 2 + 1 - core, :wide] = nothing
    sums = []
    for zl in range(4):
        sums.append(sum_over(in_ref, wide, VECS, [n * 4 + zl for n in range(8)]))
    for s in range(2):
        same = core == 0
        back_ref[s] = jnp.where(same, sums[s], sums[2 + s])
        other = jnp.where(same, sums[2 + s], sums[s])
        out_ref[y * 2 + 1 - core, s * VECS : (s + 1) * VECS] = other.astype(BF16)
    message = message_of(*read_message(sum_over(in_ref, 3 * VECS, MESSAGE)))
    for n in range(2 * 8):
        out_ref[n, wide:] = message


def solve_kernel(in_ref, back_ref, owned_ref, e_ref, out_ref):
    gram, cross = read_message(sum_over(in_ref, 2 * VECS, MESSAGE))
    wide = jnp.concatenate([cross, jnp.zeros((LANES - VECS, LANES), F32)], axis=0)
    cross = cross + jnp.transpose(wide)[:VECS]
    state = jnp.concatenate([gram, cross], axis=0)
    columns = [jnp.broadcast_to(state[:, p : p + 1], (2 * VECS, LANES)) for p in range(VECS)]
    for p in range(VECS):
        scaled = columns[p] * (1.0 / columns[p][p : p + 1])
        columns = [
            scaled if q == p else column - scaled * column[p : p + 1]
            for q, column in enumerate(columns)
        ]
    for s in range(2):
        v = owned_ref[s].astype(F32)
        product = sum_over(in_ref, s * VECS, VECS) + back_ref[s] + e_ref[s : s + 1, :] * v
        shifted = jnp.zeros((VECS, LANES), F32)
        for k in range(VECS):
            shifted = shifted + columns[k][VECS:] * v[k : k + 1, :]
        value = (product - shifted).astype(BF16)
        for n in range(2 * 8):
            out_ref[n, s * VECS : (s + 1) * VECS] = value


def collect_kernel(in_ref, out_ref, back_ref):
    wide = 2 * VECS
    for r in range(NR):
        for s in range(2):
            out_ref[col_at(2 * r + s)] = in_ref[row_at(r), s * wide : (s + 1) * wide]
    for j in range(2):
        back_ref[j] = sum_over(in_ref, (4 + j) * VECS, VECS)


def finish_kernel(in_ref, back_ref, own_ref, e_ref, residual_ref, out_ref):
    for j in range(2):
        own = own_ref[j]
        total = sum_over(in_ref, j * VECS, VECS) + back_ref[j]
        residual_ref[:, j, :] = own
        out_ref[:, j, :] = total + e_ref[j : j + 1, :] * own.astype(F32)


def owner_of(n, k):
    core, zl = n // 4, n % 4
    return n, zl // 2 * 4 + core * 2 + (zl % 2 ^ k)


def exchange(value, axis):
    return lax.all_to_all(value, axis, split_axis=0, concat_axis=0, tiled=True)


def shards(vectors, tile_values, tile_coords, tile_counts, energies):
    tiles = tile_values[0]
    piece = shape(2, VECS, LANES)
    scratch = [
        pltpu.VMEM((ROW_DEAD + 1, VECS, LANES), BF16),
        pltpu.VMEM((COL_DEAD + 1, VECS, LANES), BF16),
        pltpu.VMEM((ROW_DEAD + 1, VECS, LANES), F32),
        pltpu.VMEM((COL_DEAD + 1, VECS, LANES), F32),
        pltpu.SMEM((2, SLOTS), jnp.int32),
        pltpu.SemaphoreType.DMA,
    ]
    index_shape, energy_shape = shape(2, SLOTS, dtype=jnp.int32), shape(2, LANES, dtype=F32)
    message = shape(2 * VECS, LANES)
    spread, *messages = call(
        spread_kernel,
        (shape(NC, 2 * VECS, LANES), message, message),
        2,
        [
            pltpu.VMEM((VECS, 2, LANES), BF16),
            pltpu.VMEM((2, LANES), F32),
            pltpu.SemaphoreType.DMA((2,)),
        ],
        first=pl.BlockSpec(memory_space=pl.ANY),
        limit=60,
    )(vectors, energies)
    received = [
        lax.ppermute(message, ("core", "zl"), [owner_of(n, k) for n in range(8)])
        for k, message in enumerate(messages)
    ]
    slab = exchange(spread, COL)
    sums = shape(VECS, LANES, dtype=F32)
    index, energies, gram, cross = call(
        index_kernel, (index_shape, energy_shape, sums, sums), 4, scalars=(1,)
    )(tile_coords, tile_counts, energies, vectors)
    grouped, owned, owned_energies, index, energies = call(
        regroup_kernel,
        (shape(NR, GROUP * VECS, LANES), piece, energy_shape, index_shape, energy_shape),
        5,
    )(slab, *received, index, energies)
    fields = exchange(grouped, ROW)
    partial = call(
        functools.partial(tiles_kernel, True),
        shape(PIECES, 3 * VECS + MESSAGE, LANES),
        5,
        scratch + [pltpu.VMEM((2, PIECES, VECS, LANES), BF16)],
    )(index, fields, tiles, gram, cross)
    by_owner, back = call(
        collect_owner_kernel,
        (shape(NR, 2 * VECS + MESSAGE, LANES), shape(2, VECS, LANES, dtype=F32)),
        1,
    )(exchange(partial, PIECE))
    residual = call(solve_kernel, shape(NR, 2 * VECS, LANES), 4)(
        exchange(by_owner, OWNER), back, owned, owned_energies
    )

    grouped = call(regroup_back_kernel, shape(PIECES, 3 * VECS, LANES), 1)(exchange(residual, OWNER))
    partial, own = call(
        functools.partial(tiles_kernel, False),
        (shape(NR, GROUP * VECS, LANES), piece),
        3,
        scratch,
    )(index, exchange(grouped, PIECE), tiles)
    by_block, back = call(
        collect_kernel, (shape(NC, 2 * VECS, LANES), shape(2, VECS, LANES, dtype=F32)), 1
    )(exchange(partial, ROW))
    return call(
        finish_kernel, (shape(VECS, 2, LANES), shape(VECS, 2, LANES, dtype=F32)), 4
    )(exchange(by_block, COL), back, own, energies)


def solution(mesh):
    devices = np.asarray(mesh.devices).reshape(2, 4, 2, 8, 4)
    fine = jax.sharding.Mesh(devices, ("zh", "x", "core", "y", "zl"))
    row, col = ("zh", "x", "core"), ("y", "zl")
    in_specs = (
        P(None, row, col),
        P(row, col, None, None),
        P(None, row, col),
        P(row, col),
        P(row, col),
    )
    out_specs = (P(None, row, col), P(None, row, col))
    return jax.shard_map(shards, mesh=fine, in_specs=in_specs, out_specs=out_specs, check_vma=False)
```

```python
import functools

import jax
import jax.numpy as jnp
import numpy as np
from jax import lax
from jax.experimental import pallas as pl
from jax.experimental.pallas import tpu as pltpu
from jax.sharding import PartitionSpec as P

F32 = jnp.float32
BF16 = jnp.bfloat16
VECS = 16
LANES = 128
HALF = 64
MESSAGE = 8
NR = 16
NC = 32
GROUP = 6
PIECES = 32
SLOTS = 128
UNROLL = 32
ROW_DEAD = NR * 8
COL_DEAD = NR * 4
ROW = ("core", "x", "zh")
COL = ("zl", "y")
PIECE = ("x", "zh", "zl")
OWNER = ("y", "core")
VMEM = pl.BlockSpec(memory_space=pltpu.VMEM)
SMEM = pl.BlockSpec(memory_space=pltpu.SMEM)
NT_DIMS = (((1,), (1,)), ((), ()))


def row_at(r):
    return (r % 2) * 8 + (r // 2 % 4) * 2 + r // 8


def col_at(c):
    return (c % 4) * 8 + c // 4


def shape(*dims, dtype=BF16):
    return jax.ShapeDtypeStruct(dims, dtype)


def call(kernel, outs, n_in, scratch=(), scalars=(), first=VMEM, limit=32):
    specs = [SMEM if n in scalars else first for n in range(n_in)]
    return pl.pallas_call(
        kernel,
        out_shape=outs,
        in_specs=specs,
        out_specs=jax.tree.map(lambda _: VMEM, outs),
        scratch_shapes=list(scratch),
        compiler_params=pltpu.CompilerParams(vmem_limit_bytes=limit * 1024 * 1024),
    )


def lane_index():
    return lax.broadcasted_iota(jnp.int32, (VECS, LANES), 1)


def split2(value):
    high = value.astype(BF16)
    return high, (value - high.astype(F32)).astype(BF16)


def split3(value):
    high = value.astype(BF16)
    rest = value - high.astype(F32)
    middle = rest.astype(BF16)
    low = (rest - middle.astype(F32)).astype(BF16)
    return high, middle, low


def piece_at(x, zh, core, j):
    return x * 8 + zh * 4 + core * 2 + j


def locate(by_row, x, zh, core, j, slot):
    if by_row:
        place = slot * 2 + j if slot < 2 else 4 + j
        return core * 8 + x * 2 + zh, slice(place * VECS, (place + 1) * VECS)
    return piece_at(x, zh, core, j), slice(slot * VECS, (slot + 1) * VECS)


INNER = [(zh, core, j) for zh in range(2) for core in range(2) for j in range(2)]


def spread_kernel(x_hbm, e_hbm, out_ref, even_ref, odd_ref, x_ref, e_ref, sems):
    pairs = ((x_hbm, x_ref), (e_hbm, e_ref))
    copies = [pltpu.make_async_copy(a, b, sems.at[n]) for n, (a, b) in enumerate(pairs)]
    for copy in copies:
        copy.start()
    for copy in copies:
        copy.wait()
    for j in range(2):
        value = x_ref[:, j, :]
        for c in range(NC):
            out_ref[c, j * VECS : (j + 1) * VECS] = value
    odd = lax.rem(lax.axis_index("zl"), 2)
    row = lax.broadcasted_iota(jnp.int32, (VECS, LANES), 0)
    for k, message in enumerate((even_ref, odd_ref)):
        message[:VECS] = jnp.where(odd == k, x_ref[:, 0, :], x_ref[:, 1, :])
        terms = jnp.zeros((VECS, LANES), F32)
        for n, term in enumerate(split3(jnp.where(odd == k, e_ref[0:1], e_ref[1:2]))):
            terms = jnp.where(row == n, term.astype(F32), terms)
        message[VECS:] = terms.astype(BF16)


def index_kernel(coords_ref, counts_ref, e_ref, index_ref, energy_ref):
    live = lax.broadcasted_iota(jnp.int32, (1, SLOTS), 1) < counts_ref[0, 0]
    for n, dead in ((0, ROW_DEAD), (1, COL_DEAD)):
        coords = coords_ref[n]
        major = coords >> 6
        piece = ((major >> 2) & 3) * 8 + (major >> 4) * 4 + (major & 3)
        if n == 0:
            piece = piece * 2 + ((coords >> 1) & 1)
        index_ref[n : n + 1] = jnp.where(live, piece * 2 + (coords & 1), dead)
    energy_ref[...] = e_ref[...]


def regroup_kernel(
    in_ref, even_ref, odd_ref, index_in, e_in, out_ref, own_ref, owned_ref, energy_ref, index_out, e_out
):
    index_out[...] = index_in[...]
    e_out[...] = e_in[...]
    wide = 2 * VECS
    y, zl = lax.axis_index("y"), lax.axis_index("zl")
    own = in_ref[zl * 8 + y]
    odd = lax.rem(zl, 2)
    for j in range(2):
        own_ref[j] = own[j * VECS : (j + 1) * VECS]
        message = jnp.where(odd == j, even_ref[...], odd_ref[...])
        owned_ref[j] = message[:VECS]
        terms = message[VECS:].astype(F32)
        energy_ref[j : j + 1] = terms[0:1] + terms[1:2] + terms[2:3]
    for r in range(NR):
        at = row_at(r)
        for s in range(2):
            out_ref[at, s * wide : (s + 1) * wide] = in_ref[col_at(2 * r + s)]
        out_ref[at, 2 * wide :] = own


def regroup_back_kernel(in_ref, out_ref):
    y, core = lax.axis_index("y"), lax.axis_index("core")
    for zl in range(4):
        column = in_ref[y * 2 + zl // 2, (zl % 2) * VECS : (zl % 2 + 1) * VECS]
        for block in range(8):
            zh, x = block // 4, block % 4
            at = (x * 2 + zh) * 4 + zl
            out_ref[at, : 2 * VECS] = in_ref[block * 2 + core]
            out_ref[at, 2 * VECS :] = column


def tiles_kernel(first, *refs):
    if first:
        index_ref, x_ref, w_ref, own_ref, e_ref, out_ref, *scratch = refs
    else:
        index_ref, x_ref, w_ref, out_ref, own_ref, *scratch = refs
    field_row, field_col, acc_row, acc_col, idx_ref, sem = scratch[:6]
    fetch = pltpu.make_async_copy(index_ref, idx_ref, sem)
    fetch.start()
    low_half = lane_index() < HALF
    zero = jnp.zeros((VECS, LANES), F32)
    half_mask = [low_half, jnp.logical_not(low_half)]
    half_one = [jnp.where(m, 1.0, 0.0).astype(BF16) for m in half_mask]
    own_piece = piece_at(lax.axis_index("x"), lax.axis_index("zh"), lax.axis_index("core"), 0)

    def part(g):
        return slice(g * VECS, (g + 1) * VECS)

    def place(piece, slot):
        if slot < 2:
            return field_row, acc_row, (piece * 2 + slot) * 2
        return field_col, acc_col, piece * 2

    def duplicate(x, carry):
        for zh, core, j in INNER:
            for slot in range(3):
                chunk, rows = locate(first, x, zh, core, j, slot)
                value = x_ref[chunk, rows].astype(F32)
                turned = pltpu.roll(value, HALF, 1)
                field, acc, at = place(piece_at(x, zh, core, j), slot)
                field[at] = jnp.where(low_half, value, turned).astype(BF16)
                field[at + 1] = jnp.where(low_half, turned, value).astype(BF16)
                acc[at] = zero
                acc[at + 1] = zero
        return carry

    lax.fori_loop(0, 4, duplicate, 0, unroll=2)
    for field, acc, dead in ((field_row, acc_row, ROW_DEAD), (field_col, acc_col, COL_DEAD)):
        field[dead] = zero.astype(BF16)
        acc[dead] = zero

    def block(b, carry):
        work = []
        for u in range(UNROLL):
            q = b * UNROLL + u
            rows = [idx_ref[0, q * 4 + k] for k in range(4)]
            cols = [idx_ref[1, q * 4 + k] for k in range(4)]
            w = w_ref[pl.ds(2 * q, 2)].reshape(2 * HALF, LANES)
            left_f = jnp.concatenate([field_col[cols[k]] * half_one[k % 2] for k in range(4)], axis=0)
            left_b = jnp.concatenate([field_row[rows[k]] * half_one[k // 2] for k in range(4)], axis=0)
            forward = lax.dot_general(left_f, w, NT_DIMS, preferred_element_type=F32)
            backward = jnp.dot(left_b, w, preferred_element_type=F32)
            work.append((rows, cols, forward, backward))
        for rows, cols, forward, backward in work:
            for k in range(4):
                acc_row[rows[k]] += jnp.where(half_mask[k // 2], forward[part(k)], 0.0)
                acc_col[cols[k]] += jnp.where(half_mask[k % 2], backward[part(k)], 0.0)
        return carry

    fetch.wait()
    lax.fori_loop(0, SLOTS // 4 // UNROLL, block, 0)

    def folded(piece, slot):
        _, acc, at = place(piece, slot)
        one, two = acc[at], acc[at + 1]
        return jnp.where(low_half, one, two) + pltpu.roll(jnp.where(low_half, two, one), HALF, 1)

    def pack(x, carry):
        for zh, core, j in INNER:
            piece = piece_at(x, zh, core, j)
            for slot in range(3):
                total = folded(piece, slot)
                chunk, rows = locate(not first, x, zh, core, j, slot)
                out_ref[chunk, rows] = total.astype(BF16)
                if first and slot == 2:
                    for n, term in enumerate(split2(total)):
                        scratch[6][n, piece] = term
        return carry

    if not first:
        lax.fori_loop(0, 4, pack, 0, unroll=2)
        for j in range(2):
            own_ref[j] = x_ref[own_piece + j, part(2)]
        return

    lax.fori_loop(0, 4, pack, 0, unroll=2)
    terms = scratch[6]
    left = jnp.concatenate(
        [jnp.concatenate([terms[n, p] for p in range(PIECES)], axis=1) for n in range(2)], axis=0
    )
    pieces = []
    for x in range(4):
        for zh, core, j in INNER:
            chunk, rows = locate(True, x, zh, core, j, 2)
            pieces.append(x_ref[chunk, rows])
    crosses = lax.dot_general(
        left, jnp.concatenate(pieces, axis=1), NT_DIMS, preferred_element_type=F32
    )
    cross = crosses[:VECS] + crosses[VECS:]
    gram = jnp.zeros((VECS, VECS), F32)
    for j in range(2):
        own = own_ref[j]
        gram = gram + lax.dot_general(own, own, NT_DIMS, preferred_element_type=F32)
        for term in split3(own.astype(F32) * (0.5 * e_ref[j : j + 1, :])):
            cross = cross + lax.dot_general(term, own, NT_DIMS, preferred_element_type=F32)
    message = message_of(widen(gram), widen(cross))
    for p in range(PIECES):
        out_ref[p, 3 * VECS :] = message


def widen(value):
    return jnp.concatenate([value, jnp.zeros((VECS, LANES - VECS), F32)], axis=1)


def message_of(gram, cross):
    total = jnp.zeros((VECS, LANES), F32)
    for n, part in enumerate(split2(gram) + split2(cross)):
        part = part.astype(F32)
        total = total + (pltpu.roll(part, n * VECS, 1) if n else part)
    return (total[:MESSAGE] + pltpu.roll(total[MESSAGE:], HALF, 1)).astype(BF16)


def read_message(total):
    total = jnp.concatenate([total, pltpu.roll(total, HALF, 1)], axis=0)
    keep = lane_index() < VECS
    found = []
    for n in (0, 2):
        high = pltpu.roll(total, LANES - n * VECS, 1) if n else total
        low = pltpu.roll(total, LANES - (n + 1) * VECS, 1)
        found.append(jnp.where(keep, high + low, 0.0))
    return found


def sum_over(in_ref, start, rows, chunks=None):
    total = None
    for n in range(in_ref.shape[0]) if chunks is None else chunks:
        value = in_ref[n, start : start + rows].astype(F32)
        total = value if total is None else total + value
    return total


def collect_owner_kernel(in_ref, out_ref, back_ref):
    wide = 2 * VECS
    y, core = lax.axis_index("y"), lax.axis_index("core")
    nothing = jnp.zeros((wide, LANES), BF16)
    for block in range(8):
        zh, x = block // 4, block % 4
        chunks = [(x * 2 + zh) * 4 + zl for zl in range(4)]
        out_ref[block * 2 + core, :wide] = sum_over(in_ref, 0, wide, chunks).astype(BF16)
        out_ref[block * 2 + 1 - core, :wide] = nothing
    sums = []
    for zl in range(4):
        sums.append(sum_over(in_ref, wide, VECS, [n * 4 + zl for n in range(8)]))
    for s in range(2):
        same = core == 0
        back_ref[s] = jnp.where(same, sums[s], sums[2 + s])
        other = jnp.where(same, sums[2 + s], sums[s])
        out_ref[y * 2 + 1 - core, s * VECS : (s + 1) * VECS] = other.astype(BF16)
    message = message_of(*read_message(sum_over(in_ref, 3 * VECS, MESSAGE)))
    for n in range(2 * 8):
        out_ref[n, wide:] = message


def solve_kernel(in_ref, back_ref, owned_ref, e_ref, out_ref):
    gram, cross = read_message(sum_over(in_ref, 2 * VECS, MESSAGE))
    wide = jnp.concatenate([cross, jnp.zeros((LANES - VECS, LANES), F32)], axis=0)
    cross = cross + jnp.transpose(wide)[:VECS]
    state = jnp.concatenate([gram, cross], axis=0)
    columns = [jnp.broadcast_to(state[:, p : p + 1], (2 * VECS, LANES)) for p in range(VECS)]
    for p in range(VECS):
        scaled = columns[p] * (1.0 / columns[p][p : p + 1])
        columns = [
            scaled if q == p else column - scaled * column[p : p + 1]
            for q, column in enumerate(columns)
        ]
    for s in range(2):
        v = owned_ref[s].astype(F32)
        product = sum_over(in_ref, s * VECS, VECS) + back_ref[s] + e_ref[s : s + 1, :] * v
        shifted = jnp.zeros((VECS, LANES), F32)
        for k in range(VECS):
            shifted = shifted + columns[k][VECS:] * v[k : k + 1, :]
        value = (product - shifted).astype(BF16)
        for n in range(2 * 8):
            out_ref[n, s * VECS : (s + 1) * VECS] = value


def collect_kernel(in_ref, out_ref, back_ref):
    wide = 2 * VECS
    for r in range(NR):
        for s in range(2):
            out_ref[col_at(2 * r + s)] = in_ref[row_at(r), s * wide : (s + 1) * wide]
    for j in range(2):
        back_ref[j] = sum_over(in_ref, (4 + j) * VECS, VECS)


def finish_kernel(in_ref, back_ref, own_ref, e_ref, residual_ref, out_ref):
    for j in range(2):
        own = own_ref[j]
        total = sum_over(in_ref, j * VECS, VECS) + back_ref[j]
        residual_ref[:, j, :] = own
        out_ref[:, j, :] = total + e_ref[j : j + 1, :] * own.astype(F32)


def owner_of(n, k):
    core, zl = n // 4, n % 4
    return n, zl // 2 * 4 + core * 2 + (zl % 2 ^ k)


def exchange(value, axis):
    return lax.all_to_all(value, axis, split_axis=0, concat_axis=0, tiled=True)


def shards(vectors, tile_values, tile_coords, tile_counts, energies):
    tiles = tile_values[0]
    piece = shape(2, VECS, LANES)
    scratch = [
        pltpu.VMEM((ROW_DEAD + 1, VECS, LANES), BF16),
        pltpu.VMEM((COL_DEAD + 1, VECS, LANES), BF16),
        pltpu.VMEM((ROW_DEAD + 1, VECS, LANES), F32),
        pltpu.VMEM((COL_DEAD + 1, VECS, LANES), F32),
        pltpu.SMEM((2, SLOTS), jnp.int32),
        pltpu.SemaphoreType.DMA,
    ]
    index_shape, energy_shape = shape(2, SLOTS, dtype=jnp.int32), shape(2, LANES, dtype=F32)
    message = shape(2 * VECS, LANES)
    spread, *messages = call(
        spread_kernel,
        (shape(NC, 2 * VECS, LANES), message, message),
        2,
        [
            pltpu.VMEM((VECS, 2, LANES), BF16),
            pltpu.VMEM((2, LANES), F32),
            pltpu.SemaphoreType.DMA((2,)),
        ],
        first=pl.BlockSpec(memory_space=pl.ANY),
        limit=60,
    )(vectors, energies)
    received = [
        lax.ppermute(message, ("core", "zl"), [owner_of(n, k) for n in range(8)])
        for k, message in enumerate(messages)
    ]
    slab = exchange(spread, COL)
    index, energies = call(index_kernel, (index_shape, energy_shape), 3, scalars=(1,))(
        tile_coords, tile_counts, energies
    )
    grouped, own, owned, owned_energies, index, energies = call(
        regroup_kernel,
        (shape(NR, GROUP * VECS, LANES), piece, piece, energy_shape, index_shape, energy_shape),
        5,
    )(slab, *received, index, energies)
    fields = exchange(grouped, ROW)
    partial = call(
        functools.partial(tiles_kernel, True),
        shape(PIECES, 3 * VECS + MESSAGE, LANES),
        5,
        scratch + [pltpu.VMEM((2, PIECES, VECS, LANES), BF16)],
    )(index, fields, tiles, own, energies)
    by_owner, back = call(
        collect_owner_kernel,
        (shape(NR, 2 * VECS + MESSAGE, LANES), shape(2, VECS, LANES, dtype=F32)),
        1,
    )(exchange(partial, PIECE))
    residual = call(solve_kernel, shape(NR, 2 * VECS, LANES), 4)(
        exchange(by_owner, OWNER), back, owned, owned_energies
    )

    grouped = call(regroup_back_kernel, shape(PIECES, 3 * VECS, LANES), 1)(exchange(residual, OWNER))
    partial, own = call(
        functools.partial(tiles_kernel, False),
        (shape(NR, GROUP * VECS, LANES), piece),
        3,
        scratch,
    )(index, exchange(grouped, PIECE), tiles)
    by_block, back = call(
        collect_kernel, (shape(NC, 2 * VECS, LANES), shape(2, VECS, LANES, dtype=F32)), 1
    )(exchange(partial, ROW))
    return call(
        finish_kernel, (shape(VECS, 2, LANES), shape(VECS, 2, LANES, dtype=F32)), 4
    )(exchange(by_block, COL), back, own, energies)


def solution(mesh):
    devices = np.asarray(mesh.devices).reshape(2, 4, 2, 8, 4)
    fine = jax.sharding.Mesh(devices, ("zh", "x", "core", "y", "zl"))
    row, col = ("zh", "x", "core"), ("y", "zl")
    in_specs = (
        P(None, row, col),
        P(row, col, None, None),
        P(None, row, col),
        P(row, col),
        P(row, col),
    )
    out_specs = (P(None, row, col), P(None, row, col))
    return jax.shard_map(shards, mesh=fine, in_specs=in_specs, out_specs=out_specs, check_vma=False)
```
